32 devices in a mesh: dp: 8 (over z, core), tensor: 4 (over y, x).
Axes of the slice: x: 2, y: 2, z: 4, core: 2. Of those that a mesh axis runs over, the one named last changes fastest.
Arguments:
- tokens: bfloat16 [4096, 2048], P(('dp', 'tensor')), may hold values from -6 to 6
- cotangent: bfloat16 [4096, 2048], P(('dp', 'tensor')), may hold values from -6 to 6
- lengths: int32 [8, 6], P('dp'), may hold values from 0 to 512, as said below
- entry_weight: float32 [2048, 3, 2048], P('dp', None, 'tensor'), may hold values from -0.125 to 0.125
- entry_first: float32 [2048, 3, 2048], P('dp', None, 'tensor'), may hold values from -160 to 160
- entry_second: float32 [2048, 3, 2048], P('dp', None, 'tensor'), may hold values from 4096 to 13107.2
- exit_weight: float32 [2048, 2048], P('dp', 'tensor'), may hold values from -1 to 1
- exit_first: float32 [2048, 2048], P('dp', 'tensor'), may hold values from -20 to 20
- exit_second: float32 [2048, 2048], P('dp', 'tensor'), may hold values from 61.44 to 204.8
- gate_weight: float32 [2048, 2, 5632], P('dp', None, 'tensor'), may hold values from -0.125 to 0.125
- gate_first: float32 [2048, 2, 5632], P('dp', None, 'tensor'), may hold values from -24 to 24
- gate_second: float32 [2048, 2, 5632], P('dp', None, 'tensor'), may hold values from 81.92 to 286.72
- down_weight: float32 [2048, 5632], P('dp', 'tensor'), may hold values from -0.078125 to 0.078125
- down_first: float32 [2048, 5632], P('dp', 'tensor'), may hold values from -24 to 24
- down_second: float32 [2048, 5632], P('dp', 'tensor'), may hold values from 81.92 to 286.72
- bias_rows: float32 [5, 2048], replicated, may hold values from -3 to 3
- bias_first: float32 [5, 2048], replicated, may hold values from -160 to 160
- bias_second: float32 [5, 2048], replicated, may hold values from 4096 to 13107.2
- norm_gains: float32 [2, 2048], replicated, may hold values from 0.5 to 1.5
- gains_first: float32 [2, 2048], replicated, may hold values from -112 to 112
- gains_second: float32 [2, 2048], replicated, may hold values from 2252.8 to 7372.8
Outputs:
- output_rows: bfloat16 [4096, 2048], P(('dp', 'tensor'))
- input_gradient: float32 [4096, 2048], P(('dp', 'tensor'))
- entry_gradient: float32 [2048, 3, 2048], P('dp', None, 'tensor')
- entry_updated: float32 [2048, 3, 2048], P('dp', None, 'tensor')
- entry_first_new: float32 [2048, 3, 2048], P('dp', None, 'tensor')
- entry_second_new: float32 [2048, 3, 2048], P('dp', None, 'tensor')
- exit_gradient: float32 [2048, 2048], P('dp', 'tensor')
- exit_updated: float32 [2048, 2048], P('dp', 'tensor')
- exit_first_new: float32 [2048, 2048], P('dp', 'tensor')
- exit_second_new: float32 [2048, 2048], P('dp', 'tensor')
- gate_gradient: float32 [2048, 2, 5632], P('dp', None, 'tensor')
- gate_updated: float32 [2048, 2, 5632], P('dp', None, 'tensor')
- gate_first_new: float32 [2048, 2, 5632], P('dp', None, 'tensor')
- gate_second_new: float32 [2048, 2, 5632], P('dp', None, 'tensor')
- down_gradient: float32 [2048, 5632], P('dp', 'tensor')
- down_updated: float32 [2048, 5632], P('dp', 'tensor')
- down_first_new: float32 [2048, 5632], P('dp', 'tensor')
- down_second_new: float32 [2048, 5632], P('dp', 'tensor')
- bias_gradient: float32 [5, 2048], replicated
- bias_updated: float32 [5, 2048], replicated
- bias_first_new: float32 [5, 2048], replicated
- bias_second_new: float32 [5, 2048], replicated
- gains_gradient: float32 [2, 2048], replicated
- gains_updated: float32 [2, 2048], replicated
- gains_first_new: float32 [2, 2048], replicated
- gains_second_new: float32 [2, 2048], replicated
The draws below stay inside these ranges and needn't reach their ends.
Inputs may be any that keep to these rules, and one draw needn't show every extreme that they name: In each row the nonzero lengths come first and sum to at most 512; some row holds a length equal to 512; every row sums to 256 or more.
All inputs are finite; a program needn't handle non-finite values.
Results may differ from the reference program's by a relative error of at most 0.025.
Values may be sent and summed in bfloat16 or wider, within the bound.
No kernel may reach another device: no remote copies, remote signals or barrier semaphores. Data moves between devices by JAX's collectives and lax.ppermute only.
A program may use at most 192 MiB of HBM per device.

```python
import math
import jax
import jax.numpy as jnp
from jax import lax

D = 2048
H = 32
HD = 64
FF = 5632
ROT = 16
STEP = 3
GROUP_TOK = 512
TOKENS = 4096
SEQ_MAX = 512
SEQS = 6
N_DP = 8


def draw_lengths(key, part):
    key_pieces = jax.random.fold_in(key, 11)
    key_used = jax.random.fold_in(key, 12)
    key_full = jax.random.fold_in(key, 13)
    pieces = jax.random.randint(key_pieces, (N_DP, SEQS), SEQ_MAX // 4, SEQ_MAX + 1, dtype=jnp.int32)
    used = jax.random.randint(key_used, (N_DP, 1), GROUP_TOK // 2, GROUP_TOK + 1, dtype=jnp.int32)
    full_row = jax.random.randint(key_full, (), 0, N_DP, dtype=jnp.int32)
    row_index = jnp.arange(N_DP, dtype=jnp.int32)[:, None]
    column_index = jnp.arange(SEQS, dtype=jnp.int32)[None, :]
    chosen = row_index == full_row
    used = jnp.where(chosen, GROUP_TOK, used)
    pieces = jnp.where(chosen & (column_index == 0), SEQ_MAX, pieces)
    before = jnp.cumsum(pieces, axis=1) - pieces
    return jnp.clip(used - before, 0, pieces).astype(jnp.int32)


def steps_of(key, extent, split, smallest, largest):
    def one(axis_at, shards_of):
        draws = jax.random.uniform(jax.random.fold_in(jax.random.fold_in(key, 6), axis_at), (shards_of,), jnp.float32, smallest / len(split), largest / len(split))
        return jnp.repeat(jnp.exp(draws), extent[axis_at] // shards_of).reshape((-1,) + (1,) * (len(extent) - axis_at - 1))

    level = one(*split[0])
    for cut in split[1:]:
        level = level * one(*cut)
    return level


def gaussian(stream_key, dims, deviation, most, cuts=(), held_as=jnp.bfloat16):
    values = jax.random.normal(stream_key, dims, jnp.float32) * deviation
    if len(cuts) > 0:
        values = steps_of(stream_key, dims, cuts, -0.22, 0.18) * values
    return jnp.clip(values, min=-most, max=most).astype(held_as)


def setup_inputs(seed: int = 0) -> dict:
    streams_of = jax.random.split(jax.random.key(seed), 22)
    return {
        "tokens": gaussian(streams_of[0], (TOKENS, D), 1.0, 6.0, ((0, 32),)),
        "cotangent": gaussian(streams_of[1], (TOKENS, D), 1.0, 6.0, ((0, 32),)),
        "lengths": draw_lengths(jax.random.fold_in(streams_of[21], 71), 0),
        "entry_weight": gaussian(streams_of[3], (D, 3, D), D ** -0.5, 0.125, ((0, 8), (2, 4)), jnp.float32),
        "entry_first": gaussian(streams_of[4], (D, 3, D), (0.4 * TOKENS ** 0.5), 160.0, ((0, 8), (2, 4)), jnp.float32),
        "entry_second": jnp.clip(jnp.exp(math.log(13107.2) - 1.1631508 * jax.random.uniform(streams_of[5], (D, 3, D), jnp.float32) ** steps_of(streams_of[5], (D, 3, D), ((0, 8), (2, 4)), -0.2, 0.2)), 4096.0, 13107.2),
        "exit_weight": gaussian(streams_of[6], (D, D), (D // 64) ** -0.5, 1.0, ((0, 8), (1, 4)), jnp.float32),
        "exit_first": gaussian(streams_of[7], (D, D), (0.05 * TOKENS ** 0.5), 20.0, ((0, 8), (1, 4)), jnp.float32),
        "exit_second": jnp.clip(jnp.exp(math.log(204.8) - 1.2039728 * jax.random.uniform(streams_of[8], (D, D), jnp.float32) ** steps_of(streams_of[8], (D, D), ((0, 8), (1, 4)), -0.2, 0.2)), 61.44, 204.8),
        "gate_weight": gaussian(streams_of[9], (D, 2, FF), D ** -0.5, 0.125, ((0, 8), (2, 4)), jnp.float32),
        "gate_first": gaussian(streams_of[10], (D, 2, FF), (0.06 * TOKENS ** 0.5), 24.0, ((0, 8), (2, 4)), jnp.float32),
        "gate_second": jnp.clip(jnp.exp(math.log(286.72) - 1.252763 * jax.random.uniform(streams_of[11], (D, 2, FF), jnp.float32) ** steps_of(streams_of[11], (D, 2, FF), ((0, 8), (2, 4)), -0.2, 0.2)), 81.92, 286.72),
        "down_weight": gaussian(streams_of[12], (D, FF), FF ** -0.5, 0.078125, ((0, 8), (1, 4)), jnp.float32),
        "down_first": gaussian(streams_of[13], (D, FF), (0.06 * TOKENS ** 0.5), 24.0, ((0, 8), (1, 4)), jnp.float32),
        "down_second": jnp.clip(jnp.exp(math.log(286.72) - 1.252763 * jax.random.uniform(streams_of[14], (D, FF), jnp.float32) ** steps_of(streams_of[14], (D, FF), ((0, 8), (1, 4)), -0.2, 0.2)), 81.92, 286.72),
        "bias_rows": gaussian(streams_of[15], (5, D), 0.5, 3.0, (), jnp.float32),
        "bias_first": gaussian(streams_of[16], (5, D), (0.4 * TOKENS ** 0.5), 160.0, (), jnp.float32),
        "bias_second": jnp.clip(jnp.exp(jax.random.uniform(streams_of[17], (5, D), jnp.float32, math.log(4096.0), math.log(13107.2))), 4096.0, 13107.2),
        "norm_gains": jnp.clip(1.0 + 0.1 * jax.random.normal(streams_of[18], (2, D), jnp.float32), 0.5, 1.5),
        "gains_first": gaussian(streams_of[19], (2, D), (0.3 * TOKENS ** 0.5), 112.0, (), jnp.float32),
        "gains_second": jnp.clip(jnp.exp(jax.random.uniform(streams_of[20], (2, D), jnp.float32, math.log(2252.8), math.log(7372.8))), 2252.8, 7372.8),
    }


@jax.custom_vjp
def low(v):
    return lax.optimization_barrier(v.astype(jnp.bfloat16)).astype(jnp.float32)

@jax.custom_vjp
def low_back(v):
    return v

def low_keep(v):
    return (low(v), None)

def low_pass(kept, grad):
    return (grad,)

def back_keep(v):
    return (v, None)

def back_low(kept, grad):
    return (low(grad),)
low.defvjp(low_keep, low_pass)
low_back.defvjp(back_keep, back_low)
highest = lax.Precision.HIGHEST
norm_eps = 1e-05
rope_base = 10000.0
masked_score = -1e+30
beta_one = 0.9
beta_two = 0.95
adam_eps = 1e-08
matrix_rate = 0.08
vector_rate = 0.4
weight_decay = 0.1

def layer_norm(rows, gain, shift):
    centre = lax.optimization_barrier(jnp.mean(rows, axis=-1, keepdims=True))
    centred = rows - centre
    spread = lax.optimization_barrier(jnp.mean(centred * centred, axis=-1, keepdims=True))
    return centred * lax.rsqrt(spread + norm_eps) * gain + shift

def segments(lengths_row, count):
    ends = jnp.cumsum(lengths_row.astype(jnp.int32)).astype(jnp.int32)
    index = jnp.arange(count, dtype=jnp.int32)
    after = index[:, None] >= ends[None, :]
    segment = lax.optimization_barrier(jnp.sum(after.astype(jnp.int32), axis=1)).astype(jnp.int32)
    begin = lax.optimization_barrier(jnp.max(jnp.where(after, ends[None, :], jnp.zeros_like(ends)[None, :]), axis=1))
    return (segment, (index - begin).astype(jnp.int32))

def rotary_tables(positions):
    half = ROT // 2
    freqs = rope_base ** (-2.0 * jnp.arange(half, dtype=jnp.float32) / ROT)
    angles = positions[:, None] * freqs[None, :]
    return (jnp.cos(angles), jnp.sin(angles))

def rotate(heads, cosine, sine):
    half = ROT // 2
    first = heads[..., :half]
    second = heads[..., half:ROT]
    cosine = cosine[:, None, :]
    sine = sine[:, None, :]
    return jnp.concatenate([first * cosine - second * sine, second * cosine + first * sine, heads[..., ROT:]], axis=-1)

def forward(rows, entry_weight, exit_weight, gate_weight, down_weight, bias_rows, norm_gains, segment, positions):
    count = rows.shape[0]
    normed = low(layer_norm(rows, norm_gains[0], bias_rows[3]))
    mixed = jnp.einsum('nd,dkc->nkc', normed, low(entry_weight), precision=highest)
    rotmask = (jnp.arange(D, dtype=jnp.int32) % HD < ROT).astype(jnp.float32)
    offsets = jnp.stack([bias_rows[0], bias_rows[1] * rotmask, bias_rows[2]])
    mixed = low_back(mixed + offsets[None])
    cosine, sine = rotary_tables(positions)
    queries = low(rotate(mixed[:, 0].reshape(count, H, HD), cosine, sine))
    keys = low(rotate(mixed[:, 1].reshape(count, H, HD), cosine, sine))
    values = low(mixed[:, 2].reshape(count, H, HD))
    block = min(512, count)
    starts = jnp.arange(count // block, dtype=jnp.int32) * block
    key_index = jnp.arange(count, dtype=jnp.int32)
    score_scale = HD ** (-0.5)

    def attend(start):
        query_block = lax.dynamic_slice_in_dim(queries, start, block, 0)
        segment_block = lax.dynamic_slice_in_dim(segment, start, block, 0)
        index = start + jnp.arange(block, dtype=jnp.int32)
        scores = low_back(score_scale * jnp.einsum('qhd,khd->hqk', query_block, keys, precision=highest))
        visible = (segment_block[:, None] == segment[None, :]) & (index[:, None] >= key_index[None, :])
        scores = jnp.where(visible[None], scores, masked_score)
        summit = lax.optimization_barrier(jnp.max(scores, axis=-1, keepdims=True))
        weights = jnp.exp(scores - summit)
        weights = weights / lax.optimization_barrier(jnp.sum(weights, axis=-1, keepdims=True))
        return jnp.einsum('hqk,khd->qhd', low(weights), values, precision=highest)
    attended = lax.map(jax.checkpoint(attend), starts)
    context = low_back(low(attended.reshape(count, D)))
    branch = jnp.dot(context, low(exit_weight).T, precision=highest, preferred_element_type=jnp.float32)
    middle = rows + low_back(branch)
    second = low(layer_norm(middle, norm_gains[1], bias_rows[4]))
    gate_up = low_back(jnp.einsum('nd,dkf->nkf', second, low(gate_weight), precision=highest))
    hidden = low(jax.nn.silu(gate_up[:, 0]) * gate_up[:, 1])
    branch_two = jnp.dot(hidden, low(down_weight).T, precision=highest, preferred_element_type=jnp.float32)
    return middle + low_back(branch_two)

def adamw(weight, first, second, gradient, rate, decay):
    first_new = beta_one * first + (1.0 - beta_one) * gradient
    second_new = beta_two * second + (1.0 - beta_two) * gradient * gradient
    first_hat = first_new / (1.0 - beta_one ** STEP)
    second_hat = second_new / (1.0 - beta_two ** STEP)
    updated = weight - rate * (first_hat / (jnp.sqrt(second_hat) + adam_eps) + decay * weight)
    return (updated, first_new, second_new)

def reference(tokens, cotangent, lengths, entry_weight, entry_first, entry_second, exit_weight, exit_first, exit_second, gate_weight, gate_first, gate_second, down_weight, down_first, down_second, bias_rows, bias_first, bias_second, norm_gains, gains_first, gains_second):
    params = (entry_weight, exit_weight, gate_weight, down_weight, bias_rows, norm_gains)
    group_rows = tokens.astype(jnp.float32).reshape(N_DP, GROUP_TOK, D)
    group_cotangent = cotangent.astype(jnp.float32).reshape(N_DP, GROUP_TOK, D)

    def one_group(totals, inputs):
        rows, cotangent_rows, lengths_row = inputs
        segment, positions = segments(lengths_row, GROUP_TOK)
        positions = positions.astype(jnp.float32)

        def closed(rows, entry, exits, gates, downs, biases, gains):
            return forward(rows, entry, exits, gates, downs, biases, gains, segment, positions)
        result, pullback = jax.vjp(closed, rows, *params)
        grads = pullback(cotangent_rows)
        totals = tuple((total + piece for total, piece in zip(totals, grads[1:])))
        return (totals, (result, grads[0]))
    zeros = tuple((jnp.zeros_like(param) for param in params))
    totals, (results, input_grads) = lax.scan(one_group, zeros, (group_rows, group_cotangent, lengths))
    output_rows = results.reshape(TOKENS, D).astype(jnp.bfloat16)
    input_gradient = input_grads.reshape(TOKENS, D)
    firsts = (entry_first, exit_first, gate_first, down_first, bias_first, gains_first)
    seconds = (entry_second, exit_second, gate_second, down_second, bias_second, gains_second)
    rates = (matrix_rate, matrix_rate, matrix_rate, matrix_rate, vector_rate, vector_rate)
    decays = (weight_decay, weight_decay, weight_decay, weight_decay, 0.0, 0.0)
    pieces = []
    for param, first, second, gradient, rate, decay in zip(params, firsts, seconds, totals, rates, decays):
        updated, first_new, second_new = adamw(param, first, second, gradient, rate, decay)
        pieces.extend([gradient, updated, first_new, second_new])
    return (output_rows, input_gradient, pieces[0], pieces[1], pieces[2], pieces[3], pieces[4], pieces[5], pieces[6], pieces[7], pieces[8], pieces[9], pieces[10], pieces[11], pieces[12], pieces[13], pieces[14], pieces[15], pieces[16], pieces[17], pieces[18], pieces[19], pieces[20], pieces[21], pieces[22], pieces[23])
```

```python
import jax
import jax.numpy as jnp
from jax import lax
from jax.sharding import PartitionSpec as P

HD = 64
ROT = 16
STEP = 3


norm_eps = 1e-05
rope_base = 10000.0
masked_score = -1e30
beta_one = 0.9
beta_two = 0.95
adam_eps = 1e-08
matrix_rate = 0.08
vector_rate = 0.4
weight_decay = 0.1


def norm_forward(rows, gain, shift):
    centre = jnp.mean(rows, axis=-1, keepdims=True)
    centred = rows - centre
    spread = jnp.mean(centred * centred, axis=-1, keepdims=True)
    factor = lax.rsqrt(spread + norm_eps)
    unit = centred * factor
    return (unit * gain + shift, unit, factor)


def norm_backward(incoming, unit, factor, gain):
    scaled = incoming * gain
    mean_plain = jnp.mean(scaled, axis=-1, keepdims=True)
    mean_along = jnp.mean(scaled * unit, axis=-1, keepdims=True)
    return factor * (scaled - mean_plain - unit * mean_along)


def segments(lengths_row, count):
    ends = jnp.cumsum(lengths_row)
    index = jnp.arange(count, dtype=jnp.int32)
    after = index[:, None] >= ends[None, :]
    segment = jnp.sum(after.astype(jnp.int32), axis=1)
    begin = jnp.max(jnp.where(after, ends[None, :], jnp.zeros_like(ends)[None, :]), axis=1)
    return (segment, index - begin)


def rotary_tables(positions):
    half = ROT // 2
    freqs = rope_base ** (-2.0 * jnp.arange(half, dtype=jnp.float32) / ROT)
    angles = positions[:, None] * freqs[None, :]
    return (jnp.cos(angles), jnp.sin(angles))


def rotate(heads, cosine, sine, direction):
    half = ROT // 2
    first = heads[..., :half]
    second = heads[..., half:ROT]
    cosine = cosine[:, None, :]
    sine = direction * sine[:, None, :]
    return jnp.concatenate(
        [first * cosine - second * sine, second * cosine + first * sine, heads[..., ROT:]], axis=-1
    )


def adamw(weight, first, second, gradient, rate, decay):
    first_new = beta_one * first + (1.0 - beta_one) * gradient
    second_new = beta_two * second + (1.0 - beta_two) * gradient * gradient
    first_hat = first_new / (1.0 - beta_one**STEP)
    second_hat = second_new / (1.0 - beta_two**STEP)
    updated = weight - rate * (first_hat / (jnp.sqrt(second_hat) + adam_eps) + decay * weight)
    return (updated, first_new, second_new)


MLP_CHUNKS = 4


def pairs_up(lines, low, high, step):
    return [(z * 2 + c, (z + step) * 2 + c) for z in range(low, high) for c in range(2)]


def other_core(array):
    count = lax.axis_size("dp")
    return lax.ppermute(array, "dp", [(d, d ^ 1) for d in range(count)])


def line_gather(own, place, lines):
    ups, downs = [own], [own]
    for s in range(1, lines):
        ups.append(lax.ppermute(ups[-1], "dp", pairs_up(lines, s - 1, lines - 1, 1)))
        downs.append(lax.ppermute(downs[-1], "dp", pairs_up(lines, 1, lines - s + 1, -1)))
    return [own] + [jnp.where(place >= s, ups[s], downs[lines - s]) for s in range(1, lines)]


def full_gather(own, place, lines):
    half = jnp.concatenate(line_gather(own, place, lines), axis=0)
    return jnp.concatenate([half, other_core(half)], axis=0)


def line_scatter(blocks, lines):
    up = None
    down = None
    for j in range(lines - 1, 0, -1):
        up_send = blocks[lines - j] if up is None else blocks[lines - j] + up
        up = lax.ppermute(up_send, "dp", pairs_up(lines, 0, lines - j, 1))
        down_send = blocks[j] if down is None else blocks[j] + down
        down = lax.ppermute(down_send, "dp", pairs_up(lines, j, lines, -1))
    total = blocks[0].astype(jnp.float32)
    if up is not None:
        total = total + up.astype(jnp.float32) + down.astype(jnp.float32)
    return total


def swap_rows(array, offset):
    count = lax.axis_size("tensor")
    return lax.ppermute(array, "tensor", [(t, t ^ offset) for t in range(count)])


def gather_rows(own, parts):
    return jnp.concatenate([own] + [swap_rows(own, r) for r in range(1, parts)], axis=0)


def scatter_rows(partial, parts):
    rows = partial.shape[0] // parts
    total = partial[:rows].astype(jnp.float32)
    for r in range(1, parts):
        total = total + swap_rows(partial[r * rows : (r + 1) * rows], r).astype(jnp.float32)
    return total


def sum_all(array):
    for axis in ("dp", "tensor"):
        count = lax.axis_size(axis)
        bit = 1
        while bit < count:
            array = array + lax.ppermute(array, axis, [(i, i ^ bit) for i in range(count)])
            bit *= 2
    return array


def pick_blocks(array, indices, size):
    return jnp.concatenate(
        [lax.dynamic_slice_in_dim(array, i * size, size, array.ndim - 1) for i in indices], axis=-1
    )


def cuts(columns, count):
    tiles = -(-columns // 128)
    bounds = [min(columns, 128 * ((tiles * i + count - 1) // count)) for i in range(count + 1)]
    return [(a, b) for a, b in zip(bounds[:-1], bounds[1:]) if b > a]


def dot(a, b, contract):
    return lax.dot_general(a, b, (contract, ((), ())), preferred_element_type=jnp.float32)


def on_device(
    tokens,
    cotangent,
    lengths,
    entry_weight,
    entry_first,
    entry_second,
    exit_weight,
    exit_first,
    exit_second,
    gate_weight,
    gate_first,
    gate_second,
    down_weight,
    down_first,
    down_second,
    bias_rows,
    bias_first,
    bias_second,
    norm_gains,
    gains_first,
    gains_second,
):
    parts = lax.axis_size("tensor")
    part_index = lax.axis_index("tensor")
    dp_index = lax.axis_index("dp")
    dp_count = lax.axis_size("dp")
    lines = dp_count // 2
    place = dp_index // 2
    core = dp_index % 2
    local_rows = tokens.shape[0]
    group = local_rows * parts
    width = tokens.shape[1]
    halfwidth = width // 2
    size = width // dp_count
    head_cols = entry_weight.shape[2]
    hidden_cols = down_weight.shape[1]
    local_heads = head_cols // HD
    score_scale = HD ** (-0.5)
    bf16 = jnp.bfloat16

    to_mine = [
        ((place - s + lines) % lines) * 2 + (core ^ cc) for cc in range(2) for s in range(lines)
    ]
    to_whole = [
        (core ^ c) * lines + (place - z + lines) % lines for z in range(lines) for c in range(2)
    ]
    rows_bf = pick_blocks(tokens, to_mine, size)
    cot_bf = pick_blocks(cotangent, to_mine, size)
    gains_mine = pick_blocks(norm_gains, to_mine, size)
    shifts_mine = pick_blocks(bias_rows[3:5], to_mine, size)
    rows_in = rows_bf.astype(jnp.float32)

    entry_full = full_gather(
        entry_weight.astype(bf16).reshape(size, 3 * head_cols), place, lines
    )
    exit_full = full_gather(exit_weight.astype(bf16), place, lines)
    chunks = cuts(hidden_cols, MLP_CHUNKS)
    mlp_full = [
        full_gather(
            jnp.concatenate(
                [
                    gate_weight[:, 0, a:b].astype(bf16),
                    gate_weight[:, 1, a:b].astype(bf16),
                    down_weight[:, a:b].astype(bf16),
                ],
                axis=1,
            ),
            place,
            lines,
        )
        for a, b in chunks
    ]

    segment, positions = segments(lengths[0], group)
    row_blocks = jnp.arange(parts, dtype=jnp.int32) ^ part_index
    row_index = (
        row_blocks[:, None] * local_rows + jnp.arange(local_rows, dtype=jnp.int32)[None, :]
    ).reshape(group)
    segment = jnp.concatenate(
        [
            lax.dynamic_slice_in_dim(segment, (part_index ^ r) * local_rows, local_rows, 0)
            for r in range(parts)
        ]
    )
    positions = jnp.concatenate(
        [
            lax.dynamic_slice_in_dim(positions, (part_index ^ r) * local_rows, local_rows, 0)
            for r in range(parts)
        ]
    )
    cosine, sine = rotary_tables(positions.astype(jnp.float32))
    column_start = part_index * head_cols
    rotmask = (jnp.arange(head_cols, dtype=jnp.int32) % HD < ROT).astype(jnp.float32)
    query_bias = lax.dynamic_slice_in_dim(bias_rows[0], column_start, head_cols, 0)
    key_bias = lax.dynamic_slice_in_dim(bias_rows[1], column_start, head_cols, 0) * rotmask
    value_bias = lax.dynamic_slice_in_dim(bias_rows[2], column_start, head_cols, 0)
    offsets = jnp.concatenate([query_bias, key_bias, value_bias])

    normed, unit_one, factor_one = norm_forward(rows_in, gains_mine[0], shifts_mine[0])
    normed_all = gather_rows(normed.astype(bf16), parts)
    normed_other = other_core(normed_all[:, halfwidth:])
    mixed = dot(normed_all, entry_full, ((1,), (0,))) + offsets[None]
    queries = rotate(
        mixed[:, :head_cols].reshape(group, local_heads, HD), cosine, sine, 1.0
    ).astype(bf16)
    keys = rotate(
        mixed[:, head_cols : 2 * head_cols].reshape(group, local_heads, HD), cosine, sine, 1.0
    ).astype(bf16)
    values = mixed[:, 2 * head_cols :].reshape(group, local_heads, HD).astype(bf16)
    visible = (segment[:, None] == segment[None, :]) & (row_index[:, None] >= row_index[None, :])

    def all_scores():
        scores = score_scale * jnp.einsum(
            "qhd,khd->hqk", queries, keys, preferred_element_type=jnp.float32
        )
        return jnp.where(visible[None], scores, masked_score)

    scores = all_scores()
    summit = jnp.max(scores, axis=-1, keepdims=True)
    weights = jnp.exp(scores - summit)
    totals = jnp.sum(weights, axis=-1, keepdims=True)
    probs = (weights / totals).astype(bf16)
    attended = jnp.einsum("hqk,khd->qhd", probs, values, preferred_element_type=jnp.float32)
    log_totals = summit + jnp.log(totals)
    context = attended.reshape(group, head_cols).astype(bf16)
    context_other = other_core(context)
    branch = scatter_rows(dot(context, exit_full, ((1,), (1,))).astype(bf16), parts)
    middle = rows_in + branch
    second, unit_two, factor_two = norm_forward(middle, gains_mine[1], shifts_mine[1])
    second_all = gather_rows(second.astype(bf16), parts)
    second_other = other_core(second_all[:, halfwidth:])
    cot_all = gather_rows(cot_bf, parts)
    cot_other = other_core(cot_all[:, halfwidth:])

    branch_two = jnp.zeros((group, width), jnp.float32)
    second_grad = jnp.zeros((group, width), jnp.float32)
    gate_pieces, down_pieces = [], []
    for (a, b), full in zip(chunks, mlp_full):
        n = b - a
        gate_up = dot(second_all, full[:, : 2 * n], ((1,), (0,)))
        gate = gate_up[:, :n]
        upper = gate_up[:, n:]
        sigmoid = jax.nn.sigmoid(gate)
        activated = gate * sigmoid
        hidden = (activated * upper).astype(bf16)
        hidden_grad = dot(cot_all, full[:, 2 * n :], ((1,), (0,)))
        gate_grad = hidden_grad * upper * sigmoid * (1.0 + gate * (1.0 - sigmoid))
        upper_grad = hidden_grad * activated
        gate_up_grad = jnp.concatenate([gate_grad, upper_grad], axis=1).astype(bf16)
        branch_two = branch_two + dot(hidden, full[:, 2 * n :], ((1,), (1,)))
        second_grad = second_grad + dot(gate_up_grad, full[:, : 2 * n], ((1,), (1,)))
        hidden_other = other_core(hidden)
        gate_up_other = other_core(gate_up_grad)
        gate_term = dot(second_all[:, :halfwidth], gate_up_grad, ((0,), (0,))) + dot(
            second_other, gate_up_other, ((0,), (0,))
        )
        down_term = dot(cot_all[:, :halfwidth], hidden, ((0,), (0,))) + dot(
            cot_other, hidden_other, ((0,), (0,))
        )
        terms = jnp.concatenate([gate_term, down_term], axis=1).astype(bf16)
        total = line_scatter([terms[s * size : (s + 1) * size] for s in range(lines)], lines)
        gate_pieces.append(total[:, : 2 * n].reshape(size, 2, n))
        down_pieces.append(total[:, 2 * n :])
    gate_gradient = jnp.concatenate(gate_pieces, axis=2)
    down_gradient = jnp.concatenate(down_pieces, axis=1)

    second_grad = scatter_rows(second_grad.astype(bf16), parts)
    middle_grad = cot_bf.astype(jnp.float32) + norm_backward(
        second_grad, unit_two, factor_two, gains_mine[1]
    )
    gain_two_grad = jnp.sum(second_grad * unit_two, axis=0)
    shift_two_grad = jnp.sum(second_grad, axis=0)
    middle_all = gather_rows(middle_grad.astype(bf16), parts)
    middle_other = other_core(middle_all[:, halfwidth:])
    branch_two = scatter_rows(branch_two.astype(bf16), parts)
    output_rows = pick_blocks((middle + branch_two).astype(bf16), to_whole, size)

    exit_terms = (
        dot(middle_all[:, :halfwidth], context, ((0,), (0,)))
        + dot(middle_other, context_other, ((0,), (0,)))
    ).astype(bf16)
    exit_gradient = line_scatter([exit_terms[s * size : (s + 1) * size] for s in range(lines)], lines)
    context_grad = dot(middle_all, exit_full, ((1,), (0,)))
    context_grad = context_grad.astype(bf16).reshape(group, local_heads, HD)

    scores = all_scores()
    probs = jnp.exp(scores - log_totals)
    prob_grad = jnp.einsum("qhd,khd->hqk", context_grad, values, preferred_element_type=jnp.float32)
    inner = jnp.sum(probs * prob_grad, axis=-1, keepdims=True)
    score_grad = (probs * (prob_grad - inner)).astype(bf16)
    query_grad = score_scale * jnp.einsum(
        "hqk,khd->qhd", score_grad, keys, preferred_element_type=jnp.float32
    )
    key_grad = score_scale * jnp.einsum(
        "hqk,qhd->khd", score_grad, queries, preferred_element_type=jnp.float32
    )
    value_grad = jnp.einsum(
        "hqk,qhd->khd", probs.astype(bf16), context_grad, preferred_element_type=jnp.float32
    )
    query_grad = rotate(query_grad, cosine, sine, -1.0)
    key_grad = rotate(key_grad, cosine, sine, -1.0)
    mixed_grad = jnp.concatenate(
        [
            query_grad.reshape(group, head_cols),
            key_grad.reshape(group, head_cols),
            value_grad.reshape(group, head_cols),
        ],
        axis=1,
    ).astype(bf16)
    mixed_other = other_core(mixed_grad)
    entry_terms = (
        dot(normed_all[:, :halfwidth], mixed_grad, ((0,), (0,)))
        + dot(normed_other, mixed_other, ((0,), (0,)))
    ).astype(bf16)
    entry_gradient = line_scatter(
        [entry_terms[s * size : (s + 1) * size] for s in range(lines)], lines
    ).reshape(size, 3, head_cols)
    normed_grad = scatter_rows(dot(mixed_grad, entry_full, ((1,), (1,))).astype(bf16), parts)
    input_gradient = middle_grad + norm_backward(normed_grad, unit_one, factor_one, gains_mine[0])
    input_gradient = pick_blocks(input_gradient, to_whole, size)
    gain_one_grad = jnp.sum(normed_grad * unit_one, axis=0)
    shift_one_grad = jnp.sum(normed_grad, axis=0)

    column_sums = jnp.sum(mixed_grad.astype(jnp.float32), axis=0).reshape(3, head_cols)
    column_sums = column_sums * jnp.stack([jnp.ones_like(rotmask), rotmask, jnp.ones_like(rotmask)])
    placed = lax.dynamic_update_slice_in_dim(
        jnp.zeros((3, width), jnp.float32), column_sums, column_start, 1
    )
    norms_local = pick_blocks(
        jnp.stack([shift_one_grad, shift_two_grad, gain_one_grad, gain_two_grad]), to_whole, size
    )
    vectors = sum_all(jnp.concatenate([placed, norms_local], axis=0))
    bias_gradient = vectors[:5]
    gains_gradient = vectors[5:]
    entry_updated, entry_first_new, entry_second_new = adamw(
        entry_weight, entry_first, entry_second, entry_gradient, matrix_rate, weight_decay
    )
    exit_updated, exit_first_new, exit_second_new = adamw(
        exit_weight, exit_first, exit_second, exit_gradient, matrix_rate, weight_decay
    )
    gate_updated, gate_first_new, gate_second_new = adamw(
        gate_weight, gate_first, gate_second, gate_gradient, matrix_rate, weight_decay
    )
    down_updated, down_first_new, down_second_new = adamw(
        down_weight, down_first, down_second, down_gradient, matrix_rate, weight_decay
    )
    bias_updated, bias_first_new, bias_second_new = adamw(
        bias_rows, bias_first, bias_second, bias_gradient, vector_rate, 0.0
    )
    gains_updated, gains_first_new, gains_second_new = adamw(
        norm_gains, gains_first, gains_second, gains_gradient, vector_rate, 0.0
    )
    return (
        output_rows,
        input_gradient,
        entry_gradient,
        entry_updated,
        entry_first_new,
        entry_second_new,
        exit_gradient,
        exit_updated,
        exit_first_new,
        exit_second_new,
        gate_gradient,
        gate_updated,
        gate_first_new,
        gate_second_new,
        down_gradient,
        down_updated,
        down_first_new,
        down_second_new,
        bias_gradient,
        bias_updated,
        bias_first_new,
        bias_second_new,
        gains_gradient,
        gains_updated,
        gains_first_new,
        gains_second_new,
    )


def solution(mesh):
    return jax.shard_map(
        on_device,
        mesh=mesh,
        in_specs=(
            P(("dp", "tensor"), None),
            P(("dp", "tensor"), None),
            P("dp", None),
            P("dp", None, "tensor"),
            P("dp", None, "tensor"),
            P("dp", None, "tensor"),
            P("dp", "tensor"),
            P("dp", "tensor"),
            P("dp", "tensor"),
            P("dp", None, "tensor"),
            P("dp", None, "tensor"),
            P("dp", None, "tensor"),
            P("dp", "tensor"),
            P("dp", "tensor"),
            P("dp", "tensor"),
            P(),
            P(),
            P(),
            P(),
            P(),
            P(),
        ),
        out_specs=(
            P(("dp", "tensor"), None),
            P(("dp", "tensor"), None),
            P("dp", None, "tensor"),
            P("dp", None, "tensor"),
            P("dp", None, "tensor"),
            P("dp", None, "tensor"),
            P("dp", "tensor"),
            P("dp", "tensor"),
            P("dp", "tensor"),
            P("dp", "tensor"),
            P("dp", None, "tensor"),
            P("dp", None, "tensor"),
            P("dp", None, "tensor"),
            P("dp", None, "tensor"),
            P("dp", "tensor"),
            P("dp", "tensor"),
            P("dp", "tensor"),
            P("dp", "tensor"),
            P(),
            P(),
            P(),
            P(),
            P(),
            P(),
            P(),
            P(),
        ),
        check_vma=False,
    )
```

```python
import jax
import jax.numpy as jnp
from jax import lax
from jax.experimental import pallas as pl
from jax.experimental.pallas import tpu as pltpu
from jax.sharding import PartitionSpec as P

HD = 64
ROT = 16
STEP = 3
MLP_CHUNKS = 2


norm_eps = 1e-05
rope_base = 10000.0
masked_score = -1e30
beta_one = 0.9
beta_two = 0.95
adam_eps = 1e-08
matrix_rate = 0.08
vector_rate = 0.4
weight_decay = 0.1


def norm_forward(rows, gain, shift):
    centre = jnp.mean(rows, axis=-1, keepdims=True)
    centred = rows - centre
    spread = jnp.mean(centred * centred, axis=-1, keepdims=True)
    factor = lax.rsqrt(spread + norm_eps)
    unit = centred * factor
    return (unit * gain + shift, unit, factor)


def norm_backward(incoming, unit, factor, gain):
    scaled = incoming * gain
    mean_plain = jnp.mean(scaled, axis=-1, keepdims=True)
    mean_along = jnp.mean(scaled * unit, axis=-1, keepdims=True)
    return factor * (scaled - mean_plain - unit * mean_along)


def segments(lengths_row, count):
    ends = jnp.cumsum(lengths_row)
    index = jnp.arange(count, dtype=jnp.int32)
    after = index[:, None] >= ends[None, :]
    segment = jnp.sum(after.astype(jnp.int32), axis=1)
    begin = jnp.max(jnp.where(after, ends[None, :], jnp.zeros_like(ends)[None, :]), axis=1)
    return (segment, index - begin)


def rotary_tables(positions):
    half = ROT // 2
    freqs = rope_base ** (-2.0 * jnp.arange(half, dtype=jnp.float32) / ROT)
    angles = positions[:, None] * freqs[None, :]
    return (jnp.cos(angles), jnp.sin(angles))


def adamw(weight, first, second, gradient, rate, decay):
    first_new = beta_one * first + (1.0 - beta_one) * gradient
    second_new = beta_two * second + (1.0 - beta_two) * gradient * gradient
    first_hat = first_new / (1.0 - beta_one**STEP)
    second_hat = second_new / (1.0 - beta_two**STEP)
    updated = weight - rate * (first_hat / (jnp.sqrt(second_hat) + adam_eps) + decay * weight)
    return (updated, first_new, second_new)


def together(*groups):
    flat, tree = jax.tree.flatten(groups)
    return jax.tree.unflatten(tree, lax.optimization_barrier(flat))


def after(value, *earlier):
    return lax.optimization_barrier((value,) + tuple(earlier))[0]


def pairs_up(lines, low, high, step):
    return [(z * 2 + c, (z + step) * 2 + c) for z in range(low, high) for c in range(2)]


def other_core(array):
    count = lax.axis_size("dp")
    return lax.ppermute(array, "dp", [(d, d ^ 1) for d in range(count)])


def scatter_step(blocks, up, down, j, lines):
    up_send = blocks[lines - j] if up is None else blocks[lines - j] + up
    down_send = blocks[j] if down is None else blocks[j] + down
    up = lax.ppermute(up_send, "dp", pairs_up(lines, 0, lines - j, 1))
    down = lax.ppermute(down_send, "dp", pairs_up(lines, j, lines, -1))
    return up, down


def swap_rows(array, offset):
    count = lax.axis_size("tensor")
    return lax.ppermute(array, "tensor", [(t, t ^ offset) for t in range(count)])


def gather_rows(own, parts):
    return jnp.concatenate([own] + [swap_rows(own, r) for r in range(1, parts)], axis=0)


def scatter_rows(partial, parts):
    rows = partial.shape[0] // parts
    total = partial[:rows].astype(jnp.float32)
    for r in range(1, parts):
        total = total + swap_rows(partial[r * rows : (r + 1) * rows], r).astype(jnp.float32)
    return total


def together_streams(streams, others):
    ways, blocks, others = together(
        [way for _, way, _ in streams], [blocks for blocks, _, _ in streams], others
    )
    return [(b, w, left) for b, w, (_, _, left) in zip(blocks, ways, streams)], others


def add_terms(terms):
    total = terms[0].astype(jnp.float32)
    for term in terms[1:]:
        total = total + term.astype(jnp.float32)
    return total.astype(jnp.bfloat16)


def hop(array, axis, bit):
    count = lax.axis_size(axis)
    return array + lax.ppermute(array, axis, [(i, i ^ bit) for i in range(count)])


def cuts(columns, count):
    tiles = -(-columns // 128)
    bounds = [min(columns, 128 * (tiles * i // count)) for i in range(count + 1)]
    return [(a, b) for a, b in zip(bounds[:-1], bounds[1:]) if b > a]


def paired(array):
    rows, kinds, columns = array.shape
    array = jnp.pad(array, ((0, 0), (0, 0), (0, -columns % 128)))
    return jnp.swapaxes(array.reshape(rows, kinds, -1, 128), 1, 2)


def dot(a, b, contract):
    return lax.dot_general(a, b, (contract, ((), ())), preferred_element_type=jnp.float32)


def whole(shape):
    return pl.BlockSpec(shape, lambda *_: (0,) * len(shape))


def kernel_call(kernel, grid, in_specs, out_specs, out_shape, scratch, name, flops=1, moved=1):
    return pl.pallas_call(
        kernel,
        grid=grid,
        in_specs=in_specs,
        out_specs=out_specs,
        out_shape=out_shape,
        scratch_shapes=scratch,
        compiler_params=pltpu.CompilerParams(vmem_limit_bytes=56 * 1024 * 1024),
        cost_estimate=pl.CostEstimate(flops=flops, bytes_accessed=moved, transcendentals=0),
        name=name,
    )


def turn(x, keep, low, high, direction):
    return (
        x * keep
        + pltpu.roll(x, 120, 1) * (low * direction)
        + pltpu.roll(x, 8, 1) * (high * direction)
    )


def row_steps(rows):
    return 128 if rows % 128 == 0 else rows


def fill_bias(bias_ref, column_ref, row_ref):
    rows = bias_ref.shape[0]
    step = row_steps(rows)

    def body(r, _):
        at = pl.ds(pl.multiple_of(r * step, step), step)
        marks = column_ref[at, :]
        visible = (marks[:, 0:1] == row_ref[0:1, :]) & (marks[:, 1:2] >= row_ref[1:2, :])
        bias_ref[at, :] = jnp.where(visible, 0.0, masked_score)
        return 0

    lax.fori_loop(0, rows // step, body, 0)


def matmul(a, b, contract=((1,), (0,))):
    return lax.dot_general(a, b, (contract, ((), ())), preferred_element_type=jnp.float32)


def attend_kernel(
    normed_ref, weight_ref, offset_ref, keep_ref, low_ref, high_ref, column_ref, row_ref,
    mixed_ref, context_ref, totals_ref, bias_ref, score_ref, prob_ref,
):
    kind = pl.program_id(0)
    rows, columns = context_ref.shape
    step = row_steps(rows)
    raw = matmul(normed_ref[...], weight_ref[0]) + offset_ref[0]
    here = pl.multiple_of(kind * columns, 128)

    @pl.when(kind < 2)
    def _():
        for b in range(columns // 128):
            block = turn(raw[:, b * 128 : (b + 1) * 128], keep_ref[...], low_ref[...], high_ref[...], 1.0)
            mixed_ref[:, pl.ds(pl.multiple_of(here + b * 128, 128), 128)] = block.astype(jnp.bfloat16)

    @pl.when(kind == 2)
    def _():
        mixed_ref[:, pl.ds(here, columns)] = raw.astype(jnp.bfloat16)
        fill_bias(bias_ref, column_ref, row_ref)
        lane = lax.broadcasted_iota(jnp.int32, (1, 128), 1)

        def pair_body(pair, _):
            first = pl.multiple_of(pair * 128, 128)
            queries = mixed_ref[:, pl.ds(first, 128)]
            keys = mixed_ref[:, pl.ds(pl.multiple_of(columns + first, 128), 128)]
            values = mixed_ref[:, pl.ds(pl.multiple_of(2 * columns + first, 128), 128)]
            parts = []
            for h in range(2):
                mine = (lane >= HD * h) & (lane < HD * (h + 1))
                score_ref[...] = matmul(
                    jnp.where(mine, queries, jnp.zeros_like(queries)), keys, ((1,), (1,))
                )

                def rows_body(r, _):
                    at = pl.ds(pl.multiple_of(r * step, step), step)
                    scores = score_ref[at, :] * (HD**-0.5) + bias_ref[at, :]
                    summit = jnp.max(scores, axis=1, keepdims=True)
                    weights = jnp.exp(scores - summit)
                    total = jnp.sum(weights, axis=1, keepdims=True)
                    prob_ref[at, :] = (weights * (1.0 / total)).astype(jnp.bfloat16)
                    spot = lane == pair * 2 + h
                    totals_ref[at, :] = jnp.where(
                        spot, summit + jnp.log(total), totals_ref[at, :]
                    )
                    return 0

                lax.fori_loop(0, rows // step, rows_body, 0, unroll=True)
                parts.append(matmul(prob_ref[...], values))
            both = jnp.where(lane < HD, parts[0], parts[1])
            context_ref[:, pl.ds(first, 128)] = both.astype(jnp.bfloat16)
            return 0

        totals_ref[...] = jnp.zeros_like(totals_ref)
        lax.fori_loop(0, columns // 128, pair_body, 0)


def attend(normed_all, entry_full, offsets, tables, marks):
    rows, width = normed_all.shape
    columns = entry_full.shape[2]
    bf16, f32 = jnp.bfloat16, jnp.float32
    return kernel_call(
        attend_kernel,
        (3,),
        [whole((rows, width)), pl.BlockSpec((1, width, columns), lambda k: (k, 0, 0)),
         pl.BlockSpec((1, 1, columns), lambda k: (k, 0, 0))]
        + [whole((rows, 128))] * 3 + [whole((rows, 2)), whole((2, rows))],
        [whole((rows, 3 * columns)), whole((rows, columns)), whole((rows, 128))],
        [jax.ShapeDtypeStruct((rows, 3 * columns), bf16), jax.ShapeDtypeStruct((rows, columns), bf16),
         jax.ShapeDtypeStruct((rows, 128), f32)],
        [pltpu.VMEM((rows, rows), f32), pltpu.VMEM((rows, rows), f32), pltpu.VMEM((rows, rows), bf16)],
        "attention",
    )(normed_all, entry_full, offsets.reshape(3, 1, columns), *tables, *marks)


def attend_back_kernel(
    middle_ref, exit_ref, mixed_ref, totals_ref, keep_ref, low_ref, high_ref, column_ref, row_ref,
    grad_ref, bias_ref, score_ref, prob_grad_ref, prob_ref, score_grad_ref, context_grad_ref,
):
    rows = middle_ref.shape[0]
    columns = exit_ref.shape[2]
    step = row_steps(rows)
    context_grad_ref[...] = matmul(middle_ref[...], exit_ref[0]).astype(jnp.bfloat16)
    fill_bias(bias_ref, column_ref, row_ref)
    lane = lax.broadcasted_iota(jnp.int32, (1, 128), 1)

    def pair_body(pair, _):
        first = pl.multiple_of(pair * 128, 128)
        second = pl.multiple_of(columns + first, 128)
        third = pl.multiple_of(2 * columns + first, 128)
        queries = mixed_ref[:, pl.ds(first, 128)]
        keys = mixed_ref[:, pl.ds(second, 128)]
        values = mixed_ref[:, pl.ds(third, 128)]
        incoming = context_grad_ref[:, pl.ds(first, 128)]
        query_parts, key_parts, value_parts = [], [], []
        for h in range(2):
            mine = (lane >= HD * h) & (lane < HD * (h + 1))
            score_ref[...] = matmul(
                jnp.where(mine, queries, jnp.zeros_like(queries)), keys, ((1,), (1,))
            )
            prob_grad_ref[...] = matmul(
                jnp.where(mine, incoming, jnp.zeros_like(incoming)), values, ((1,), (1,))
            )

            def rows_body(r, _):
                at = pl.ds(pl.multiple_of(r * step, step), step)
                spot = lane == pair * 2 + h
                total = jnp.sum(jnp.where(spot, totals_ref[at, :], 0.0), axis=1, keepdims=True)
                probs = jnp.exp(score_ref[at, :] * (HD**-0.5) + bias_ref[at, :] - total)
                prob_grad = prob_grad_ref[at, :]
                inner = jnp.sum(probs * prob_grad, axis=1, keepdims=True)
                score_grad_ref[at, :] = (probs * (prob_grad - inner)).astype(jnp.bfloat16)
                prob_ref[at, :] = probs.astype(jnp.bfloat16)
                return 0

            lax.fori_loop(0, rows // step, rows_body, 0, unroll=True)
            query_parts.append(matmul(score_grad_ref[...], keys))
            key_parts.append(matmul(score_grad_ref[...], queries, ((0,), (0,))))
            value_parts.append(matmul(prob_ref[...], incoming, ((0,), (0,))))
        keep, low, high = keep_ref[...], low_ref[...], high_ref[...]
        scale = HD**-0.5
        query_grad = jnp.where(lane < HD, query_parts[0], query_parts[1]) * scale
        key_grad = jnp.where(lane < HD, key_parts[0], key_parts[1]) * scale
        value_grad = jnp.where(lane < HD, value_parts[0], value_parts[1])
        grad_ref[:, pl.ds(first, 128)] = turn(query_grad, keep, low, high, -1.0).astype(jnp.bfloat16)
        grad_ref[:, pl.ds(second, 128)] = turn(key_grad, keep, low, high, -1.0).astype(jnp.bfloat16)
        grad_ref[:, pl.ds(third, 128)] = value_grad.astype(jnp.bfloat16)
        return 0

    lax.fori_loop(0, columns // 128, pair_body, 0)


def attend_back(middle_all, exit_full, mixed, totals, tables, marks):
    rows, width = middle_all.shape
    columns = exit_full.shape[2]
    bf16, f32 = jnp.bfloat16, jnp.float32
    square = (rows, rows)
    return kernel_call(
        attend_back_kernel,
        (1,),
        [whole((rows, width)), pl.BlockSpec((1, width, columns), lambda *_: (3, 0, 0)),
         whole((rows, 3 * columns)), whole((rows, 128))]
        + [whole((rows, 128))] * 3 + [whole((rows, 2)), whole((2, rows))],
        whole((rows, 3 * columns)),
        jax.ShapeDtypeStruct((rows, 3 * columns), bf16),
        [pltpu.VMEM(square, f32), pltpu.VMEM(square, f32), pltpu.VMEM(square, f32),
         pltpu.VMEM(square, bf16), pltpu.VMEM(square, bf16), pltpu.VMEM((rows, columns), bf16)],
        "attention_back",
    )(middle_all, exit_full, mixed, totals, *tables, *marks)


def feed_kernel(
    second_ref, cot_ref, full_ref, acts_ref, branch_ref, second_grad_ref, weight_ref, hidden_grad_ref, sems
):
    j = pl.program_id(0)
    rows, width = second_ref.shape
    padded = acts_ref.shape[1] // 3
    pairs = padded // 128
    step = row_steps(rows)
    bf16 = jnp.bfloat16

    def load(at, size, which):
        here = pl.ds(at, size)
        return pltpu.make_async_copy(full_ref.at[:, here], weight_ref.at[:, here], sems.at[which])

    @pl.when(j == 0)
    def _():
        load(2 * padded, padded, 0).start()
        for p in range(pairs):
            load(p * 256, 256, p + 1).start()
        load(2 * padded, padded, 0).wait()
        for low in range(0, padded, 256):
            high = min(low + 256, padded)
            hidden_grad_ref[:, low:high] = matmul(
                cot_ref[...], weight_ref[:, 2 * padded + low : 2 * padded + high]
            )
        for p in range(pairs):
            load(p * 256, 256, p + 1).wait()
            gate_up = matmul(second_ref[...], weight_ref[:, p * 256 : (p + 1) * 256])
            gate, upper = gate_up[:, :128], gate_up[:, 128:]
            grad = hidden_grad_ref[:, p * 128 : (p + 1) * 128]
            sigmoid = jax.nn.sigmoid(gate)
            activated = gate * sigmoid
            acts_ref[:, p * 256 : p * 256 + 128] = (
                grad * upper * sigmoid * (1.0 + gate * (1.0 - sigmoid))
            ).astype(bf16)
            acts_ref[:, p * 256 + 128 : (p + 1) * 256] = (grad * activated).astype(bf16)
            hidden = 2 * padded + p * 128
            acts_ref[:, hidden : hidden + 128] = (activated * upper).astype(bf16)

    @pl.when(j > 0)
    def _():
        size = branch_ref.shape[1]
        here = pl.ds(pl.multiple_of((j - 1) * size, size), size)
        over = ((1,), (1,))
        second_grad_ref[...] = matmul(
            acts_ref[:, : 2 * padded], weight_ref[here, : 2 * padded], over
        ).astype(bf16)
        branch_ref[...] = matmul(
            acts_ref[:, 2 * padded :], weight_ref[here, 2 * padded :], over
        ).astype(bf16)


def feed(second_all, cot_all, full):
    rows, width = second_all.shape
    padded = full.shape[1] // 3
    chunk = 256
    bf16, f32 = jnp.bfloat16, jnp.float32
    out = pl.BlockSpec((rows, chunk), lambda j: (0, jnp.maximum(j - 1, 0)))
    return kernel_call(
        feed_kernel,
        (1 + width // chunk,),
        [whole((rows, width))] * 2 + [pl.BlockSpec(memory_space=pl.ANY)],
        [whole((rows, 3 * padded)), out, out],
        [jax.ShapeDtypeStruct((rows, 3 * padded), bf16)] + [jax.ShapeDtypeStruct((rows, width), bf16)] * 2,
        [pltpu.VMEM((width, 3 * padded), bf16), pltpu.VMEM((rows, padded), f32),
         pltpu.SemaphoreType.DMA((1 + padded // 128,))],
        "feed_forward",
    )(second_all, cot_all, full)


def turned_kernel(blocks_ref, rows_ref, out_ref):
    out_ref[...] = rows_ref[...].T


def turned_blocks(array, blocks, size):
    rows = array.shape[0]
    return pl.pallas_call(
        turned_kernel,
        grid_spec=pltpu.PrefetchScalarGridSpec(
            num_scalar_prefetch=1,
            grid=(len(blocks),),
            in_specs=[pl.BlockSpec((rows, size), lambda b, blocks_ref: (0, blocks_ref[b]))],
            out_specs=pl.BlockSpec((size, rows), lambda b, blocks_ref: (b, 0)),
        ),
        out_shape=jax.ShapeDtypeStruct((len(blocks) * size, rows), array.dtype),
        compiler_params=pltpu.CompilerParams(vmem_limit_bytes=32 * 1024 * 1024),
        cost_estimate=pl.CostEstimate(flops=1, bytes_accessed=1, transcendentals=0),
        name="turned_blocks",
    )(jnp.stack(blocks).astype(jnp.int32), array)


def terms_kernel(split, own_left, other_left, own_last, other_last, own_ref, other_ref, *outs):
    k = pl.program_id(0)

    def write(own, other):
        total = (matmul(own[...], own_ref[...]) + matmul(other[...], other_ref[...])).astype(jnp.bfloat16)
        size = outs[0].shape[0]
        for s, out in enumerate(outs):
            out[...] = total[s * size : (s + 1) * size]

    @pl.when(k < split)
    def _():
        write(own_left, other_left)

    @pl.when(k >= split)
    def _():
        write(own_last, other_last)


def weight_terms(left, left_last, right, tile, split, lines):
    count, rows = left[0].shape
    columns = right[0].shape[1]
    size = count // lines
    left_spec = whole((count, rows))
    right_spec = pl.BlockSpec((rows, tile), lambda k: (0, k))
    return list(
        kernel_call(
            lambda *refs: terms_kernel(split, *refs),
            (columns // tile,),
            [left_spec] * 4 + [right_spec] * 2,
            [pl.BlockSpec((size, tile), lambda k: (0, k))] * lines,
            [jax.ShapeDtypeStruct((size, columns), jnp.bfloat16)] * lines,
            [],
            "weight_terms",
            4 * count * rows * columns,
            2 * (4 * count * rows + 2 * rows * columns + count * columns),
        )(*left, *left_last, *right)
    )


def summed(refs, rows, columns):
    own, up, down = [ref[rows, columns].astype(jnp.float32) for ref in refs]
    return own + up + down


def plain_step_kernel(own, up, down, weight, first, second, *outs):
    everything = slice(None)
    gradient = summed((own, up, down), everything, everything)
    news = adamw(weight[0], first[0], second[0], gradient, matrix_rate, weight_decay)
    for out, value in zip(outs, (gradient,) + tuple(news)):
        out[0] = value


def plain_step(parts_of_sum, params):
    kinds, rows, columns = params[0].shape
    tile = rows // 2
    part = pl.BlockSpec((tile, columns), lambda k, r: (r, k))
    block = pl.BlockSpec((1, tile, columns), lambda k, r: (k, r, 0))
    return kernel_call(
        plain_step_kernel,
        (kinds, 2),
        [part] * 3 + [block] * 3,
        [block] * 4,
        [jax.ShapeDtypeStruct((kinds, rows, columns), jnp.float32)] * 4,
        [],
        "plain_step",
    )(*parts_of_sum, *params)


def feed_step_kernel(runs, *refs):
    count = 3 * len(runs)
    gate, down = refs[count : count + 3], refs[count + 3 : count + 6]
    gate_outs, down_outs = refs[count + 6 : count + 10], refs[count + 10 : count + 14]
    everything = slice(None)
    for at, (low, high) in enumerate(runs):
        sums = refs[3 * at : 3 * at + 3]
        padded = sums[0].shape[1] // 3
        for c in range(0, high - low, 128):
            size = min(128, high - low - c)
            here = slice(low + c, low + c + size)
            for k in range(2):
                gradient = summed(sums, everything, slice(2 * c + 128 * k, 2 * c + 128 * k + size))
                news = adamw(
                    *[ref[:, k, here] for ref in gate], gradient, matrix_rate, weight_decay
                )
                for out, value in zip(gate_outs, (gradient,) + tuple(news)):
                    out[:, k, here] = value
        here = slice(low, high)
        gradient = summed(sums, everything, slice(2 * padded, 2 * padded + high - low))
        news = adamw(*[ref[:, here] for ref in down], gradient, matrix_rate, weight_decay)
        for out, value in zip(down_outs, (gradient,) + tuple(news)):
            out[:, here] = value


def feed_step(runs, sums, gate, down):
    rows, columns = down[0].shape
    tile = 32
    gate_block = pl.BlockSpec((tile, 2, columns), lambda r: (r, 0, 0))
    down_block = pl.BlockSpec((tile, columns), lambda r: (r, 0))
    flat = [part for parts_of_sum in sums for part in parts_of_sum]
    return kernel_call(
        lambda *refs: feed_step_kernel(runs, *refs),
        (rows // tile,),
        [pl.BlockSpec((tile, part.shape[1]), lambda r: (r, 0)) for part in flat]
        + [gate_block] * 3
        + [down_block] * 3,
        [gate_block] * 4 + [down_block] * 4,
        [jax.ShapeDtypeStruct((rows, 2, columns), jnp.float32)] * 4
        + [jax.ShapeDtypeStruct((rows, columns), jnp.float32)] * 4,
        [],
        "feed_step",
    )(*flat, *gate, *down)


def on_device(
    tokens,
    cotangent,
    lengths,
    entry_weight,
    entry_first,
    entry_second,
    exit_weight,
    exit_first,
    exit_second,
    gate_weight,
    gate_first,
    gate_second,
    down_weight,
    down_first,
    down_second,
    bias_rows,
    bias_first,
    bias_second,
    norm_gains,
    gains_first,
    gains_second,
):
    parts = lax.axis_size("tensor")
    part_index = lax.axis_index("tensor")
    dp_index = lax.axis_index("dp")
    dp_count = lax.axis_size("dp")
    lines = dp_count // 2
    last = lines - 1
    place = dp_index // 2
    core = dp_index % 2
    local_rows = tokens.shape[0]
    group = local_rows * parts
    width = tokens.shape[1]
    size = width // dp_count
    head_cols = entry_weight.shape[2]
    hidden_cols = down_weight.shape[1]
    bf16 = jnp.bfloat16
    own_blocks = [((place - s + lines) % lines) * 2 + core for s in range(lines)]
    other_blocks = [((place - s + lines) % lines) * 2 + 1 - core for s in range(lines)]
    none = (None, None)

    def advance(streams):
        return [
            (blocks, scatter_step(blocks, *way, left, lines), left - 1) if left > 0 else stream
            for stream in streams
            for blocks, way, left in [stream]
        ]

    def begin(blocks):
        return advance([(blocks, none, last)])

    def finish(streams):
        while any(left > 0 for _, _, left in streams):
            streams = advance(streams)
        return streams

    def parts_of(stream):
        blocks, way, _ = stream
        return (blocks[0],) + tuple(way)

    def both_cores(array):
        both = turned_blocks(array, own_blocks + other_blocks, size)
        return both[: width // 2], other_core(both[width // 2 :])

    kinds_own = jnp.concatenate(
        [jnp.swapaxes(entry_weight, 0, 1).astype(bf16), exit_weight.astype(bf16)[None]], axis=0
    )
    kinds = lax.all_gather(kinds_own, "dp", axis=1, tiled=True)
    chunks = cuts(hidden_cols, MLP_CHUNKS)

    def unit_of(a, b):
        gates = paired(gate_weight[:, :, a:b].astype(bf16)).reshape(size, -1)
        downs = jnp.pad(down_weight[:, a:b].astype(bf16), ((0, 0), (0, -(b - a) % 128)))
        return jnp.concatenate([gates, downs], axis=1)

    fulls = []
    earlier = kinds_own
    for a, b in chunks:
        earlier = after(unit_of(a, b), earlier)
        fulls.append(lax.all_gather(earlier, "dp", axis=0, tiled=True))

    segment, positions = segments(lengths[0], group)
    row_blocks = jnp.arange(parts, dtype=jnp.int32) ^ part_index
    row_index = (
        row_blocks[:, None] * local_rows + jnp.arange(local_rows, dtype=jnp.int32)[None, :]
    ).reshape(group)
    segment, positions = [
        jnp.concatenate(
            [
                lax.dynamic_slice_in_dim(array, (part_index ^ r) * local_rows, local_rows, 0)
                for r in range(parts)
            ]
        )
        for array in (segment, positions)
    ]
    cosine, sine = rotary_tables(positions.astype(jnp.float32))
    ones = jnp.ones((group, HD - ROT), jnp.float32)
    blank = jnp.zeros((group, ROT // 2), jnp.float32)
    empty = jnp.zeros((group, HD - ROT), jnp.float32)
    tables = [
        jnp.concatenate([a, b, c] * 2, axis=1)
        for a, b, c in ((cosine, cosine, ones), (-sine, blank, empty), (blank, sine, empty))
    ]
    marks = (jnp.stack([segment, row_index], axis=1), jnp.stack([segment, row_index], axis=0))
    column_start = part_index * head_cols
    rotmask = (jnp.arange(head_cols, dtype=jnp.int32) % HD < ROT).astype(jnp.float32)
    query_bias = lax.dynamic_slice_in_dim(bias_rows[0], column_start, head_cols, 0)
    key_bias = lax.dynamic_slice_in_dim(bias_rows[1], column_start, head_cols, 0) * rotmask
    value_bias = lax.dynamic_slice_in_dim(bias_rows[2], column_start, head_cols, 0)
    offsets = jnp.stack([query_bias, key_bias, value_bias])

    rows_in = tokens.astype(jnp.float32)
    normed, unit_one, factor_one = norm_forward(rows_in, norm_gains[0], bias_rows[3])
    normed_all = gather_rows(normed.astype(bf16), parts)
    cot_all = gather_rows(after(cotangent, normed_all), parts)
    normed_sides = both_cores(after(normed_all, cot_all))
    cot_sides = both_cores(after(cot_all, normed_sides[0]))
    kinds, normed_all, normed_sides, cot_all, cot_sides, tables, marks = together(
        kinds, normed_all, normed_sides, cot_all, cot_sides, tables, marks
    )

    mixed, context, log_totals = attend(normed_all, kinds, offsets, tables, marks)
    branch = dot(context, kinds[3], ((1,), (1,))).astype(bf16)
    context_other = other_core(context)
    branch, context_other = together(branch, context_other)
    branch = scatter_rows(branch, parts)
    middle = rows_in + branch
    second, unit_two, factor_two = norm_forward(middle, norm_gains[1], bias_rows[4])
    second_all = gather_rows(second.astype(bf16), parts)
    second_all, fulls[0] = together(second_all, fulls[0])

    second_sides = both_cores(second_all)
    streams, branch_terms, second_terms = [], [], []
    for at, full in enumerate(fulls):
        streams = advance(streams)
        acts, branch_term, second_term = feed(second_all, cot_all, fulls[at])
        branch_terms.append(branch_term)
        second_terms.append(second_term)
        if at + 1 < len(fulls):
            padded = acts.shape[1] // 3
            terms = weight_terms(
                second_sides, cot_sides, (acts, other_core(acts)), padded, 2, lines
            )
            streams = streams + begin(terms)
            streams, fulls[at + 1] = together_streams(streams, fulls[at + 1])
    second_grad = add_terms(second_terms)
    second_grad, acts = together(second_grad, acts)
    acts_other = other_core(acts)
    second_grad = scatter_rows(second_grad, parts)
    branch_two = add_terms(branch_terms)
    padded = acts.shape[1] // 3
    terms = weight_terms(second_sides, cot_sides, (acts, acts_other), padded, 2, lines)
    streams, (second_grad, terms, branch_two) = together_streams(
        streams, (second_grad, terms, branch_two)
    )

    streams = advance(streams) + begin(terms)
    middle_grad = cotangent.astype(jnp.float32) + norm_backward(
        second_grad, unit_two, factor_two, norm_gains[1]
    )
    middle_all = gather_rows(middle_grad.astype(bf16), parts)
    streams, middle_all = together_streams(streams, middle_all)

    streams = advance(streams)
    mixed_grad = attend_back(middle_all, kinds, mixed, log_totals, tables, marks)
    middle_sides = both_cores(middle_all)
    exit_terms = weight_terms(
        middle_sides, middle_sides, (context, context_other), head_cols, 1, lines
    )
    streams, (mixed_grad, exit_terms) = together_streams(streams, (mixed_grad, exit_terms))

    streams = advance(streams) + begin(exit_terms)
    entry_terms = weight_terms(
        normed_sides, normed_sides, (mixed_grad, other_core(mixed_grad)), head_cols, 3, lines
    )
    mixed_grad, entry_terms = together(mixed_grad, entry_terms)
    streams = streams + begin(entry_terms)
    normed_grad = sum(
        dot(mixed_grad[:, k * head_cols : (k + 1) * head_cols], kinds[k], ((1,), (1,)))
        for k in range(3)
    )
    normed_grad = scatter_rows(normed_grad.astype(bf16), parts)
    streams, normed_grad = together_streams(streams, normed_grad)

    streams = finish(streams[:-2]) + advance(streams[-2:])
    input_gradient = middle_grad + norm_backward(normed_grad, unit_one, factor_one, norm_gains[0])
    gain_two_grad = jnp.sum(second_grad * unit_two, axis=0)
    shift_two_grad = jnp.sum(second_grad, axis=0)
    gain_one_grad = jnp.sum(normed_grad * unit_one, axis=0)
    shift_one_grad = jnp.sum(normed_grad, axis=0)
    column_sums = jnp.sum(mixed_grad.astype(jnp.float32), axis=0).reshape(3, head_cols)
    column_sums = column_sums * jnp.stack([jnp.ones_like(rotmask), rotmask, jnp.ones_like(rotmask)])
    placed = lax.dynamic_update_slice_in_dim(
        jnp.zeros((3, width), jnp.float32), column_sums, column_start, 1
    )
    norms_local = jnp.stack([shift_one_grad, shift_two_grad, gain_one_grad, gain_two_grad])
    vectors = jnp.concatenate([placed, norms_local], axis=0)
    bit = 1
    while bit < parts:
        vectors = hop(vectors, "tensor", bit)
        bit *= 2
    vectors = hop(vectors, "dp", 1)

    (
        gate_gradient, gate_updated, gate_first_new, gate_second_new,
        down_gradient, down_updated, down_first_new, down_second_new,
    ) = feed_step(
        chunks,
        [parts_of(stream) for stream in streams[:-2]],
        (gate_weight, gate_first, gate_second),
        (down_weight, down_first, down_second),
    )
    streams, (vectors, gate_updated, down_updated) = together_streams(
        streams, (vectors, gate_updated, down_updated)
    )

    bit = 2
    while bit < dp_count:
        vectors = hop(vectors, "dp", bit)
        bit *= 2
    streams = finish(streams)
    branch_two = scatter_rows(after(branch_two, vectors), parts)
    output_rows = (middle + branch_two).astype(bf16)
    bias_gradient = vectors[:5]
    gains_gradient = vectors[5:]
    exit_gradient, exit_updated, exit_first_new, exit_second_new = [
        array[0]
        for array in plain_step(
            parts_of(streams[-2]), [array[None] for array in (exit_weight, exit_first, exit_second)]
        )
    ]
    entry_gradient, entry_updated, entry_first_new, entry_second_new = [
        jnp.swapaxes(array, 0, 1)
        for array in plain_step(
            parts_of(streams[-1]),
            [jnp.swapaxes(array, 0, 1) for array in (entry_weight, entry_first, entry_second)],
        )
    ]
    bias_updated, bias_first_new, bias_second_new = adamw(
        bias_rows, bias_first, bias_second, bias_gradient, vector_rate, 0.0
    )
    gains_updated, gains_first_new, gains_second_new = adamw(
        norm_gains, gains_first, gains_second, gains_gradient, vector_rate, 0.0
    )
    return (
        output_rows,
        input_gradient,
        entry_gradient,
        entry_updated,
        entry_first_new,
        entry_second_new,
        exit_gradient,
        exit_updated,
        exit_first_new,
        exit_second_new,
        gate_gradient,
        gate_updated,
        gate_first_new,
        gate_second_new,
        down_gradient,
        down_updated,
        down_first_new,
        down_second_new,
        bias_gradient,
        bias_updated,
        bias_first_new,
        bias_second_new,
        gains_gradient,
        gains_updated,
        gains_first_new,
        gains_second_new,
    )


def solution(mesh):
    return jax.shard_map(
        on_device,
        mesh=mesh,
        in_specs=(
            P(("dp", "tensor"), None),
            P(("dp", "tensor"), None),
            P("dp", None),
            P("dp", None, "tensor"),
            P("dp", None, "tensor"),
            P("dp", None, "tensor"),
            P("dp", "tensor"),
            P("dp", "tensor"),
            P("dp", "tensor"),
            P("dp", None, "tensor"),
            P("dp", None, "tensor"),
            P("dp", None, "tensor"),
            P("dp", "tensor"),
            P("dp", "tensor"),
            P("dp", "tensor"),
            P(),
            P(),
            P(),
            P(),
            P(),
            P(),
        ),
        out_specs=(
            P(("dp", "tensor"), None),
            P(("dp", "tensor"), None),
            P("dp", None, "tensor"),
            P("dp", None, "tensor"),
            P("dp", None, "tensor"),
            P("dp", None, "tensor"),
            P("dp", "tensor"),
            P("dp", "tensor"),
            P("dp", "tensor"),
            P("dp", "tensor"),
            P("dp", None, "tensor"),
            P("dp", None, "tensor"),
            P("dp", None, "tensor"),
            P("dp", None, "tensor"),
            P("dp", "tensor"),
            P("dp", "tensor"),
            P("dp", "tensor"),
            P("dp", "tensor"),
            P(),
            P(),
            P(),
            P(),
            P(),
            P(),
            P(),
            P(),
        ),
        check_vma=False,
    )
```

```python
import jax
import jax.numpy as jnp
from jax import lax
from jax.experimental import pallas as pl
from jax.experimental.pallas import tpu as pltpu
from jax.sharding import PartitionSpec as P

HD = 64
ROT = 16
STEP = 3
MLP_CHUNKS = 2


norm_eps = 1e-05
rope_base = 10000.0
masked_score = -1e30
beta_one = 0.9
beta_two = 0.95
adam_eps = 1e-08
matrix_rate = 0.08
vector_rate = 0.4
weight_decay = 0.1


def norm_forward(rows, gain, shift):
    centre = jnp.mean(rows, axis=-1, keepdims=True)
    centred = rows - centre
    spread = jnp.mean(centred * centred, axis=-1, keepdims=True)
    factor = lax.rsqrt(spread + norm_eps)
    unit = centred * factor
    return (unit * gain + shift, unit, factor)


def norm_backward(incoming, unit, factor, gain):
    scaled = incoming * gain
    mean_plain = jnp.mean(scaled, axis=-1, keepdims=True)
    mean_along = jnp.mean(scaled * unit, axis=-1, keepdims=True)
    return factor * (scaled - mean_plain - unit * mean_along)


def segments(lengths_row, count):
    ends = jnp.cumsum(lengths_row)
    index = jnp.arange(count, dtype=jnp.int32)
    after = index[:, None] >= ends[None, :]
    segment = jnp.sum(after.astype(jnp.int32), axis=1)
    begin = jnp.max(jnp.where(after, ends[None, :], jnp.zeros_like(ends)[None, :]), axis=1)
    return (segment, index - begin)


def rotary_tables(positions):
    half = ROT // 2
    freqs = rope_base ** (-2.0 * jnp.arange(half, dtype=jnp.float32) / ROT)
    angles = positions[:, None] * freqs[None, :]
    return (jnp.cos(angles), jnp.sin(angles))


def adamw(weight, first, second, gradient, rate, decay):
    first_new = beta_one * first + (1.0 - beta_one) * gradient
    second_new = beta_two * second + (1.0 - beta_two) * gradient * gradient
    first_hat = first_new / (1.0 - beta_one**STEP)
    second_hat = second_new / (1.0 - beta_two**STEP)
    updated = weight - rate * (first_hat / (jnp.sqrt(second_hat) + adam_eps) + decay * weight)
    return (updated, first_new, second_new)


def together(*groups):
    flat, tree = jax.tree.flatten(groups)
    return jax.tree.unflatten(tree, lax.optimization_barrier(flat))


def after(value, *earlier):
    return lax.optimization_barrier((value,) + tuple(earlier))[0]


def pairs_up(lines, low, high, step):
    return [(z * 2 + c, (z + step) * 2 + c) for z in range(low, high) for c in range(2)]


def other_core(array):
    count = lax.axis_size("dp")
    return lax.ppermute(array, "dp", [(d, d ^ 1) for d in range(count)])


def gather_step(ups, downs, s, lines):
    up = lax.ppermute(ups[-1], "dp", pairs_up(lines, s - 1, lines - 1, 1))
    down = lax.ppermute(downs[-1], "dp", pairs_up(lines, 1, lines - s + 1, -1))
    return ups + [up], downs + [down]


def gather_from(way, low, high, lines):
    for s in range(low, high):
        way = gather_step(*way, s, lines)
    return way


def pack_kernel(lines, place_ref, *refs):
    pieces, out = refs[:-1], refs[-1]
    place = place_ref[0]
    s = pl.program_id(0)
    for at in range(lines):

        @pl.when((s == at) & (place >= at))
        def _():
            out[...] = pieces[at][...]

        if at > 0:

            @pl.when((s == at) & (place < at))
            def _():
                out[...] = pieces[2 * lines - 1 - at][...]


def pack(ups, downs, place, lines):
    rows, columns = ups[0].shape
    tile = min(128, rows)
    tiles = rows // tile

    def spec(at, is_up):
        def index(s, t, place_ref):
            wanted = (s == at) & ((place_ref[0] >= at) if is_up else (place_ref[0] < at))
            return (jnp.where(wanted, t, jnp.where(s > at, tiles - 1, 0)), 0)

        return pl.BlockSpec((tile, columns), index)

    return pl.pallas_call(
        lambda *refs: pack_kernel(lines, *refs),
        grid_spec=pltpu.PrefetchScalarGridSpec(
            num_scalar_prefetch=1,
            grid=(lines, tiles),
            in_specs=[spec(at, True) for at in range(lines)]
            + [spec(lines - at, False) for at in range(1, lines)],
            out_specs=pl.BlockSpec((tile, columns), lambda s, t, place_ref: (s * tiles + t, 0)),
        ),
        out_shape=jax.ShapeDtypeStruct((lines * rows, columns), ups[0].dtype),
        compiler_params=pltpu.CompilerParams(vmem_limit_bytes=40 * 1024 * 1024),
        cost_estimate=pl.CostEstimate(
            flops=0, bytes_accessed=4 * lines * rows * columns, transcendentals=0
        ),
        name="pack_blocks",
    )(place.reshape(1).astype(jnp.int32), *ups, *downs[1:])


def scatter_step(blocks, up, down, j, lines):
    up_send = blocks[lines - j] if up is None else blocks[lines - j] + up
    down_send = blocks[j] if down is None else blocks[j] + down
    up = lax.ppermute(up_send, "dp", pairs_up(lines, 0, lines - j, 1))
    down = lax.ppermute(down_send, "dp", pairs_up(lines, j, lines, -1))
    return up, down


def swap_rows(array, offset):
    count = lax.axis_size("tensor")
    return lax.ppermute(array, "tensor", [(t, t ^ offset) for t in range(count)])


def gather_rows(own, parts):
    return jnp.concatenate([own] + [swap_rows(own, r) for r in range(1, parts)], axis=0)


def send_rows(partial, parts):
    rows = partial.shape[0] // parts
    blocks = [partial[r * rows : (r + 1) * rows] for r in range(parts)]
    return [blocks[0]] + [swap_rows(blocks[r], r) for r in range(1, parts)]


def add_up(terms):
    total = terms[0].astype(jnp.float32)
    for term in terms[1:]:
        total = total + term.astype(jnp.float32)
    return total


def scatter_rows(partial, parts):
    return add_up(send_rows(partial, parts))


def together_streams(streams, others):
    ways, blocks, others = together(
        [way for _, way, _ in streams], [blocks for blocks, _, _ in streams], others
    )
    return [(b, w, left) for b, w, (_, _, left) in zip(blocks, ways, streams)], others


def add_terms(terms):
    return add_up(terms).astype(jnp.bfloat16)


def hop(array, axis, bit):
    count = lax.axis_size(axis)
    return array + lax.ppermute(array, axis, [(i, i ^ bit) for i in range(count)])


def cuts(columns, count):
    tiles = -(-columns // 128)
    bounds = [min(columns, 128 * (tiles * i // count)) for i in range(count + 1)]
    return [(a, b) for a, b in zip(bounds[:-1], bounds[1:]) if b > a]


def paired(array):
    rows, kinds, columns = array.shape
    array = jnp.pad(array, ((0, 0), (0, 0), (0, -columns % 128)))
    return jnp.swapaxes(array.reshape(rows, kinds, -1, 128), 1, 2)


def dot(a, b, contract):
    return lax.dot_general(a, b, (contract, ((), ())), preferred_element_type=jnp.float32)


def whole(shape):
    return pl.BlockSpec(shape, lambda *_: (0,) * len(shape))


def kernel_call(kernel, grid, in_specs, out_specs, out_shape, scratch, name, flops=1, moved=1):
    return pl.pallas_call(
        kernel,
        grid=grid,
        in_specs=in_specs,
        out_specs=out_specs,
        out_shape=out_shape,
        scratch_shapes=scratch,
        compiler_params=pltpu.CompilerParams(vmem_limit_bytes=56 * 1024 * 1024),
        cost_estimate=pl.CostEstimate(flops=flops, bytes_accessed=moved, transcendentals=0),
        name=name,
    )


def turn(x, keep, low, high, direction):
    return (
        x * keep
        + pltpu.roll(x, 120, 1) * (low * direction)
        + pltpu.roll(x, 8, 1) * (high * direction)
    )


def row_steps(rows):
    return 128 if rows % 128 == 0 else rows


def fill_bias(bias_ref, column_ref, row_ref):
    rows = bias_ref.shape[0]
    step = row_steps(rows)

    def body(r, _):
        at = pl.ds(pl.multiple_of(r * step, step), step)
        marks = column_ref[at, :]
        visible = (marks[:, 0:1] == row_ref[0:1, :]) & (marks[:, 1:2] >= row_ref[1:2, :])
        bias_ref[at, :] = jnp.where(visible, 0.0, masked_score)
        return 0

    lax.fori_loop(0, rows // step, body, 0)


def matmul(a, b, contract=((1,), (0,))):
    return lax.dot_general(a, b, (contract, ((), ())), preferred_element_type=jnp.float32)


def attend_kernel(
    normed_ref, weight_ref, offset_ref, keep_ref, low_ref, high_ref, column_ref, row_ref,
    mixed_ref, context_ref, totals_ref, bias_ref, score_ref, prob_ref,
):
    kind = pl.program_id(0)
    rows, columns = context_ref.shape
    step = row_steps(rows)
    raw = matmul(normed_ref[...], weight_ref[0]) + offset_ref[0]
    here = pl.multiple_of(kind * columns, 128)

    @pl.when(kind < 2)
    def _():
        for b in range(columns // 128):
            block = turn(raw[:, b * 128 : (b + 1) * 128], keep_ref[...], low_ref[...], high_ref[...], 1.0)
            mixed_ref[:, pl.ds(pl.multiple_of(here + b * 128, 128), 128)] = block.astype(jnp.bfloat16)

    @pl.when(kind == 2)
    def _():
        mixed_ref[:, pl.ds(here, columns)] = raw.astype(jnp.bfloat16)
        fill_bias(bias_ref, column_ref, row_ref)
        lane = lax.broadcasted_iota(jnp.int32, (1, 128), 1)

        def pair_body(pair, _):
            first = pl.multiple_of(pair * 128, 128)
            queries = mixed_ref[:, pl.ds(first, 128)]
            keys = mixed_ref[:, pl.ds(pl.multiple_of(columns + first, 128), 128)]
            values = mixed_ref[:, pl.ds(pl.multiple_of(2 * columns + first, 128), 128)]
            parts = []
            for h in range(2):
                mine = (lane >= HD * h) & (lane < HD * (h + 1))
                score_ref[...] = matmul(
                    jnp.where(mine, queries, jnp.zeros_like(queries)), keys, ((1,), (1,))
                )

                def rows_body(r, _):
                    at = pl.ds(pl.multiple_of(r * step, step), step)
                    scores = score_ref[at, :] * (HD**-0.5) + bias_ref[at, :]
                    summit = jnp.max(scores, axis=1, keepdims=True)
                    weights = jnp.exp(scores - summit)
                    total = jnp.sum(weights, axis=1, keepdims=True)
                    prob_ref[at, :] = (weights * (1.0 / total)).astype(jnp.bfloat16)
                    spot = lane == pair * 2 + h
                    totals_ref[at, :] = jnp.where(
                        spot, summit + jnp.log(total), totals_ref[at, :]
                    )
                    return 0

                lax.fori_loop(0, rows // step, rows_body, 0, unroll=True)
                parts.append(matmul(prob_ref[...], values))
            both = jnp.where(lane < HD, parts[0], parts[1])
            context_ref[:, pl.ds(first, 128)] = both.astype(jnp.bfloat16)
            return 0

        totals_ref[...] = jnp.zeros_like(totals_ref)
        lax.fori_loop(0, columns // 128, pair_body, 0)


def attend(normed_all, entry_full, offsets, tables, marks):
    rows, width = normed_all.shape
    columns = entry_full.shape[2]
    bf16, f32 = jnp.bfloat16, jnp.float32
    return kernel_call(
        attend_kernel,
        (3,),
        [whole((rows, width)), pl.BlockSpec((1, width, columns), lambda k: (k, 0, 0)),
         pl.BlockSpec((1, 1, columns), lambda k: (k, 0, 0))]
        + [whole((rows, 128))] * 3 + [whole((rows, 2)), whole((2, rows))],
        [whole((rows, 3 * columns)), whole((rows, columns)), whole((rows, 128))],
        [jax.ShapeDtypeStruct((rows, 3 * columns), bf16), jax.ShapeDtypeStruct((rows, columns), bf16),
         jax.ShapeDtypeStruct((rows, 128), f32)],
        [pltpu.VMEM((rows, rows), f32), pltpu.VMEM((rows, rows), f32), pltpu.VMEM((rows, rows), bf16)],
        "attention",
        24 * rows * width * columns,
        8 * rows * width,
    )(normed_all, entry_full, offsets.reshape(3, 1, columns), *tables, *marks)


def attend_back_kernel(
    middle_ref, exit_ref, mixed_ref, context_ref, totals_ref, keep_ref, low_ref, high_ref, column_ref,
    row_ref, kinds_ref, grad_ref, normed_ref, bias_ref, score_ref, prob_grad_ref, prob_ref,
    score_grad_ref, context_grad_ref, weight_ref, sem,
):
    rows = middle_ref.shape[0]
    columns = exit_ref.shape[2]
    step = row_steps(rows)
    load = pltpu.make_async_copy(kinds_ref.at[pl.ds(0, 3)], weight_ref, sem)
    load.start()
    grad_ref[:, 3 * columns :] = context_ref[...]
    context_grad_ref[...] = matmul(middle_ref[...], exit_ref[0]).astype(jnp.bfloat16)
    fill_bias(bias_ref, column_ref, row_ref)
    lane = lax.broadcasted_iota(jnp.int32, (1, 128), 1)

    def pair_body(pair, _):
        first = pl.multiple_of(pair * 128, 128)
        second = pl.multiple_of(columns + first, 128)
        third = pl.multiple_of(2 * columns + first, 128)
        queries = mixed_ref[:, pl.ds(first, 128)]
        keys = mixed_ref[:, pl.ds(second, 128)]
        values = mixed_ref[:, pl.ds(third, 128)]
        incoming = context_grad_ref[:, pl.ds(first, 128)]
        query_parts, key_parts, value_parts = [], [], []
        for h in range(2):
            mine = (lane >= HD * h) & (lane < HD * (h + 1))
            score_ref[...] = matmul(
                jnp.where(mine, queries, jnp.zeros_like(queries)), keys, ((1,), (1,))
            )
            prob_grad_ref[...] = matmul(
                jnp.where(mine, incoming, jnp.zeros_like(incoming)), values, ((1,), (1,))
            )

            def rows_body(r, _):
                at = pl.ds(pl.multiple_of(r * step, step), step)
                spot = lane == pair * 2 + h
                total = jnp.sum(jnp.where(spot, totals_ref[at, :], 0.0), axis=1, keepdims=True)
                probs = jnp.exp(score_ref[at, :] * (HD**-0.5) + bias_ref[at, :] - total)
                prob_grad = prob_grad_ref[at, :]
                inner = jnp.sum(probs * prob_grad, axis=1, keepdims=True)
                score_grad_ref[at, :] = (probs * (prob_grad - inner)).astype(jnp.bfloat16)
                prob_ref[at, :] = probs.astype(jnp.bfloat16)
                return 0

            lax.fori_loop(0, rows // step, rows_body, 0, unroll=True)
            query_parts.append(matmul(score_grad_ref[...], keys))
            key_parts.append(matmul(score_grad_ref[...], queries, ((0,), (0,))))
            value_parts.append(matmul(prob_ref[...], incoming, ((0,), (0,))))
        keep, low, high = keep_ref[...], low_ref[...], high_ref[...]
        scale = HD**-0.5
        query_grad = jnp.where(lane < HD, query_parts[0], query_parts[1]) * scale
        key_grad = jnp.where(lane < HD, key_parts[0], key_parts[1]) * scale
        value_grad = jnp.where(lane < HD, value_parts[0], value_parts[1])
        grad_ref[:, pl.ds(first, 128)] = turn(query_grad, keep, low, high, -1.0).astype(jnp.bfloat16)
        grad_ref[:, pl.ds(second, 128)] = turn(key_grad, keep, low, high, -1.0).astype(jnp.bfloat16)
        grad_ref[:, pl.ds(third, 128)] = value_grad.astype(jnp.bfloat16)
        return 0

    lax.fori_loop(0, columns // 128, pair_body, 0)
    load.wait()
    width = normed_ref.shape[1]
    for low in range(0, width, 512):
        here = slice(low, min(low + 512, width))
        total = None
        for k in range(3):
            term = matmul(
                grad_ref[:, k * columns : (k + 1) * columns], weight_ref[k, here, :], ((1,), (1,))
            )
            total = term if total is None else total + term
        normed_ref[:, here] = total.astype(jnp.bfloat16)


def attend_back(middle_all, exit_full, mixed, context, totals, tables, marks):
    rows, width = middle_all.shape
    columns = exit_full.shape[2]
    bf16, f32 = jnp.bfloat16, jnp.float32
    square = (rows, rows)
    return kernel_call(
        attend_back_kernel,
        (1,),
        [whole((rows, width)), pl.BlockSpec((1, width, columns), lambda *_: (3, 0, 0)),
         whole((rows, 3 * columns)), whole((rows, columns)), whole((rows, 128))]
        + [whole((rows, 128))] * 3 + [whole((rows, 2)), whole((2, rows))]
        + [pl.BlockSpec(memory_space=pl.ANY)],
        [whole((rows, 4 * columns)), whole((rows, width))],
        [jax.ShapeDtypeStruct((rows, 4 * columns), bf16), jax.ShapeDtypeStruct((rows, width), bf16)],
        [pltpu.VMEM(square, f32), pltpu.VMEM(square, f32), pltpu.VMEM(square, f32),
         pltpu.VMEM(square, bf16), pltpu.VMEM(square, bf16), pltpu.VMEM((rows, columns), bf16),
         pltpu.VMEM((3, width, columns), bf16), pltpu.SemaphoreType.DMA],
        "attention_back",
        24 * rows * width * columns,
        8 * rows * width,
    )(middle_all, exit_full, mixed, context, totals, *tables, *marks, exit_full)


def feed_kernel(pieces, order_ref, second_in, cot_in, *refs):
    fulls, refs = refs[:pieces], refs[pieces:]
    acts_ref, branch_ref, second_grad_ref, weight_ref, hidden_grad_ref, sems = refs[:6]
    j = pl.program_id(0)
    rows, width = second_in.shape
    padded = acts_ref.shape[1] // 3
    pairs = padded // 128
    size = branch_ref.shape[1]
    height = width // pieces
    bf16 = jnp.bfloat16
    second_ref, cot_ref = (second_in, cot_in) if pieces == 1 else refs[6:]

    def loads(at, columns, which):
        here = pl.ds(at, columns)
        return [
            pltpu.make_async_copy(
                full.at[:, here], weight_ref.at[pl.ds(p * height, height), here], sems.at[p, which]
            )
            for p, full in enumerate(fulls)
        ]

    @pl.when(j == 0)
    def _():
        for load in loads(2 * padded, padded, 0):
            load.start()
        for p in range(pairs):
            for load in loads(p * 256, 256, p + 1):
                load.start()
        if pieces > 1:
            for b in range(width // size):
                there = pl.ds(pl.multiple_of(order_ref[b] * size, size), size)
                second_ref[:, b * size : (b + 1) * size] = second_in[:, there]
                cot_ref[:, b * size : (b + 1) * size] = cot_in[:, there]
        for load in loads(2 * padded, padded, 0):
            load.wait()
        for low in range(0, padded, 256):
            high = min(low + 256, padded)
            hidden_grad_ref[:, low:high] = matmul(
                cot_ref[...], weight_ref[:, 2 * padded + low : 2 * padded + high]
            )
        for p in range(pairs):
            for load in loads(p * 256, 256, p + 1):
                load.wait()
            gate_up = matmul(second_ref[...], weight_ref[:, p * 256 : (p + 1) * 256])
            gate, upper = gate_up[:, :128], gate_up[:, 128:]
            grad = hidden_grad_ref[:, p * 128 : (p + 1) * 128]
            sigmoid = jax.nn.sigmoid(gate)
            activated = gate * sigmoid
            acts_ref[:, p * 256 : p * 256 + 128] = (
                grad * upper * sigmoid * (1.0 + gate * (1.0 - sigmoid))
            ).astype(bf16)
            acts_ref[:, p * 256 + 128 : (p + 1) * 256] = (grad * activated).astype(bf16)
            hidden = 2 * padded + p * 128
            acts_ref[:, hidden : hidden + 128] = (activated * upper).astype(bf16)

    @pl.when(j > 0)
    def _():
        here = pl.ds(pl.multiple_of((j - 1) * size, size), size)
        over = ((1,), (1,))
        second_grad_ref[...] = matmul(
            acts_ref[:, : 2 * padded], weight_ref[here, : 2 * padded], over
        ).astype(bf16)
        branch_ref[...] = matmul(
            acts_ref[:, 2 * padded :], weight_ref[here, 2 * padded :], over
        ).astype(bf16)


def feed(second_all, cot_all, fulls, order, size):
    rows, width = second_all.shape
    padded = fulls[0].shape[1] // 3
    pieces = len(fulls)
    bf16, f32 = jnp.bfloat16, jnp.float32
    full = pl.BlockSpec((rows, width), lambda j, order_ref: (0, 0))
    out = pl.BlockSpec((rows, size), lambda j, order_ref: (0, order_ref[jnp.maximum(j - 1, 0)]))
    scratch = [
        pltpu.VMEM((width, 3 * padded), bf16), pltpu.VMEM((rows, padded), f32),
        pltpu.SemaphoreType.DMA((pieces, 1 + padded // 128)),
    ]
    if pieces > 1:
        scratch += [pltpu.VMEM((rows, width), bf16)] * 2
    return pl.pallas_call(
        lambda *refs: feed_kernel(pieces, *refs),
        grid_spec=pltpu.PrefetchScalarGridSpec(
            num_scalar_prefetch=1,
            grid=(1 + width // size,),
            in_specs=[full] * 2 + [pl.BlockSpec(memory_space=pl.ANY)] * pieces,
            out_specs=[pl.BlockSpec((rows, 3 * padded), lambda j, order_ref: (0, 0)), out, out],
            scratch_shapes=scratch,
        ),
        out_shape=[jax.ShapeDtypeStruct((rows, 3 * padded), bf16)]
        + [jax.ShapeDtypeStruct((rows, width), bf16)] * 2,
        compiler_params=pltpu.CompilerParams(vmem_limit_bytes=56 * 1024 * 1024),
        cost_estimate=pl.CostEstimate(
            flops=24 * rows * width * padded,
            bytes_accessed=12 * width * padded + 16 * rows * width,
            transcendentals=0,
        ),
        name="feed_forward",
    )(order, second_all, cot_all, *fulls)


def turned_kernel(blocks_ref, rows_ref, out_ref):
    out_ref[...] = rows_ref[...].T


def turned_blocks(array, blocks, size):
    rows = array.shape[0]
    return pl.pallas_call(
        turned_kernel,
        grid_spec=pltpu.PrefetchScalarGridSpec(
            num_scalar_prefetch=1,
            grid=(len(blocks),),
            in_specs=[pl.BlockSpec((rows, size), lambda b, blocks_ref: (0, blocks_ref[b]))],
            out_specs=pl.BlockSpec((size, rows), lambda b, blocks_ref: (b, 0)),
        ),
        out_shape=jax.ShapeDtypeStruct((len(blocks) * size, rows), array.dtype),
        compiler_params=pltpu.CompilerParams(vmem_limit_bytes=32 * 1024 * 1024),
        cost_estimate=pl.CostEstimate(flops=1, bytes_accessed=1, transcendentals=0),
        name="turned_blocks",
    )(jnp.stack(blocks).astype(jnp.int32), array)


def terms_kernel(split, own_left, other_left, own_last, other_last, own_ref, other_ref, *outs):
    k = pl.program_id(0)

    def write(own, other):
        total = (matmul(own[...], own_ref[...]) + matmul(other[...], other_ref[...])).astype(jnp.bfloat16)
        size = outs[0].shape[0]
        for s, out in enumerate(outs):
            out[...] = total[s * size : (s + 1) * size]

    @pl.when(k < split)
    def _():
        write(own_left, other_left)

    @pl.when(k >= split)
    def _():
        write(own_last, other_last)


def weight_terms(left, left_last, right, tile, split, lines):
    count, rows = left[0].shape
    columns = right[0].shape[1]
    size = count // lines
    left_spec = whole((count, rows))
    right_spec = pl.BlockSpec((rows, tile), lambda k: (0, k))
    return list(
        kernel_call(
            lambda *refs: terms_kernel(split, *refs),
            (columns // tile,),
            [left_spec] * 4 + [right_spec] * 2,
            [pl.BlockSpec((size, tile), lambda k: (0, k))] * lines,
            [jax.ShapeDtypeStruct((size, columns), jnp.bfloat16)] * lines,
            [],
            "weight_terms",
            4 * count * rows * columns,
            2 * (4 * count * rows + 2 * rows * columns + count * columns),
        )(*left, *left_last, *right)
    )


def summed(refs, rows, columns):
    own, up, down = [ref[rows, columns].astype(jnp.float32) for ref in refs]
    return own + up + down


def plain_step_kernel(own, up, down, weight, first, second, *outs):
    everything = slice(None)
    gradient = summed((own, up, down), everything, everything)
    news = adamw(weight[0], first[0], second[0], gradient, matrix_rate, weight_decay)
    for out, value in zip(outs, (gradient,) + tuple(news)):
        out[0] = value


def plain_step(start, parts_of_sum, params):
    kinds, rows, columns = params[0].shape
    tile = rows // 2
    part = pl.BlockSpec((tile, columns), lambda k, r: (r, start + k))
    block = pl.BlockSpec((1, tile, columns), lambda k, r: (k, r, 0))
    return kernel_call(
        plain_step_kernel,
        (kinds, 2),
        [part] * 3 + [block] * 3,
        [block] * 4,
        [jax.ShapeDtypeStruct((kinds, rows, columns), jnp.float32)] * 4,
        [],
        "plain_step",
    )(*parts_of_sum, *params)


def feed_step_kernel(runs, *refs):
    count = 3 * len(runs)
    gate, down = refs[count : count + 3], refs[count + 3 : count + 6]
    gate_outs, down_outs = refs[count + 6 : count + 10], refs[count + 10 : count + 14]
    everything = slice(None)
    for at, (low, high) in enumerate(runs):
        sums = refs[3 * at : 3 * at + 3]
        padded = sums[0].shape[1] // 3
        for c in range(0, high - low, 128):
            size = min(128, high - low - c)
            here = slice(low + c, low + c + size)
            for k in range(2):
                gradient = summed(sums, everything, slice(2 * c + 128 * k, 2 * c + 128 * k + size))
                news = adamw(
                    *[ref[:, k, here] for ref in gate], gradient, matrix_rate, weight_decay
                )
                for out, value in zip(gate_outs, (gradient,) + tuple(news)):
                    out[:, k, here] = value
        here = slice(low, high)
        gradient = summed(sums, everything, slice(2 * padded, 2 * padded + high - low))
        news = adamw(*[ref[:, here] for ref in down], gradient, matrix_rate, weight_decay)
        for out, value in zip(down_outs, (gradient,) + tuple(news)):
            out[:, here] = value


def feed_step(runs, sums, gate, down):
    rows, columns = down[0].shape
    tile = 32
    gate_block = pl.BlockSpec((tile, 2, columns), lambda r: (r, 0, 0))
    down_block = pl.BlockSpec((tile, columns), lambda r: (r, 0))
    flat = [part for parts_of_sum in sums for part in parts_of_sum]
    return kernel_call(
        lambda *refs: feed_step_kernel(runs, *refs),
        (rows // tile,),
        [pl.BlockSpec((tile, part.shape[1]), lambda r: (r, 0)) for part in flat]
        + [gate_block] * 3
        + [down_block] * 3,
        [gate_block] * 4 + [down_block] * 4,
        [jax.ShapeDtypeStruct((rows, 2, columns), jnp.float32)] * 4
        + [jax.ShapeDtypeStruct((rows, columns), jnp.float32)] * 4,
        [],
        "feed_step",
        0,
        84 * rows * columns,
    )(*flat, *gate, *down)


def on_device(
    tokens,
    cotangent,
    lengths,
    entry_weight,
    entry_first,
    entry_second,
    exit_weight,
    exit_first,
    exit_second,
    gate_weight,
    gate_first,
    gate_second,
    down_weight,
    down_first,
    down_second,
    bias_rows,
    bias_first,
    bias_second,
    norm_gains,
    gains_first,
    gains_second,
):
    parts = lax.axis_size("tensor")
    part_index = lax.axis_index("tensor")
    dp_index = lax.axis_index("dp")
    dp_count = lax.axis_size("dp")
    lines = dp_count // 2
    last = lines - 1
    place = dp_index // 2
    core = dp_index % 2
    local_rows = tokens.shape[0]
    group = local_rows * parts
    width = tokens.shape[1]
    size = width // dp_count
    head_cols = entry_weight.shape[2]
    hidden_cols = down_weight.shape[1]
    bf16 = jnp.bfloat16
    own_blocks = [((place - s + lines) % lines) * 2 + core for s in range(lines)]
    other_blocks = [((place - s + lines) % lines) * 2 + 1 - core for s in range(lines)]
    none = (None, None)

    def advance(streams):
        return [
            (blocks, scatter_step(blocks, *way, left, lines), left - 1) if left > 0 else stream
            for stream in streams
            for blocks, way, left in [stream]
        ]

    def begin(blocks):
        return advance([(blocks, none, last)])

    def finish(streams):
        while any(left > 0 for _, _, left in streams):
            streams = advance(streams)
        return streams

    def parts_of(stream):
        blocks, way, _ = stream
        return (blocks[0],) + tuple(way)

    def both_cores(array):
        both = turned_blocks(array, own_blocks + other_blocks, size)
        return both[: width // 2], other_core(both[width // 2 :])

    kinds_own = jnp.concatenate(
        [jnp.swapaxes(entry_weight, 0, 1).astype(bf16), exit_weight.astype(bf16)[None]], axis=0
    )
    kinds = lax.all_gather(kinds_own, "dp", axis=1, tiled=True)
    chunks = cuts(hidden_cols, MLP_CHUNKS)

    def unit_of(a, b):
        gates = paired(gate_weight[:, :, a:b].astype(bf16)).reshape(size, -1)
        downs = jnp.pad(down_weight[:, a:b].astype(bf16), ((0, 0), (0, -(b - a) % 128)))
        return jnp.concatenate([gates, downs], axis=1)

    unit_a, unit_b = [unit_of(a, b) for a, b in chunks]
    full_a = lax.all_gather(after(unit_a, kinds_own), "dp", axis=0, tiled=True)

    segment, positions = segments(lengths[0], group)
    row_blocks = jnp.arange(parts, dtype=jnp.int32) ^ part_index
    row_index = (
        row_blocks[:, None] * local_rows + jnp.arange(local_rows, dtype=jnp.int32)[None, :]
    ).reshape(group)
    segment, positions = [
        jnp.concatenate(
            [
                lax.dynamic_slice_in_dim(array, (part_index ^ r) * local_rows, local_rows, 0)
                for r in range(parts)
            ]
        )
        for array in (segment, positions)
    ]
    cosine, sine = rotary_tables(positions.astype(jnp.float32))
    ones = jnp.ones((group, HD - ROT), jnp.float32)
    blank = jnp.zeros((group, ROT // 2), jnp.float32)
    empty = jnp.zeros((group, HD - ROT), jnp.float32)
    tables = [
        jnp.concatenate([a, b, c] * 2, axis=1)
        for a, b, c in ((cosine, cosine, ones), (-sine, blank, empty), (blank, sine, empty))
    ]
    marks = (jnp.stack([segment, row_index], axis=1), jnp.stack([segment, row_index], axis=0))
    column_start = part_index * head_cols
    rotmask = (jnp.arange(head_cols, dtype=jnp.int32) % HD < ROT).astype(jnp.float32)
    query_bias = lax.dynamic_slice_in_dim(bias_rows[0], column_start, head_cols, 0)
    key_bias = lax.dynamic_slice_in_dim(bias_rows[1], column_start, head_cols, 0) * rotmask
    value_bias = lax.dynamic_slice_in_dim(bias_rows[2], column_start, head_cols, 0)
    offsets = jnp.stack([query_bias, key_bias, value_bias])

    rows_in = tokens.astype(jnp.float32)
    normed, unit_one, factor_one = norm_forward(rows_in, norm_gains[0], bias_rows[3])
    normed_all = gather_rows(normed.astype(bf16), parts)
    cot_all = gather_rows(after(cotangent, normed_all), parts)
    normed_sides = both_cores(after(normed_all, cot_all))
    cot_sides = both_cores(after(cot_all, normed_sides[0]))
    kinds, normed_all, normed_sides, cot_all, cot_sides, tables, marks = together(
        kinds, normed_all, normed_sides, cot_all, cot_sides, tables, marks
    )

    mixed, context, log_totals = attend(normed_all, kinds, offsets, tables, marks)
    branch = dot(context, kinds[3], ((1,), (1,))).astype(bf16)
    branch = scatter_rows(branch, parts)
    middle = rows_in + branch
    second, unit_two, factor_two = norm_forward(middle, norm_gains[1], bias_rows[4])
    second_all = gather_rows(second.astype(bf16), parts)
    second_all, full_a, unit_b = together(second_all, full_a, unit_b)

    way_b = gather_from(([unit_b], [unit_b]), 1, 2, lines)
    natural = jnp.arange(dp_count, dtype=jnp.int32)
    acts, branch_a, second_a = feed(second_all, cot_all, [full_a], natural, size)
    acts, branch_a, second_a, way_b = together(acts, branch_a, second_a, way_b)

    way_b = gather_from(way_b, 2, 3, lines)
    acts_other = other_core(acts)
    second_sides = both_cores(after(second_all, acts))
    padded = acts.shape[1] // 3
    terms = weight_terms(second_sides, cot_sides, (acts, acts_other), padded, 2, lines)
    terms, way_b = together(terms, way_b)

    way_b = gather_from(way_b, 3, lines, lines)
    streams = begin(terms)
    streams, way_b = together_streams(streams, way_b)

    streams = advance(streams)
    half = pack(*way_b, place, lines)
    order = jnp.stack(own_blocks + other_blocks).astype(jnp.int32)
    acts, branch_b, second_b = feed(second_all, cot_all, [half, other_core(half)], order, size)
    streams, (second_b, branch_b, acts) = together_streams(streams, (second_b, branch_b, acts))
    second_grad = add_terms([second_a, second_b])
    branch_terms = [branch_a, branch_b]
    streams, second_grad = together_streams(streams, second_grad)

    streams = advance(streams)
    acts_other = other_core(acts)
    arrived = send_rows(second_grad, parts)
    padded = acts.shape[1] // 3
    terms = weight_terms(second_sides, cot_sides, (acts, acts_other), padded, 2, lines)
    streams, (arrived, terms) = together_streams(streams, (arrived, terms))

    second_grad = add_up(arrived)
    middle_grad = cotangent.astype(jnp.float32) + norm_backward(
        second_grad, unit_two, factor_two, norm_gains[1]
    )
    middle_low = middle_grad.astype(bf16)
    streams, (middle_low, terms) = together_streams(streams, (middle_low, terms))
    middle_all = gather_rows(middle_low, parts)
    streams = advance(streams) + begin(terms)
    streams, middle_all = together_streams(streams, middle_all)

    streams = advance(streams)
    mixed_grad, normed_terms = attend_back(
        middle_all, kinds, mixed, context, log_totals, tables, marks
    )
    streams, (mixed_grad, normed_terms, middle_all) = together_streams(
        streams, (mixed_grad, normed_terms, middle_all)
    )

    arrived = send_rows(normed_terms, parts)
    streams = advance(streams)
    mixed_other = other_core(mixed_grad)
    middle_sides = both_cores(middle_all)
    entry_terms = weight_terms(
        normed_sides, middle_sides, (mixed_grad, mixed_other), head_cols, 3, lines
    )
    streams, (arrived, entry_terms) = together_streams(streams, (arrived, entry_terms))

    streams = streams + begin(entry_terms)
    normed_grad = add_up(arrived)
    input_gradient = middle_grad + norm_backward(normed_grad, unit_one, factor_one, norm_gains[0])
    gain_two_grad = jnp.sum(second_grad * unit_two, axis=0)
    shift_two_grad = jnp.sum(second_grad, axis=0)
    gain_one_grad = jnp.sum(normed_grad * unit_one, axis=0)
    shift_one_grad = jnp.sum(normed_grad, axis=0)
    column_sums = jnp.sum(mixed_grad[:, : 3 * head_cols].astype(jnp.float32), axis=0).reshape(3, head_cols)
    column_sums = column_sums * jnp.stack([jnp.ones_like(rotmask), rotmask, jnp.ones_like(rotmask)])
    placed = lax.dynamic_update_slice_in_dim(
        jnp.zeros((3, width), jnp.float32), column_sums, column_start, 1
    )
    norms_local = jnp.stack([shift_one_grad, shift_two_grad, gain_one_grad, gain_two_grad])
    vectors = jnp.concatenate([placed, norms_local], axis=0)
    bit = 1
    while bit < parts:
        vectors = hop(vectors, "tensor", bit)
        bit *= 2
    vectors = hop(vectors, "dp", 1)

    streams, vectors = together_streams(streams, vectors)

    streams = finish(streams[:-1]) + advance(streams[-1:])
    bit = 2
    while bit < dp_count:
        vectors = hop(vectors, "dp", bit)
        bit *= 2
    streams, (vectors, branch_terms) = together_streams(streams, (vectors, branch_terms))

    streams = finish(streams)
    (
        gate_gradient, gate_updated, gate_first_new, gate_second_new,
        down_gradient, down_updated, down_first_new, down_second_new,
    ) = feed_step(
        chunks,
        [parts_of(stream) for stream in streams[:-1]],
        (gate_weight, gate_first, gate_second),
        (down_weight, down_first, down_second),
    )
    branch_two = scatter_rows(add_terms(branch_terms), parts)
    output_rows = (middle + branch_two).astype(bf16)
    bias_gradient = vectors[:5]
    gains_gradient = vectors[5:]
    streams, _ = together_streams(streams, gate_updated)
    kind_first = lambda array: jnp.swapaxes(array, 0, 1)
    entry_gradient, entry_updated, entry_first_new, entry_second_new = [
        kind_first(array)
        for array in plain_step(
            0, parts_of(streams[-1]), [kind_first(array) for array in (entry_weight, entry_first, entry_second)]
        )
    ]
    exit_gradient, exit_updated, exit_first_new, exit_second_new = [
        array[0]
        for array in plain_step(
            3, parts_of(streams[-1]), [array[None] for array in (exit_weight, exit_first, exit_second)]
        )
    ]
    bias_updated, bias_first_new, bias_second_new = adamw(
        bias_rows, bias_first, bias_second, bias_gradient, vector_rate, 0.0
    )
    gains_updated, gains_first_new, gains_second_new = adamw(
        norm_gains, gains_first, gains_second, gains_gradient, vector_rate, 0.0
    )
    return (
        output_rows,
        input_gradient,
        entry_gradient,
        entry_updated,
        entry_first_new,
        entry_second_new,
        exit_gradient,
        exit_updated,
        exit_first_new,
        exit_second_new,
        gate_gradient,
        gate_updated,
        gate_first_new,
        gate_second_new,
        down_gradient,
        down_updated,
        down_first_new,
        down_second_new,
        bias_gradient,
        bias_updated,
        bias_first_new,
        bias_second_new,
        gains_gradient,
        gains_updated,
        gains_first_new,
        gains_second_new,
    )


def solution(mesh):
    return jax.shard_map(
        on_device,
        mesh=mesh,
        in_specs=(
            P(("dp", "tensor"), None),
            P(("dp", "tensor"), None),
            P("dp", None),
            P("dp", None, "tensor"),
            P("dp", None, "tensor"),
            P("dp", None, "tensor"),
            P("dp", "tensor"),
            P("dp", "tensor"),
            P("dp", "tensor"),
            P("dp", None, "tensor"),
            P("dp", None, "tensor"),
            P("dp", None, "tensor"),
            P("dp", "tensor"),
            P("dp", "tensor"),
            P("dp", "tensor"),
            P(),
            P(),
            P(),
            P(),
            P(),
            P(),
        ),
        out_specs=(
            P(("dp", "tensor"), None),
            P(("dp", "tensor"), None),
            P("dp", None, "tensor"),
            P("dp", None, "tensor"),
            P("dp", None, "tensor"),
            P("dp", None, "tensor"),
            P("dp", "tensor"),
            P("dp", "tensor"),
            P("dp", "tensor"),
            P("dp", "tensor"),
            P("dp", None, "tensor"),
            P("dp", None, "tensor"),
            P("dp", None, "tensor"),
            P("dp", None, "tensor"),
            P("dp", "tensor"),
            P("dp", "tensor"),
            P("dp", "tensor"),
            P("dp", "tensor"),
            P(),
            P(),
            P(),
            P(),
            P(),
            P(),
            P(),
            P(),
        ),
        check_vma=False,
    )
```

```python
import jax
import jax.numpy as jnp
from jax import lax
from jax.experimental import pallas as pl
from jax.experimental.pallas import tpu as pltpu
from jax.sharding import PartitionSpec as P

HD = 64
ROT = 16
STEP = 3


norm_eps = 1e-05
rope_base = 10000.0
masked_score = -1e30
beta_one = 0.9
beta_two = 0.95
adam_eps = 1e-08
matrix_rate = 0.08
vector_rate = 0.4
weight_decay = 0.1


def norm_forward(rows, gain, shift):
    centre = jnp.mean(rows, axis=-1, keepdims=True)
    centred = rows - centre
    spread = jnp.mean(centred * centred, axis=-1, keepdims=True)
    factor = lax.rsqrt(spread + norm_eps)
    unit = centred * factor
    return (unit * gain + shift, unit, factor)


def norm_backward(incoming, unit, factor, gain):
    scaled = incoming * gain
    mean_plain = jnp.mean(scaled, axis=-1, keepdims=True)
    mean_along = jnp.mean(scaled * unit, axis=-1, keepdims=True)
    return factor * (scaled - mean_plain - unit * mean_along)


def segments(lengths_row, count):
    ends = jnp.cumsum(lengths_row)
    index = jnp.arange(count, dtype=jnp.int32)
    after = index[:, None] >= ends[None, :]
    segment = jnp.sum(after.astype(jnp.int32), axis=1)
    begin = jnp.max(jnp.where(after, ends[None, :], jnp.zeros_like(ends)[None, :]), axis=1)
    return (segment, index - begin)


def rotary_tables(positions):
    half = ROT // 2
    freqs = rope_base ** (-2.0 * jnp.arange(half, dtype=jnp.float32) / ROT)
    angles = positions[:, None] * freqs[None, :]
    return (jnp.cos(angles), jnp.sin(angles))


def adamw(weight, first, second, gradient, rate, decay):
    first_new = beta_one * first + (1.0 - beta_one) * gradient
    second_new = beta_two * second + (1.0 - beta_two) * gradient * gradient
    first_hat = first_new / (1.0 - beta_one**STEP)
    second_hat = second_new / (1.0 - beta_two**STEP)
    updated = weight - rate * (first_hat / (jnp.sqrt(second_hat) + adam_eps) + decay * weight)
    return (updated, first_new, second_new)


def together(*groups):
    flat, tree = jax.tree.flatten(groups)
    return jax.tree.unflatten(tree, lax.optimization_barrier(flat))


def after(value, *earlier):
    return lax.optimization_barrier((value,) + tuple(earlier))[0]


def pairs_up(lines, low, high, step):
    return [(z * 2 + c, (z + step) * 2 + c) for z in range(low, high) for c in range(2)]


def other_core(array):
    count = lax.axis_size("dp")
    return lax.ppermute(array, "dp", [(d, d ^ 1) for d in range(count)])


def gather_step(ups, downs, s, lines):
    up = lax.ppermute(ups[-1], "dp", pairs_up(lines, s - 1, lines - 1, 1))
    down = lax.ppermute(downs[-1], "dp", pairs_up(lines, 1, lines - s + 1, -1))
    return ups + [up], downs + [down]


def gather_from(way, low, high, lines):
    for s in range(low, high):
        way = gather_step(*way, s, lines)
    return way


def pack_kernel(lines, place_ref, *refs):
    pieces, out = refs[:-1], refs[-1]
    place = place_ref[0]
    s = pl.program_id(0)
    for at in range(lines):

        @pl.when((s == at) & (place >= at))
        def _():
            out[...] = pieces[at][...]

        if at > 0:

            @pl.when((s == at) & (place < at))
            def _():
                out[...] = pieces[2 * lines - 1 - at][...]


def pack(ups, downs, place, lines):
    rows, columns = ups[0].shape
    tile = min(128, rows)
    tiles = rows // tile

    def spec(at, is_up):
        def index(s, t, place_ref):
            wanted = (s == at) & ((place_ref[0] >= at) if is_up else (place_ref[0] < at))
            return (jnp.where(wanted, t, jnp.where(s > at, tiles - 1, 0)), 0)

        return pl.BlockSpec((tile, columns), index)

    return pl.pallas_call(
        lambda *refs: pack_kernel(lines, *refs),
        grid_spec=pltpu.PrefetchScalarGridSpec(
            num_scalar_prefetch=1,
            grid=(lines, tiles),
            in_specs=[spec(at, True) for at in range(lines)]
            + [spec(lines - at, False) for at in range(1, lines)],
            out_specs=pl.BlockSpec((tile, columns), lambda s, t, place_ref: (s * tiles + t, 0)),
        ),
        out_shape=jax.ShapeDtypeStruct((lines * rows, columns), ups[0].dtype),
        compiler_params=pltpu.CompilerParams(vmem_limit_bytes=40 * 1024 * 1024),
        cost_estimate=pl.CostEstimate(
            flops=0, bytes_accessed=4 * lines * rows * columns, transcendentals=0
        ),
        name="pack_blocks",
    )(place.reshape(1).astype(jnp.int32), *ups, *downs[1:])


def scatter_step(blocks, up, down, j, lines):
    up_send = blocks[lines - j] if up is None else blocks[lines - j] + up
    down_send = blocks[j] if down is None else blocks[j] + down
    up = lax.ppermute(up_send, "dp", pairs_up(lines, 0, lines - j, 1))
    down = lax.ppermute(down_send, "dp", pairs_up(lines, j, lines, -1))
    return up, down


def swap_rows(array, offset):
    count = lax.axis_size("tensor")
    return lax.ppermute(array, "tensor", [(t, t ^ offset) for t in range(count)])


def gather_rows(own, parts):
    return jnp.concatenate([own] + [swap_rows(own, r) for r in range(1, parts)], axis=0)


def send_rows(partial, parts):
    rows = partial.shape[0] // parts
    blocks = [partial[r * rows : (r + 1) * rows] for r in range(parts)]
    return [blocks[0]] + [swap_rows(blocks[r], r) for r in range(1, parts)]


def add_up(terms):
    total = terms[0].astype(jnp.float32)
    for term in terms[1:]:
        total = total + term.astype(jnp.float32)
    return total


def scatter_rows(partial, parts):
    return add_up(send_rows(partial, parts))


def together_streams(streams, others):
    ways, blocks, others = together(
        [way for _, way, _ in streams], [blocks for blocks, _, _ in streams], others
    )
    return [(b, w, left) for b, w, (_, _, left) in zip(blocks, ways, streams)], others


def hop(array, axis, bit):
    count = lax.axis_size(axis)
    return array + lax.ppermute(array, axis, [(i, i ^ bit) for i in range(count)])


def cuts(columns):
    first = min(columns, 128 * -(-(-(-columns // 128) * 5) // 11))
    return [(0, first), (first, columns)]


def paired(array):
    rows, kinds, columns = array.shape
    array = jnp.pad(array, ((0, 0), (0, 0), (0, -columns % 128)))
    return jnp.swapaxes(array.reshape(rows, kinds, -1, 128), 1, 2)


def dot(a, b, contract):
    return lax.dot_general(a, b, (contract, ((), ())), preferred_element_type=jnp.float32)


def whole(shape):
    return pl.BlockSpec(shape, lambda *_: (0,) * len(shape))


def kernel_call(kernel, grid, in_specs, out_specs, out_shape, scratch, name, flops=1, moved=1):
    return pl.pallas_call(
        kernel,
        grid=grid,
        in_specs=in_specs,
        out_specs=out_specs,
        out_shape=out_shape,
        scratch_shapes=scratch,
        compiler_params=pltpu.CompilerParams(vmem_limit_bytes=56 * 1024 * 1024),
        cost_estimate=pl.CostEstimate(flops=flops, bytes_accessed=moved, transcendentals=0),
        name=name,
    )


def turn(x, keep, low, high, direction):
    return (
        x * keep
        + pltpu.roll(x, 120, 1) * (low * direction)
        + pltpu.roll(x, 8, 1) * (high * direction)
    )


def row_steps(rows):
    return 128 if rows % 128 == 0 else rows


def fill_bias(bias_ref, column_ref, row_ref):
    rows = bias_ref.shape[0]
    step = row_steps(rows)

    def body(r, _):
        at = pl.ds(pl.multiple_of(r * step, step), step)
        marks = column_ref[at, :]
        visible = (marks[:, 0:1] == row_ref[0:1, :]) & (marks[:, 1:2] >= row_ref[1:2, :])
        bias_ref[at, :] = jnp.where(visible, 0.0, masked_score)
        return 0

    lax.fori_loop(0, rows // step, body, 0)


def matmul(a, b, contract=((1,), (0,))):
    return lax.dot_general(a, b, (contract, ((), ())), preferred_element_type=jnp.float32)


def attend_kernel(
    normed_ref, weight_ref, offset_ref, keep_ref, low_ref, high_ref, column_ref, row_ref,
    mixed_ref, context_ref, totals_ref, bias_ref, score_ref, prob_ref,
):
    kind = pl.program_id(0)
    rows, columns = context_ref.shape
    step = row_steps(rows)
    raw = matmul(normed_ref[...], weight_ref[0]) + offset_ref[0]
    here = pl.multiple_of(kind * columns, 128)

    @pl.when(kind < 2)
    def _():
        for b in range(columns // 128):
            block = turn(raw[:, b * 128 : (b + 1) * 128], keep_ref[...], low_ref[...], high_ref[...], 1.0)
            mixed_ref[:, pl.ds(pl.multiple_of(here + b * 128, 128), 128)] = block.astype(jnp.bfloat16)

    @pl.when(kind == 2)
    def _():
        mixed_ref[:, pl.ds(here, columns)] = raw.astype(jnp.bfloat16)
        fill_bias(bias_ref, column_ref, row_ref)
        lane = lax.broadcasted_iota(jnp.int32, (1, 128), 1)

        def pair_body(pair, _):
            first = pl.multiple_of(pair * 128, 128)
            queries = mixed_ref[:, pl.ds(first, 128)]
            keys = mixed_ref[:, pl.ds(pl.multiple_of(columns + first, 128), 128)]
            values = mixed_ref[:, pl.ds(pl.multiple_of(2 * columns + first, 128), 128)]
            parts = []
            for h in range(2):
                mine = (lane >= HD * h) & (lane < HD * (h + 1))
                score_ref[...] = matmul(
                    jnp.where(mine, queries, jnp.zeros_like(queries)), keys, ((1,), (1,))
                )

                def rows_body(r, _):
                    at = pl.ds(pl.multiple_of(r * step, step), step)
                    scores = score_ref[at, :] * (HD**-0.5) + bias_ref[at, :]
                    summit = jnp.max(scores, axis=1, keepdims=True)
                    weights = jnp.exp(scores - summit)
                    total = jnp.sum(weights, axis=1, keepdims=True)
                    prob_ref[at, :] = (weights * (1.0 / total)).astype(jnp.bfloat16)
                    spot = lane == pair * 2 + h
                    totals_ref[at, :] = jnp.where(
                        spot, summit + jnp.log(total), totals_ref[at, :]
                    )
                    return 0

                lax.fori_loop(0, rows // step, rows_body, 0, unroll=True)
                parts.append(matmul(prob_ref[...], values))
            both = jnp.where(lane < HD, parts[0], parts[1])
            context_ref[:, pl.ds(first, 128)] = both.astype(jnp.bfloat16)
            return 0

        totals_ref[...] = jnp.zeros_like(totals_ref)
        lax.fori_loop(0, columns // 128, pair_body, 0)


def attend(normed_all, entry_full, offsets, tables, marks):
    rows, width = normed_all.shape
    columns = entry_full.shape[2]
    bf16, f32 = jnp.bfloat16, jnp.float32
    return kernel_call(
        attend_kernel,
        (3,),
        [whole((rows, width)), pl.BlockSpec((1, width, columns), lambda k: (k, 0, 0)),
         pl.BlockSpec((1, 1, columns), lambda k: (k, 0, 0))]
        + [whole((rows, 128))] * 3 + [whole((rows, 2)), whole((2, rows))],
        [whole((rows, 3 * columns)), whole((rows, columns)), whole((rows, 128))],
        [jax.ShapeDtypeStruct((rows, 3 * columns), bf16), jax.ShapeDtypeStruct((rows, columns), bf16),
         jax.ShapeDtypeStruct((rows, 128), f32)],
        [pltpu.VMEM((rows, rows), f32), pltpu.VMEM((rows, rows), f32), pltpu.VMEM((rows, rows), bf16)],
        "attention",
        24 * rows * width * columns,
        8 * rows * width,
    )(normed_all, entry_full, offsets.reshape(3, 1, columns), *tables, *marks)


def attend_back_kernel(
    middle_ref, exit_ref, mixed_ref, context_ref, totals_ref, keep_ref, low_ref, high_ref, column_ref,
    row_ref, kinds_ref, grad_ref, normed_ref, bias_ref, score_ref, prob_grad_ref, prob_ref,
    score_grad_ref, context_grad_ref, weight_ref, sem,
):
    rows = middle_ref.shape[0]
    columns = exit_ref.shape[2]
    step = row_steps(rows)
    load = pltpu.make_async_copy(kinds_ref.at[pl.ds(0, 3)], weight_ref, sem)
    load.start()
    grad_ref[:, 3 * columns :] = context_ref[...]
    context_grad_ref[...] = matmul(middle_ref[...], exit_ref[0]).astype(jnp.bfloat16)
    fill_bias(bias_ref, column_ref, row_ref)
    lane = lax.broadcasted_iota(jnp.int32, (1, 128), 1)

    def pair_body(pair, _):
        first = pl.multiple_of(pair * 128, 128)
        second = pl.multiple_of(columns + first, 128)
        third = pl.multiple_of(2 * columns + first, 128)
        queries = mixed_ref[:, pl.ds(first, 128)]
        keys = mixed_ref[:, pl.ds(second, 128)]
        values = mixed_ref[:, pl.ds(third, 128)]
        incoming = context_grad_ref[:, pl.ds(first, 128)]
        query_parts, key_parts, value_parts = [], [], []
        for h in range(2):
            mine = (lane >= HD * h) & (lane < HD * (h + 1))
            score_ref[...] = matmul(
                jnp.where(mine, queries, jnp.zeros_like(queries)), keys, ((1,), (1,))
            )
            prob_grad_ref[...] = matmul(
                jnp.where(mine, incoming, jnp.zeros_like(incoming)), values, ((1,), (1,))
            )

            def rows_body(r, _):
                at = pl.ds(pl.multiple_of(r * step, step), step)
                spot = lane == pair * 2 + h
                total = jnp.sum(jnp.where(spot, totals_ref[at, :], 0.0), axis=1, keepdims=True)
                probs = jnp.exp(score_ref[at, :] * (HD**-0.5) + bias_ref[at, :] - total)
                prob_grad = prob_grad_ref[at, :]
                inner = jnp.sum(probs * prob_grad, axis=1, keepdims=True)
                score_grad_ref[at, :] = (probs * (prob_grad - inner)).astype(jnp.bfloat16)
                prob_ref[at, :] = probs.astype(jnp.bfloat16)
                return 0

            lax.fori_loop(0, rows // step, rows_body, 0, unroll=True)
            query_parts.append(matmul(score_grad_ref[...], keys))
            key_parts.append(matmul(score_grad_ref[...], queries, ((0,), (0,))))
            value_parts.append(matmul(prob_ref[...], incoming, ((0,), (0,))))
        keep, low, high = keep_ref[...], low_ref[...], high_ref[...]
        scale = HD**-0.5
        query_grad = jnp.where(lane < HD, query_parts[0], query_parts[1]) * scale
        key_grad = jnp.where(lane < HD, key_parts[0], key_parts[1]) * scale
        value_grad = jnp.where(lane < HD, value_parts[0], value_parts[1])
        grad_ref[:, pl.ds(first, 128)] = turn(query_grad, keep, low, high, -1.0).astype(jnp.bfloat16)
        grad_ref[:, pl.ds(second, 128)] = turn(key_grad, keep, low, high, -1.0).astype(jnp.bfloat16)
        grad_ref[:, pl.ds(third, 128)] = value_grad.astype(jnp.bfloat16)
        return 0

    lax.fori_loop(0, columns // 128, pair_body, 0)
    load.wait()
    width = normed_ref.shape[1]
    for low in range(0, width, 512):
        here = slice(low, min(low + 512, width))
        total = None
        for k in range(3):
            term = matmul(
                grad_ref[:, k * columns : (k + 1) * columns], weight_ref[k, here, :], ((1,), (1,))
            )
            total = term if total is None else total + term
        normed_ref[:, here] = total.astype(jnp.bfloat16)


def attend_back(middle_all, exit_full, mixed, context, totals, tables, marks):
    rows, width = middle_all.shape
    columns = exit_full.shape[2]
    bf16, f32 = jnp.bfloat16, jnp.float32
    square = (rows, rows)
    return kernel_call(
        attend_back_kernel,
        (1,),
        [whole((rows, width)), pl.BlockSpec((1, width, columns), lambda *_: (3, 0, 0)),
         whole((rows, 3 * columns)), whole((rows, columns)), whole((rows, 128))]
        + [whole((rows, 128))] * 3 + [whole((rows, 2)), whole((2, rows))]
        + [pl.BlockSpec(memory_space=pl.ANY)],
        [whole((rows, 4 * columns)), whole((rows, width))],
        [jax.ShapeDtypeStruct((rows, 4 * columns), bf16), jax.ShapeDtypeStruct((rows, width), bf16)],
        [pltpu.VMEM(square, f32), pltpu.VMEM(square, f32), pltpu.VMEM(square, f32),
         pltpu.VMEM(square, bf16), pltpu.VMEM(square, bf16), pltpu.VMEM((rows, columns), bf16),
         pltpu.VMEM((3, width, columns), bf16), pltpu.SemaphoreType.DMA],
        "attention_back",
        24 * rows * width * columns,
        8 * rows * width,
    )(middle_all, exit_full, mixed, context, totals, *tables, *marks, exit_full)


def feed_kernel(pieces, order_ref, second_in, cot_in, *refs):
    fulls, refs = refs[:pieces], refs[pieces:]
    earlier, refs = (refs[:2], refs[2:]) if pieces > 1 else ((), refs)
    acts_ref, branch_ref, second_grad_ref, weight_ref, hidden_grad_ref, sems = refs[:6]
    j = pl.program_id(0)
    rows, width = second_in.shape
    padded = acts_ref.shape[1] // 3
    pairs = padded // 128
    size = branch_ref.shape[1]
    height = width // pieces
    bf16 = jnp.bfloat16
    second_ref, cot_ref = (second_in, cot_in) if pieces == 1 else refs[6:]

    def loads(at, columns, which):
        here = pl.ds(at, columns)
        return [
            pltpu.make_async_copy(
                full.at[:, here], weight_ref.at[pl.ds(p * height, height), here], sems.at[p, which]
            )
            for p, full in enumerate(fulls)
        ]

    @pl.when(j == 0)
    def _():
        for load in loads(2 * padded, padded, 0):
            load.start()
        for p in range(pairs):
            for load in loads(p * 256, 256, p + 1):
                load.start()
        if pieces > 1:
            for b in range(width // size):
                there = pl.ds(pl.multiple_of(order_ref[b] * size, size), size)
                second_ref[:, b * size : (b + 1) * size] = second_in[:, there]
                cot_ref[:, b * size : (b + 1) * size] = cot_in[:, there]
        for load in loads(2 * padded, padded, 0):
            load.wait()
        for low in range(0, padded, 256):
            high = min(low + 256, padded)
            hidden_grad_ref[:, low:high] = matmul(
                cot_ref[...], weight_ref[:, 2 * padded + low : 2 * padded + high]
            )
        for p in range(pairs):
            for load in loads(p * 256, 256, p + 1):
                load.wait()
            gate_up = matmul(second_ref[...], weight_ref[:, p * 256 : (p + 1) * 256])
            gate, upper = gate_up[:, :128], gate_up[:, 128:]
            grad = hidden_grad_ref[:, p * 128 : (p + 1) * 128]
            sigmoid = jax.nn.sigmoid(gate)
            activated = gate * sigmoid
            acts_ref[:, p * 256 : p * 256 + 128] = (
                grad * upper * sigmoid * (1.0 + gate * (1.0 - sigmoid))
            ).astype(bf16)
            acts_ref[:, p * 256 + 128 : (p + 1) * 256] = (grad * activated).astype(bf16)
            hidden = 2 * padded + p * 128
            acts_ref[:, hidden : hidden + 128] = (activated * upper).astype(bf16)

    @pl.when(j > 0)
    def _():
        here = pl.ds(pl.multiple_of((j - 1) * size, size), size)
        over = ((1,), (1,))
        branch = matmul(acts_ref[:, 2 * padded :], weight_ref[here, 2 * padded :], over)
        second_grad = matmul(acts_ref[:, : 2 * padded], weight_ref[here, : 2 * padded], over)
        if pieces > 1:
            branch = branch + earlier[0][...].astype(jnp.float32)
            second_grad = second_grad + earlier[1][...].astype(jnp.float32)
        branch_ref[...] = branch.astype(bf16)
        second_grad_ref[...] = second_grad.astype(bf16)


def feed(second_all, cot_all, fulls, order, size, earlier=()):
    rows, width = second_all.shape
    padded = fulls[0].shape[1] // 3
    pieces = len(fulls)
    bf16, f32 = jnp.bfloat16, jnp.float32
    full = pl.BlockSpec((rows, width), lambda j, order_ref: (0, 0))
    out = pl.BlockSpec((rows, size), lambda j, order_ref: (0, order_ref[jnp.maximum(j - 1, 0)]))
    scratch = [
        pltpu.VMEM((width, 3 * padded), bf16), pltpu.VMEM((rows, padded), f32),
        pltpu.SemaphoreType.DMA((pieces, 1 + padded // 128)),
    ]
    if pieces > 1:
        scratch += [pltpu.VMEM((rows, width), bf16)] * 2
    return pl.pallas_call(
        lambda *refs: feed_kernel(pieces, *refs),
        grid_spec=pltpu.PrefetchScalarGridSpec(
            num_scalar_prefetch=1,
            grid=(1 + width // size,),
            in_specs=[full] * 2 + [pl.BlockSpec(memory_space=pl.ANY)] * pieces + [out] * len(earlier),
            out_specs=[pl.BlockSpec((rows, 3 * padded), lambda j, order_ref: (0, 0)), out, out],
            scratch_shapes=scratch,
        ),
        out_shape=[jax.ShapeDtypeStruct((rows, 3 * padded), bf16)]
        + [jax.ShapeDtypeStruct((rows, width), bf16)] * 2,
        compiler_params=pltpu.CompilerParams(vmem_limit_bytes=56 * 1024 * 1024),
        cost_estimate=pl.CostEstimate(
            flops=24 * rows * width * padded,
            bytes_accessed=12 * width * padded + 16 * rows * width,
            transcendentals=0,
        ),
        name="feed_forward",
    )(order, second_all, cot_all, *fulls, *earlier)


def turned_kernel(blocks_ref, rows_ref, out_ref):
    out_ref[...] = rows_ref[...].T


def turned_blocks(array, blocks, size):
    rows = array.shape[0]
    return pl.pallas_call(
        turned_kernel,
        grid_spec=pltpu.PrefetchScalarGridSpec(
            num_scalar_prefetch=1,
            grid=(len(blocks),),
            in_specs=[pl.BlockSpec((rows, size), lambda b, blocks_ref: (0, blocks_ref[b]))],
            out_specs=pl.BlockSpec((size, rows), lambda b, blocks_ref: (b, 0)),
        ),
        out_shape=jax.ShapeDtypeStruct((len(blocks) * size, rows), array.dtype),
        compiler_params=pltpu.CompilerParams(vmem_limit_bytes=32 * 1024 * 1024),
        cost_estimate=pl.CostEstimate(flops=1, bytes_accessed=1, transcendentals=0),
        name="turned_blocks",
    )(jnp.stack(blocks).astype(jnp.int32), array)


def terms_kernel(split, groups, own_left, other_left, own_last, other_last, own_ref, other_ref, *outs):
    k = pl.program_id(0)
    lines = len(outs) // groups
    per_group = pl.num_programs(0) // groups

    def write(own, other):
        total = (matmul(own[...], own_ref[...]) + matmul(other[...], other_ref[...])).astype(jnp.bfloat16)
        size = outs[0].shape[0]
        for g in range(groups):

            @pl.when(k // per_group == g)
            def _():
                for s, out in enumerate(outs[g * lines : (g + 1) * lines]):
                    out[...] = total[s * size : (s + 1) * size]

    @pl.when(k < split)
    def _():
        write(own_left, other_left)

    @pl.when(k >= split)
    def _():
        write(own_last, other_last)


def weight_terms(left, left_last, right, tile, split, lines, groups=1):
    count, rows = left[0].shape
    columns = right[0].shape[1]
    size = count // lines
    per_group = columns // tile // groups
    left_spec = whole((count, rows))
    right_spec = pl.BlockSpec((rows, tile), lambda k: (0, k))

    def out_spec(g):
        return pl.BlockSpec((size, tile), lambda k: (0, jnp.clip(k - g * per_group, 0, per_group - 1)))

    outs = kernel_call(
        lambda *refs: terms_kernel(split, groups, *refs),
        (columns // tile,),
        [left_spec] * 4 + [right_spec] * 2,
        [out_spec(g) for g in range(groups) for _ in range(lines)],
        [jax.ShapeDtypeStruct((size, columns // groups), jnp.bfloat16)] * (lines * groups),
        [],
        "weight_terms",
        4 * count * rows * columns,
        2 * (4 * count * rows + 2 * rows * columns + count * columns),
    )(*left, *left_last, *right)
    return [list(outs[g * lines : (g + 1) * lines]) for g in range(groups)]


def summed(refs, rows, columns):
    own, up, down = [ref[rows, columns].astype(jnp.float32) for ref in refs]
    return own + up + down


def plain_step_kernel(own, up, down, weight, first, second, *outs):
    outs = outs[-4:]
    everything = slice(None)
    gradient = summed((own, up, down), everything, everything)
    news = adamw(weight[0], first[0], second[0], gradient, matrix_rate, weight_decay)
    for out, value in zip(outs, (gradient,) + tuple(news)):
        out[0] = value


def plain_step(start, parts_of_sum, params, kinds, earlier=()):
    count, rows, columns = params[0].shape
    tile = rows // 2
    part = pl.BlockSpec((tile, columns), lambda k, r: (r, start + k))
    block = pl.BlockSpec((1, tile, columns), lambda k, r: (kinds[0] + k, r, 0))
    return pl.pallas_call(
        plain_step_kernel,
        grid=(len(kinds), 2),
        in_specs=[part] * 3 + [block] * 3 + [pl.BlockSpec(memory_space=pl.ANY)] * len(earlier),
        out_specs=[block] * 4,
        out_shape=[jax.ShapeDtypeStruct((count, rows, columns), jnp.float32)] * 4,
        input_output_aliases={6 + i: i for i in range(len(earlier))},
        compiler_params=pltpu.CompilerParams(vmem_limit_bytes=56 * 1024 * 1024),
        cost_estimate=pl.CostEstimate(flops=1, bytes_accessed=1, transcendentals=0),
        name="plain_step",
    )(*parts_of_sum, *params, *earlier)


def feed_step_kernel(*refs):
    pairs, singles, gate, down = refs[:3], refs[3:6], refs[6:9], refs[9:12]
    gate_outs, down_outs = refs[-8:-4], refs[-4:]
    everything = slice(None)
    for k in range(2):
        gradient = summed(pairs, everything, slice(128 * k, 128 * k + 128))
        news = adamw(*[ref[:, k, :] for ref in gate], gradient, matrix_rate, weight_decay)
        for out, value in zip(gate_outs, (gradient,) + tuple(news)):
            out[:, k, :] = value
    gradient = summed(singles, everything, everything)
    news = adamw(*[ref[...] for ref in down], gradient, matrix_rate, weight_decay)
    for out, value in zip(down_outs, (gradient,) + tuple(news)):
        out[...] = value


def feed_step(run, parts_of_sum, gate, down, earlier=()):
    rows, columns = down[0].shape
    low, high = run
    blocks = -(-(high - low) // 128)
    gate_block = pl.BlockSpec((rows, 2, 128), lambda c: (0, 0, low // 128 + c))
    down_block = pl.BlockSpec((rows, 128), lambda c: (0, low // 128 + c))
    pair = pl.BlockSpec((rows, 256), lambda c: (0, c))
    single = pl.BlockSpec((rows, 128), lambda c: (0, 2 * blocks + c))
    return pl.pallas_call(
        feed_step_kernel,
        grid=(blocks,),
        in_specs=[pair] * 3 + [single] * 3 + [gate_block] * 3 + [down_block] * 3
        + [pl.BlockSpec(memory_space=pl.ANY)] * len(earlier),
        out_specs=[gate_block] * 4 + [down_block] * 4,
        out_shape=[jax.ShapeDtypeStruct((rows, 2, columns), jnp.float32)] * 4
        + [jax.ShapeDtypeStruct((rows, columns), jnp.float32)] * 4,
        input_output_aliases={12 + i: i for i in range(len(earlier))},
        compiler_params=pltpu.CompilerParams(vmem_limit_bytes=56 * 1024 * 1024),
        cost_estimate=pl.CostEstimate(
            flops=0, bytes_accessed=84 * rows * (high - low), transcendentals=0
        ),
        name="feed_step",
    )(*parts_of_sum, *parts_of_sum, *gate, *down, *earlier)


def on_device(
    tokens,
    cotangent,
    lengths,
    entry_weight,
    entry_first,
    entry_second,
    exit_weight,
    exit_first,
    exit_second,
    gate_weight,
    gate_first,
    gate_second,
    down_weight,
    down_first,
    down_second,
    bias_rows,
    bias_first,
    bias_second,
    norm_gains,
    gains_first,
    gains_second,
):
    parts = lax.axis_size("tensor")
    part_index = lax.axis_index("tensor")
    dp_index = lax.axis_index("dp")
    dp_count = lax.axis_size("dp")
    lines = dp_count // 2
    last = lines - 1
    place = dp_index // 2
    core = dp_index % 2
    local_rows = tokens.shape[0]
    group = local_rows * parts
    width = tokens.shape[1]
    size = width // dp_count
    head_cols = entry_weight.shape[2]
    hidden_cols = down_weight.shape[1]
    bf16 = jnp.bfloat16
    own_blocks = [((place - s + lines) % lines) * 2 + core for s in range(lines)]
    other_blocks = [((place - s + lines) % lines) * 2 + 1 - core for s in range(lines)]
    none = (None, None)

    def advance(streams):
        return [
            (blocks, scatter_step(blocks, *way, left, lines), left - 1) if left > 0 else stream
            for stream in streams
            for blocks, way, left in [stream]
        ]

    def begin(blocks):
        return advance([(blocks, none, last)])

    def finish(streams):
        while any(left > 0 for _, _, left in streams):
            streams = advance(streams)
        return streams

    def parts_of(stream):
        blocks, way, _ = stream
        return (blocks[0],) + tuple(way)

    def both_cores(array):
        both = turned_blocks(array, own_blocks + other_blocks, size)
        return both[: width // 2], other_core(both[width // 2 :])

    kinds_own = jnp.concatenate(
        [jnp.swapaxes(entry_weight, 0, 1).astype(bf16), exit_weight.astype(bf16)[None]], axis=0
    )
    kinds = lax.all_gather(kinds_own, "dp", axis=1, tiled=True)
    chunks = cuts(hidden_cols)

    def unit_of(a, b):
        gates = paired(gate_weight[:, :, a:b].astype(bf16)).reshape(size, -1)
        downs = jnp.pad(down_weight[:, a:b].astype(bf16), ((0, 0), (0, -(b - a) % 128)))
        return jnp.concatenate([gates, downs], axis=1)

    unit_a, unit_b = [unit_of(a, b) for a, b in chunks]
    full_a = lax.all_gather(after(unit_a, kinds_own), "dp", axis=0, tiled=True)

    segment, positions = segments(lengths[0], group)
    row_blocks = jnp.arange(parts, dtype=jnp.int32) ^ part_index
    row_index = (
        row_blocks[:, None] * local_rows + jnp.arange(local_rows, dtype=jnp.int32)[None, :]
    ).reshape(group)
    segment, positions = [
        jnp.concatenate(
            [
                lax.dynamic_slice_in_dim(array, (part_index ^ r) * local_rows, local_rows, 0)
                for r in range(parts)
            ]
        )
        for array in (segment, positions)
    ]
    cosine, sine = rotary_tables(positions.astype(jnp.float32))
    ones = jnp.ones((group, HD - ROT), jnp.float32)
    blank = jnp.zeros((group, ROT // 2), jnp.float32)
    empty = jnp.zeros((group, HD - ROT), jnp.float32)
    tables = [
        jnp.concatenate([a, b, c] * 2, axis=1)
        for a, b, c in ((cosine, cosine, ones), (-sine, blank, empty), (blank, sine, empty))
    ]
    marks = (jnp.stack([segment, row_index], axis=1), jnp.stack([segment, row_index], axis=0))
    column_start = part_index * head_cols
    rotmask = (jnp.arange(head_cols, dtype=jnp.int32) % HD < ROT).astype(jnp.float32)
    query_bias = lax.dynamic_slice_in_dim(bias_rows[0], column_start, head_cols, 0)
    key_bias = lax.dynamic_slice_in_dim(bias_rows[1], column_start, head_cols, 0) * rotmask
    value_bias = lax.dynamic_slice_in_dim(bias_rows[2], column_start, head_cols, 0)
    offsets = jnp.stack([query_bias, key_bias, value_bias])

    rows_in = tokens.astype(jnp.float32)
    normed, unit_one, factor_one = norm_forward(rows_in, norm_gains[0], bias_rows[3])
    normed_all = gather_rows(normed.astype(bf16), parts)
    cot_all = gather_rows(after(cotangent, normed_all), parts)
    normed_sides = both_cores(after(normed_all, cot_all))
    cot_sides = both_cores(after(cot_all, normed_sides[0]))
    kinds, normed_all, normed_sides, cot_all, cot_sides, tables, marks = together(
        kinds, normed_all, normed_sides, cot_all, cot_sides, tables, marks
    )

    mixed, context, log_totals = attend(normed_all, kinds, offsets, tables, marks)
    branch = dot(context, kinds[3], ((1,), (1,))).astype(bf16)
    branch = scatter_rows(branch, parts)
    middle = rows_in + branch
    second, unit_two, factor_two = norm_forward(middle, norm_gains[1], bias_rows[4])
    second_all = gather_rows(second.astype(bf16), parts)
    second_all, full_a, unit_b = together(second_all, full_a, unit_b)

    way_b = gather_from(([unit_b], [unit_b]), 1, 2, lines)
    natural = jnp.arange(dp_count, dtype=jnp.int32)
    acts, branch_a, second_a = feed(second_all, cot_all, [full_a], natural, size)
    acts, branch_a, second_a, way_b = together(acts, branch_a, second_a, way_b)

    way_b = gather_from(way_b, 2, 3, lines)
    acts_other = other_core(acts)
    second_sides = both_cores(after(second_all, acts))
    padded = acts.shape[1] // 3
    (terms,) = weight_terms(second_sides, cot_sides, (acts, acts_other), padded, 2, lines)
    terms, way_b = together(terms, way_b)

    way_b = gather_from(way_b, 3, lines, lines)
    streams = begin(terms)
    streams, way_b = together_streams(streams, way_b)

    streams = advance(streams)
    half = pack(*way_b, place, lines)
    order = jnp.stack(own_blocks + other_blocks).astype(jnp.int32)
    acts, branch_two, second_grad = feed(
        second_all, cot_all, [half, other_core(half)], order, size, (branch_a, second_a)
    )
    streams, (second_grad, branch_two, acts) = together_streams(
        streams, (second_grad, branch_two, acts)
    )

    streams = advance(streams)
    acts_other = other_core(acts)
    arrived = send_rows(second_grad, parts)
    padded = acts.shape[1] // 3
    (terms,) = weight_terms(second_sides, cot_sides, (acts, acts_other), padded, 2, lines)
    streams, (arrived, terms) = together_streams(streams, (arrived, terms))

    second_grad = add_up(arrived)
    middle_grad = cotangent.astype(jnp.float32) + norm_backward(
        second_grad, unit_two, factor_two, norm_gains[1]
    )
    middle_low = middle_grad.astype(bf16)
    streams, (middle_low, terms) = together_streams(streams, (middle_low, terms))
    middle_all = gather_rows(middle_low, parts)
    streams = advance(streams) + begin(terms)
    gate_params = (gate_weight, gate_first, gate_second)
    down_params = (down_weight, down_first, down_second)
    feed_news = feed_step(chunks[0], parts_of(finish(streams[:1])[0]), gate_params, down_params)
    streams, (middle_all, feed_news, branch_two) = together_streams(
        streams, (middle_all, feed_news, branch_two)
    )

    streams = advance(streams)
    leaving = send_rows(branch_two, parts)
    mixed_grad, normed_terms = attend_back(
        middle_all, kinds, mixed, context, log_totals, tables, marks
    )
    streams, (mixed_grad, normed_terms, middle_all, leaving) = together_streams(
        streams, (mixed_grad, normed_terms, middle_all, leaving)
    )

    arrived = send_rows(normed_terms, parts)
    streams = advance(streams)
    mixed_other = other_core(mixed_grad)
    middle_sides = both_cores(middle_all)
    entry_terms = weight_terms(
        normed_sides, middle_sides, (mixed_grad, mixed_other), head_cols, 3, lines, 2
    )
    streams, (arrived, entry_terms) = together_streams(streams, (arrived, entry_terms))

    early, late = begin(entry_terms[0]), begin(entry_terms[1])
    feed_news = feed_step(chunks[1], parts_of(streams[1]), gate_params, down_params, feed_news)
    early, (arrived, feed_news) = together_streams(early, (arrived, feed_news))
    (
        gate_gradient, gate_updated, gate_first_new, gate_second_new,
        down_gradient, down_updated, down_first_new, down_second_new,
    ) = feed_news

    early = advance(early)
    late, arrived = together_streams(late, arrived)
    late = advance(late)
    normed_grad = add_up(arrived)
    input_gradient = middle_grad + norm_backward(normed_grad, unit_one, factor_one, norm_gains[0])
    gain_two_grad = jnp.sum(second_grad * unit_two, axis=0)
    shift_two_grad = jnp.sum(second_grad, axis=0)
    gain_one_grad = jnp.sum(normed_grad * unit_one, axis=0)
    shift_one_grad = jnp.sum(normed_grad, axis=0)
    column_sums = jnp.sum(mixed_grad[:, : 3 * head_cols].astype(jnp.float32), axis=0).reshape(3, head_cols)
    column_sums = column_sums * jnp.stack([jnp.ones_like(rotmask), rotmask, jnp.ones_like(rotmask)])
    placed = lax.dynamic_update_slice_in_dim(
        jnp.zeros((3, width), jnp.float32), column_sums, column_start, 1
    )
    norms_local = jnp.stack([shift_one_grad, shift_two_grad, gain_one_grad, gain_two_grad])
    vectors = jnp.concatenate([placed, norms_local], axis=0)
    hops = [
        (axis, 1 << power)
        for axis, count in (("tensor", parts), ("dp", dp_count))
        for power in range(count.bit_length() - 1)
    ]
    vectors = hop(vectors, *hops[0])
    early, vectors = together_streams(early, vectors)

    early = advance(early)
    for which in hops[1:3]:
        vectors = hop(vectors, *which)
    late, vectors = together_streams(late, vectors)

    late = advance(late)
    vectors = hop(vectors, *hops[3])
    early = finish(early)
    early, (vectors, leaving) = together_streams(early, (vectors, leaving))
    output_rows = (middle + add_up(leaving)).astype(bf16)

    for which in hops[4:]:
        vectors = hop(vectors, *which)
    kind_first = lambda array: jnp.swapaxes(array, 0, 1)
    entry_params = [kind_first(array) for array in (entry_weight, entry_first, entry_second)]
    entry_news = plain_step(0, parts_of(early[0]), entry_params, (0, 1))
    late = finish(late)
    late, entry_news = together_streams(late, entry_news)
    bias_gradient = vectors[:5]
    gains_gradient = vectors[5:]
    entry_gradient, entry_updated, entry_first_new, entry_second_new = [
        kind_first(array) for array in plain_step(0, parts_of(late[0]), entry_params, (2,), entry_news)
    ]
    exit_gradient, exit_updated, exit_first_new, exit_second_new = [
        array[0]
        for array in plain_step(
            1, parts_of(late[0]), [array[None] for array in (exit_weight, exit_first, exit_second)], (0,)
        )
    ]
    bias_updated, bias_first_new, bias_second_new = adamw(
        bias_rows, bias_first, bias_second, bias_gradient, vector_rate, 0.0
    )
    gains_updated, gains_first_new, gains_second_new = adamw(
        norm_gains, gains_first, gains_second, gains_gradient, vector_rate, 0.0
    )
    return (
        output_rows,
        input_gradient,
        entry_gradient,
        entry_updated,
        entry_first_new,
        entry_second_new,
        exit_gradient,
        exit_updated,
        exit_first_new,
        exit_second_new,
        gate_gradient,
        gate_updated,
        gate_first_new,
        gate_second_new,
        down_gradient,
        down_updated,
        down_first_new,
        down_second_new,
        bias_gradient,
        bias_updated,
        bias_first_new,
        bias_second_new,
        gains_gradient,
        gains_updated,
        gains_first_new,
        gains_second_new,
    )


def solution(mesh):
    return jax.shard_map(
        on_device,
        mesh=mesh,
        in_specs=(
            P(("dp", "tensor"), None),
            P(("dp", "tensor"), None),
            P("dp", None),
            P("dp", None, "tensor"),
            P("dp", None, "tensor"),
            P("dp", None, "tensor"),
            P("dp", "tensor"),
            P("dp", "tensor"),
            P("dp", "tensor"),
            P("dp", None, "tensor"),
            P("dp", None, "tensor"),
            P("dp", None, "tensor"),
            P("dp", "tensor"),
            P("dp", "tensor"),
            P("dp", "tensor"),
            P(),
            P(),
            P(),
            P(),
            P(),
            P(),
        ),
        out_specs=(
            P(("dp", "tensor"), None),
            P(("dp", "tensor"), None),
            P("dp", None, "tensor"),
            P("dp", None, "tensor"),
            P("dp", None, "tensor"),
            P("dp", None, "tensor"),
            P("dp", "tensor"),
            P("dp", "tensor"),
            P("dp", "tensor"),
            P("dp", "tensor"),
            P("dp", None, "tensor"),
            P("dp", None, "tensor"),
            P("dp", None, "tensor"),
            P("dp", None, "tensor"),
            P("dp", "tensor"),
            P("dp", "tensor"),
            P("dp", "tensor"),
            P("dp", "tensor"),
            P(),
            P(),
            P(),
            P(),
            P(),
            P(),
            P(),
            P(),
        ),
        check_vma=False,
    )
```

```python
import jax
import jax.numpy as jnp
from jax import lax
from jax.experimental import pallas as pl
from jax.experimental.pallas import tpu as pltpu
from jax.sharding import PartitionSpec as P

HD = 64
ROT = 16
STEP = 3


norm_eps = 1e-05
rope_base = 10000.0
masked_score = -1e30
beta_one = 0.9
beta_two = 0.95
adam_eps = 1e-08
matrix_rate = 0.08
vector_rate = 0.4
weight_decay = 0.1


def norm_forward(rows, gain, shift):
    centre = jnp.mean(rows, axis=-1, keepdims=True)
    centred = rows - centre
    spread = jnp.mean(centred * centred, axis=-1, keepdims=True)
    factor = lax.rsqrt(spread + norm_eps)
    unit = centred * factor
    return (unit * gain + shift, unit, factor)


def norm_backward(incoming, unit, factor, gain):
    scaled = incoming * gain
    mean_plain = jnp.mean(scaled, axis=-1, keepdims=True)
    mean_along = jnp.mean(scaled * unit, axis=-1, keepdims=True)
    return factor * (scaled - mean_plain - unit * mean_along)


def segments(lengths_row, count):
    ends = jnp.cumsum(lengths_row)
    index = jnp.arange(count, dtype=jnp.int32)
    after = index[:, None] >= ends[None, :]
    segment = jnp.sum(after.astype(jnp.int32), axis=1)
    begin = jnp.max(jnp.where(after, ends[None, :], jnp.zeros_like(ends)[None, :]), axis=1)
    return (segment, index - begin)


def rotary_tables(positions):
    half = ROT // 2
    freqs = rope_base ** (-2.0 * jnp.arange(half, dtype=jnp.float32) / ROT)
    angles = positions[:, None] * freqs[None, :]
    return (jnp.cos(angles), jnp.sin(angles))


def adamw(weight, first, second, gradient, rate, decay):
    first_new = beta_one * first + (1.0 - beta_one) * gradient
    second_new = beta_two * second + (1.0 - beta_two) * gradient * gradient
    first_hat = first_new / (1.0 - beta_one**STEP)
    second_hat = second_new / (1.0 - beta_two**STEP)
    updated = weight - rate * (first_hat / (jnp.sqrt(second_hat) + adam_eps) + decay * weight)
    return (updated, first_new, second_new)


def together(*groups):
    flat, tree = jax.tree.flatten(groups)
    return jax.tree.unflatten(tree, lax.optimization_barrier(flat))


def after(value, *earlier):
    return lax.optimization_barrier((value,) + tuple(earlier))[0]


def pairs_up(lines, low, high, step):
    return [(z * 2 + c, (z + step) * 2 + c) for z in range(low, high) for c in range(2)]


def other_core(array):
    count = lax.axis_size("dp")
    return lax.ppermute(array, "dp", [(d, d ^ 1) for d in range(count)])


def gather_step(ups, downs, s, lines):
    up = lax.ppermute(ups[-1], "dp", pairs_up(lines, s - 1, lines - 1, 1))
    down = lax.ppermute(downs[-1], "dp", pairs_up(lines, 1, lines - s + 1, -1))
    return ups + [up], downs + [down]


def gather_from(way, low, high, lines):
    for s in range(low, high):
        way = gather_step(*way, s, lines)
    return way


def pack_kernel(lines, place_ref, *refs):
    pieces, out = refs[:-1], refs[-1]
    place = place_ref[0]
    s = pl.program_id(0)
    for at in range(lines):

        @pl.when((s == at) & (place >= at))
        def _():
            out[...] = pieces[at][...]

        if at > 0:

            @pl.when((s == at) & (place < at))
            def _():
                out[...] = pieces[2 * lines - 1 - at][...]


def pack(ups, downs, place, lines):
    rows, columns = ups[0].shape
    tile = min(128, rows)
    tiles = rows // tile

    def spec(at, is_up):
        def index(s, t, place_ref):
            wanted = (s == at) & ((place_ref[0] >= at) if is_up else (place_ref[0] < at))
            return (jnp.where(wanted, t, jnp.where(s > at, tiles - 1, 0)), 0)

        return pl.BlockSpec((tile, columns), index)

    return pl.pallas_call(
        lambda *refs: pack_kernel(lines, *refs),
        grid_spec=pltpu.PrefetchScalarGridSpec(
            num_scalar_prefetch=1,
            grid=(lines, tiles),
            in_specs=[spec(at, True) for at in range(lines)]
            + [spec(lines - at, False) for at in range(1, lines)],
            out_specs=pl.BlockSpec((tile, columns), lambda s, t, place_ref: (s * tiles + t, 0)),
        ),
        out_shape=jax.ShapeDtypeStruct((lines * rows, columns), ups[0].dtype),
        compiler_params=pltpu.CompilerParams(vmem_limit_bytes=40 * 1024 * 1024),
        cost_estimate=pl.CostEstimate(
            flops=0, bytes_accessed=4 * lines * rows * columns, transcendentals=0
        ),
        name="pack_blocks",
    )(place.reshape(1).astype(jnp.int32), *ups, *downs[1:])


def scatter_step(blocks, up, down, j, lines):
    up_send = blocks[lines - j] if up is None else blocks[lines - j] + up
    down_send = blocks[j] if down is None else blocks[j] + down
    up = lax.ppermute(up_send, "dp", pairs_up(lines, 0, lines - j, 1))
    down = lax.ppermute(down_send, "dp", pairs_up(lines, j, lines, -1))
    return up, down


def swap_rows(array, offset):
    count = lax.axis_size("tensor")
    return lax.ppermute(array, "tensor", [(t, t ^ offset) for t in range(count)])


def gather_rows(own, parts):
    return jnp.concatenate([own] + [swap_rows(own, r) for r in range(1, parts)], axis=0)


def send_rows(partial, parts):
    rows = partial.shape[0] // parts
    blocks = [partial[r * rows : (r + 1) * rows] for r in range(parts)]
    return [blocks[0]] + [swap_rows(blocks[r], r) for r in range(1, parts)]


def add_up(terms):
    total = terms[0].astype(jnp.float32)
    for term in terms[1:]:
        total = total + term.astype(jnp.float32)
    return total


def scatter_rows(partial, parts):
    return add_up(send_rows(partial, parts))


def together_streams(streams, others):
    ways, blocks, others = together(
        [way for _, way, _ in streams], [blocks for blocks, _, _ in streams], others
    )
    return [(b, w, left) for b, w, (_, _, left) in zip(blocks, ways, streams)], others


def hop(array, axis, bit):
    count = lax.axis_size(axis)
    return array + lax.ppermute(array, axis, [(i, i ^ bit) for i in range(count)])


def cuts(columns):
    first = min(columns, 128 * -(-(-(-columns // 128) * 5) // 11))
    return [(0, first), (first, columns)]


def paired(array):
    rows, kinds, columns = array.shape
    array = jnp.pad(array, ((0, 0), (0, 0), (0, -columns % 128)))
    return jnp.swapaxes(array.reshape(rows, kinds, -1, 128), 1, 2)


def dot(a, b, contract):
    return lax.dot_general(a, b, (contract, ((), ())), preferred_element_type=jnp.float32)


def whole(shape):
    return pl.BlockSpec(shape, lambda *_: (0,) * len(shape))


def kernel_call(kernel, grid, in_specs, out_specs, out_shape, scratch, name, flops=1, moved=1):
    return pl.pallas_call(
        kernel,
        grid=grid,
        in_specs=in_specs,
        out_specs=out_specs,
        out_shape=out_shape,
        scratch_shapes=scratch,
        compiler_params=pltpu.CompilerParams(vmem_limit_bytes=56 * 1024 * 1024),
        cost_estimate=pl.CostEstimate(flops=flops, bytes_accessed=moved, transcendentals=0),
        name=name,
    )


def turn(x, keep, low, high, direction):
    return (
        x * keep
        + pltpu.roll(x, 120, 1) * (low * direction)
        + pltpu.roll(x, 8, 1) * (high * direction)
    )


def row_steps(rows):
    return 128 if rows % 128 == 0 else rows


def fill_bias(bias_ref, column_ref, row_ref):
    rows = bias_ref.shape[0]
    step = row_steps(rows)

    def body(r, _):
        at = pl.ds(pl.multiple_of(r * step, step), step)
        marks = column_ref[at, :]
        visible = (marks[:, 0:1] == row_ref[0:1, :]) & (marks[:, 1:2] >= row_ref[1:2, :])
        bias_ref[at, :] = jnp.where(visible, 0.0, masked_score)
        return 0

    lax.fori_loop(0, rows // step, body, 0)


def matmul(a, b, contract=((1,), (0,))):
    return lax.dot_general(a, b, (contract, ((), ())), preferred_element_type=jnp.float32)


def attend_kernel(
    normed_ref, weight_ref, offset_ref, keep_ref, low_ref, high_ref, column_ref, row_ref,
    mixed_ref, context_ref, totals_ref, bias_ref, score_ref, prob_ref,
):
    kind = pl.program_id(0)
    rows, columns = context_ref.shape
    step = row_steps(rows)
    raw = matmul(normed_ref[...], weight_ref[0]) + offset_ref[0]
    here = pl.multiple_of(kind * columns, 128)

    @pl.when(kind < 2)
    def _():
        for b in range(columns // 128):
            block = turn(raw[:, b * 128 : (b + 1) * 128], keep_ref[...], low_ref[...], high_ref[...], 1.0)
            mixed_ref[:, pl.ds(pl.multiple_of(here + b * 128, 128), 128)] = block.astype(jnp.bfloat16)

    @pl.when(kind == 2)
    def _():
        mixed_ref[:, pl.ds(here, columns)] = raw.astype(jnp.bfloat16)
        fill_bias(bias_ref, column_ref, row_ref)
        lane = lax.broadcasted_iota(jnp.int32, (1, 128), 1)

        def pair_body(pair, _):
            first = pl.multiple_of(pair * 128, 128)
            queries = mixed_ref[:, pl.ds(first, 128)]
            keys = mixed_ref[:, pl.ds(pl.multiple_of(columns + first, 128), 128)]
            values = mixed_ref[:, pl.ds(pl.multiple_of(2 * columns + first, 128), 128)]
            parts = []
            for h in range(2):
                mine = (lane >= HD * h) & (lane < HD * (h + 1))
                score_ref[...] = matmul(
                    jnp.where(mine, queries, jnp.zeros_like(queries)), keys, ((1,), (1,))
                )

                def rows_body(r, _):
                    at = pl.ds(pl.multiple_of(r * step, step), step)
                    scores = score_ref[at, :] * (HD**-0.5) + bias_ref[at, :]
                    summit = jnp.max(scores, axis=1, keepdims=True)
                    weights = jnp.exp(scores - summit)
                    total = jnp.sum(weights, axis=1, keepdims=True)
                    prob_ref[at, :] = (weights * (1.0 / total)).astype(jnp.bfloat16)
                    spot = lane == pair * 2 + h
                    totals_ref[at, :] = jnp.where(
                        spot, summit + jnp.log(total), totals_ref[at, :]
                    )
                    return 0

                lax.fori_loop(0, rows // step, rows_body, 0, unroll=True)
                parts.append(matmul(prob_ref[...], values))
            both = jnp.where(lane < HD, parts[0], parts[1])
            context_ref[:, pl.ds(first, 128)] = both.astype(jnp.bfloat16)
            return 0

        totals_ref[...] = jnp.zeros_like(totals_ref)
        lax.fori_loop(0, columns // 128, pair_body, 0)


def attend(normed_all, entry_full, offsets, tables, marks):
    rows, width = normed_all.shape
    columns = entry_full.shape[2]
    bf16, f32 = jnp.bfloat16, jnp.float32
    return kernel_call(
        attend_kernel,
        (3,),
        [whole((rows, width)), pl.BlockSpec((1, width, columns), lambda k: (k, 0, 0)),
         pl.BlockSpec((1, 1, columns), lambda k: (k, 0, 0))]
        + [whole((rows, 128))] * 3 + [whole((rows, 2)), whole((2, rows))],
        [whole((rows, 3 * columns)), whole((rows, columns)), whole((rows, 128))],
        [jax.ShapeDtypeStruct((rows, 3 * columns), bf16), jax.ShapeDtypeStruct((rows, columns), bf16),
         jax.ShapeDtypeStruct((rows, 128), f32)],
        [pltpu.VMEM((rows, rows), f32), pltpu.VMEM((rows, rows), f32), pltpu.VMEM((rows, rows), bf16)],
        "attention",
        24 * rows * width * columns,
        8 * rows * width,
    )(normed_all, entry_full, offsets.reshape(3, 1, columns), *tables, *marks)


def attend_back_kernel(
    middle_ref, exit_ref, mixed_ref, context_ref, totals_ref, keep_ref, low_ref, high_ref, column_ref,
    row_ref, kinds_ref, grad_ref, normed_ref, bias_ref, score_ref, prob_grad_ref, prob_ref,
    score_grad_ref, context_grad_ref, weight_ref, sem,
):
    rows = middle_ref.shape[0]
    columns = exit_ref.shape[2]
    step = row_steps(rows)
    load = pltpu.make_async_copy(kinds_ref.at[pl.ds(0, 3)], weight_ref, sem)
    load.start()
    grad_ref[:, 3 * columns :] = context_ref[...]
    context_grad_ref[...] = matmul(middle_ref[...], exit_ref[0]).astype(jnp.bfloat16)
    fill_bias(bias_ref, column_ref, row_ref)
    lane = lax.broadcasted_iota(jnp.int32, (1, 128), 1)

    def pair_body(pair, _):
        first = pl.multiple_of(pair * 128, 128)
        second = pl.multiple_of(columns + first, 128)
        third = pl.multiple_of(2 * columns + first, 128)
        queries = mixed_ref[:, pl.ds(first, 128)]
        keys = mixed_ref[:, pl.ds(second, 128)]
        values = mixed_ref[:, pl.ds(third, 128)]
        incoming = context_grad_ref[:, pl.ds(first, 128)]
        query_parts, key_parts, value_parts = [], [], []
        for h in range(2):
            mine = (lane >= HD * h) & (lane < HD * (h + 1))
            score_ref[...] = matmul(
                jnp.where(mine, queries, jnp.zeros_like(queries)), keys, ((1,), (1,))
            )
            prob_grad_ref[...] = matmul(
                jnp.where(mine, incoming, jnp.zeros_like(incoming)), values, ((1,), (1,))
            )

            def rows_body(r, _):
                at = pl.ds(pl.multiple_of(r * step, step), step)
                spot = lane == pair * 2 + h
                total = jnp.sum(jnp.where(spot, totals_ref[at, :], 0.0), axis=1, keepdims=True)
                probs = jnp.exp(score_ref[at, :] * (HD**-0.5) + bias_ref[at, :] - total)
                prob_grad = prob_grad_ref[at, :]
                inner = jnp.sum(probs * prob_grad, axis=1, keepdims=True)
                score_grad_ref[at, :] = (probs * (prob_grad - inner)).astype(jnp.bfloat16)
                prob_ref[at, :] = probs.astype(jnp.bfloat16)
                return 0

            lax.fori_loop(0, rows // step, rows_body, 0, unroll=True)
            query_parts.append(matmul(score_grad_ref[...], keys))
            key_parts.append(matmul(score_grad_ref[...], queries, ((0,), (0,))))
            value_parts.append(matmul(prob_ref[...], incoming, ((0,), (0,))))
        keep, low, high = keep_ref[...], low_ref[...], high_ref[...]
        scale = HD**-0.5
        query_grad = jnp.where(lane < HD, query_parts[0], query_parts[1]) * scale
        key_grad = jnp.where(lane < HD, key_parts[0], key_parts[1]) * scale
        value_grad = jnp.where(lane < HD, value_parts[0], value_parts[1])
        grad_ref[:, pl.ds(first, 128)] = turn(query_grad, keep, low, high, -1.0).astype(jnp.bfloat16)
        grad_ref[:, pl.ds(second, 128)] = turn(key_grad, keep, low, high, -1.0).astype(jnp.bfloat16)
        grad_ref[:, pl.ds(third, 128)] = value_grad.astype(jnp.bfloat16)
        return 0

    lax.fori_loop(0, columns // 128, pair_body, 0)
    load.wait()
    width = normed_ref.shape[1]
    for low in range(0, width, 512):
        here = slice(low, min(low + 512, width))
        total = None
        for k in range(3):
            term = matmul(
                grad_ref[:, k * columns : (k + 1) * columns], weight_ref[k, here, :], ((1,), (1,))
            )
            total = term if total is None else total + term
        normed_ref[:, here] = total.astype(jnp.bfloat16)


def attend_back(middle_all, exit_full, mixed, context, totals, tables, marks):
    rows, width = middle_all.shape
    columns = exit_full.shape[2]
    bf16, f32 = jnp.bfloat16, jnp.float32
    square = (rows, rows)
    return kernel_call(
        attend_back_kernel,
        (1,),
        [whole((rows, width)), pl.BlockSpec((1, width, columns), lambda *_: (3, 0, 0)),
         whole((rows, 3 * columns)), whole((rows, columns)), whole((rows, 128))]
        + [whole((rows, 128))] * 3 + [whole((rows, 2)), whole((2, rows))]
        + [pl.BlockSpec(memory_space=pl.ANY)],
        [whole((rows, 4 * columns)), whole((rows, width))],
        [jax.ShapeDtypeStruct((rows, 4 * columns), bf16), jax.ShapeDtypeStruct((rows, width), bf16)],
        [pltpu.VMEM(square, f32), pltpu.VMEM(square, f32), pltpu.VMEM(square, f32),
         pltpu.VMEM(square, bf16), pltpu.VMEM(square, bf16), pltpu.VMEM((rows, columns), bf16),
         pltpu.VMEM((3, width, columns), bf16), pltpu.SemaphoreType.DMA],
        "attention_back",
        24 * rows * width * columns,
        8 * rows * width,
    )(middle_all, exit_full, mixed, context, totals, *tables, *marks, exit_full)


def feed_kernel(pieces, order_ref, second_in, cot_in, *refs):
    fulls, refs = refs[:pieces], refs[pieces:]
    earlier, refs = (refs[:2], refs[2:]) if pieces > 1 else ((), refs)
    acts_ref, branch_ref, second_grad_ref, weight_ref, hidden_grad_ref, sems = refs[:6]
    j = pl.program_id(0)
    rows, width = second_in.shape
    padded = acts_ref.shape[1] // 3
    pairs = padded // 128
    size = branch_ref.shape[1]
    height = width // pieces
    bf16 = jnp.bfloat16
    second_ref, cot_ref = (second_in, cot_in) if pieces == 1 else refs[6:]

    def loads(at, columns, which):
        here = pl.ds(at, columns)
        return [
            pltpu.make_async_copy(
                full.at[:, here], weight_ref.at[pl.ds(p * height, height), here], sems.at[p, which]
            )
            for p, full in enumerate(fulls)
        ]

    @pl.when(j == 0)
    def _():
        for load in loads(2 * padded, padded, 0):
            load.start()
        for p in range(pairs):
            for load in loads(p * 256, 256, p + 1):
                load.start()
        if pieces > 1:
            for b in range(width // size):
                there = pl.ds(pl.multiple_of(order_ref[b] * size, size), size)
                second_ref[:, b * size : (b + 1) * size] = second_in[:, there]
                cot_ref[:, b * size : (b + 1) * size] = cot_in[:, there]
        for load in loads(2 * padded, padded, 0):
            load.wait()
        for low in range(0, padded, 256):
            high = min(low + 256, padded)
            hidden_grad_ref[:, low:high] = matmul(
                cot_ref[...], weight_ref[:, 2 * padded + low : 2 * padded + high]
            )
        for p in range(pairs):
            for load in loads(p * 256, 256, p + 1):
                load.wait()
            gate_up = matmul(second_ref[...], weight_ref[:, p * 256 : (p + 1) * 256])
            gate, upper = gate_up[:, :128], gate_up[:, 128:]
            grad = hidden_grad_ref[:, p * 128 : (p + 1) * 128]
            sigmoid = jax.nn.sigmoid(gate)
            activated = gate * sigmoid
            acts_ref[:, p * 256 : p * 256 + 128] = (
                grad * upper * sigmoid * (1.0 + gate * (1.0 - sigmoid))
            ).astype(bf16)
            acts_ref[:, p * 256 + 128 : (p + 1) * 256] = (grad * activated).astype(bf16)
            hidden = 2 * padded + p * 128
            acts_ref[:, hidden : hidden + 128] = (activated * upper).astype(bf16)

    @pl.when(j > 0)
    def _():
        here = pl.ds(pl.multiple_of((j - 1) * size, size), size)
        over = ((1,), (1,))
        branch = matmul(acts_ref[:, 2 * padded :], weight_ref[here, 2 * padded :], over)
        second_grad = matmul(acts_ref[:, : 2 * padded], weight_ref[here, : 2 * padded], over)
        if pieces > 1:
            branch = branch + earlier[0][...].astype(jnp.float32)
            second_grad = second_grad + earlier[1][...].astype(jnp.float32)
        branch_ref[...] = branch.astype(bf16)
        second_grad_ref[...] = second_grad.astype(bf16)


def feed(second_all, cot_all, fulls, order, size, earlier=()):
    rows, width = second_all.shape
    padded = fulls[0].shape[1] // 3
    pieces = len(fulls)
    bf16, f32 = jnp.bfloat16, jnp.float32
    full = pl.BlockSpec((rows, width), lambda j, order_ref: (0, 0))
    out = pl.BlockSpec((rows, size), lambda j, order_ref: (0, order_ref[jnp.maximum(j - 1, 0)]))
    scratch = [
        pltpu.VMEM((width, 3 * padded), bf16), pltpu.VMEM((rows, padded), f32),
        pltpu.SemaphoreType.DMA((pieces, 1 + padded // 128)),
    ]
    if pieces > 1:
        scratch += [pltpu.VMEM((rows, width), bf16)] * 2
    return pl.pallas_call(
        lambda *refs: feed_kernel(pieces, *refs),
        grid_spec=pltpu.PrefetchScalarGridSpec(
            num_scalar_prefetch=1,
            grid=(1 + width // size,),
            in_specs=[full] * 2 + [pl.BlockSpec(memory_space=pl.ANY)] * pieces + [out] * len(earlier),
            out_specs=[pl.BlockSpec((rows, 3 * padded), lambda j, order_ref: (0, 0)), out, out],
            scratch_shapes=scratch,
        ),
        out_shape=[jax.ShapeDtypeStruct((rows, 3 * padded), bf16)]
        + [jax.ShapeDtypeStruct((rows, width), bf16)] * 2,
        compiler_params=pltpu.CompilerParams(vmem_limit_bytes=56 * 1024 * 1024),
        cost_estimate=pl.CostEstimate(
            flops=24 * rows * width * padded,
            bytes_accessed=12 * width * padded + 16 * rows * width,
            transcendentals=0,
        ),
        name="feed_forward",
    )(order, second_all, cot_all, *fulls, *earlier)


def turned_kernel(blocks_ref, rows_ref, out_ref):
    out_ref[...] = rows_ref[...].T


def turned_blocks(array, blocks, size):
    rows = array.shape[0]
    return pl.pallas_call(
        turned_kernel,
        grid_spec=pltpu.PrefetchScalarGridSpec(
            num_scalar_prefetch=1,
            grid=(len(blocks),),
            in_specs=[pl.BlockSpec((rows, size), lambda b, blocks_ref: (0, blocks_ref[b]))],
            out_specs=pl.BlockSpec((size, rows), lambda b, blocks_ref: (b, 0)),
        ),
        out_shape=jax.ShapeDtypeStruct((len(blocks) * size, rows), array.dtype),
        compiler_params=pltpu.CompilerParams(vmem_limit_bytes=32 * 1024 * 1024),
        cost_estimate=pl.CostEstimate(flops=1, bytes_accessed=1, transcendentals=0),
        name="turned_blocks",
    )(jnp.stack(blocks).astype(jnp.int32), array)


def terms_kernel(split, groups, own_left, other_left, own_last, other_last, own_ref, other_ref, *outs):
    k = pl.program_id(0)
    lines = len(outs) // groups
    per_group = pl.num_programs(0) // groups

    def write(own, other):
        total = (matmul(own[...], own_ref[...]) + matmul(other[...], other_ref[...])).astype(jnp.bfloat16)
        size = outs[0].shape[0]
        for g in range(groups):

            @pl.when(k // per_group == g)
            def _():
                for s, out in enumerate(outs[g * lines : (g + 1) * lines]):
                    out[...] = total[s * size : (s + 1) * size]

    @pl.when(k < split)
    def _():
        write(own_left, other_left)

    @pl.when(k >= split)
    def _():
        write(own_last, other_last)


def weight_terms(left, left_last, right, tile, split, lines, groups=1):
    count, rows = left[0].shape
    columns = right[0].shape[1]
    size = count // lines
    per_group = columns // tile // groups
    left_spec = whole((count, rows))
    right_spec = pl.BlockSpec((rows, tile), lambda k: (0, k))

    def out_spec(g):
        return pl.BlockSpec((size, tile), lambda k: (0, jnp.clip(k - g * per_group, 0, per_group - 1)))

    outs = kernel_call(
        lambda *refs: terms_kernel(split, groups, *refs),
        (columns // tile,),
        [left_spec] * 4 + [right_spec] * 2,
        [out_spec(g) for g in range(groups) for _ in range(lines)],
        [jax.ShapeDtypeStruct((size, columns // groups), jnp.bfloat16)] * (lines * groups),
        [],
        "weight_terms",
        4 * count * rows * columns,
        2 * (4 * count * rows + 2 * rows * columns + count * columns),
    )(*left, *left_last, *right)
    return [list(outs[g * lines : (g + 1) * lines]) for g in range(groups)]


def summed(refs, rows, columns):
    own, up, down = [ref[rows, columns].astype(jnp.float32) for ref in refs]
    return own + up + down


def plain_step_kernel(own, up, down, weight, first, second, *outs):
    outs = outs[-4:]
    everything = slice(None)
    gradient = summed((own, up, down), everything, everything)
    news = adamw(weight[0], first[0], second[0], gradient, matrix_rate, weight_decay)
    for out, value in zip(outs, (gradient,) + tuple(news)):
        out[0] = value


def plain_step(start, parts_of_sum, params, kinds, earlier=()):
    count, rows, columns = params[0].shape
    tile = rows // 2
    part = pl.BlockSpec((tile, columns), lambda k, r: (r, start + k))
    block = pl.BlockSpec((1, tile, columns), lambda k, r: (kinds[0] + k, r, 0))
    return pl.pallas_call(
        plain_step_kernel,
        grid=(len(kinds), 2),
        in_specs=[part] * 3 + [block] * 3 + [pl.BlockSpec(memory_space=pl.ANY)] * len(earlier),
        out_specs=[block] * 4,
        out_shape=[jax.ShapeDtypeStruct((count, rows, columns), jnp.float32)] * 4,
        input_output_aliases={6 + i: i for i in range(len(earlier))},
        compiler_params=pltpu.CompilerParams(vmem_limit_bytes=56 * 1024 * 1024),
        cost_estimate=pl.CostEstimate(flops=1, bytes_accessed=1, transcendentals=0),
        name="plain_step",
    )(*parts_of_sum, *params, *earlier)


def feed_step_kernel(*refs):
    pairs, singles, gate, down = refs[:3], refs[3:6], refs[6:9], refs[9:12]
    gate_outs, down_outs = refs[-8:-4], refs[-4:]
    everything = slice(None)
    for k in range(2):
        gradient = summed(pairs, everything, slice(128 * k, 128 * k + 128))
        news = adamw(*[ref[:, k, :] for ref in gate], gradient, matrix_rate, weight_decay)
        for out, value in zip(gate_outs, (gradient,) + tuple(news)):
            out[:, k, :] = value
    gradient = summed(singles, everything, everything)
    news = adamw(*[ref[...] for ref in down], gradient, matrix_rate, weight_decay)
    for out, value in zip(down_outs, (gradient,) + tuple(news)):
        out[...] = value


def feed_step(run, parts_of_sum, gate, down, earlier=()):
    rows, columns = down[0].shape
    low, high = run
    blocks = -(-(high - low) // 128)
    gate_block = pl.BlockSpec((rows, 2, 128), lambda c: (0, 0, low // 128 + c))
    down_block = pl.BlockSpec((rows, 128), lambda c: (0, low // 128 + c))
    pair = pl.BlockSpec((rows, 256), lambda c: (0, c))
    single = pl.BlockSpec((rows, 128), lambda c: (0, 2 * blocks + c))
    return pl.pallas_call(
        feed_step_kernel,
        grid=(blocks,),
        in_specs=[pair] * 3 + [single] * 3 + [gate_block] * 3 + [down_block] * 3
        + [pl.BlockSpec(memory_space=pl.ANY)] * len(earlier),
        out_specs=[gate_block] * 4 + [down_block] * 4,
        out_shape=[jax.ShapeDtypeStruct((rows, 2, columns), jnp.float32)] * 4
        + [jax.ShapeDtypeStruct((rows, columns), jnp.float32)] * 4,
        input_output_aliases={12 + i: i for i in range(len(earlier))},
        compiler_params=pltpu.CompilerParams(vmem_limit_bytes=56 * 1024 * 1024),
        cost_estimate=pl.CostEstimate(
            flops=0, bytes_accessed=84 * rows * (high - low), transcendentals=0
        ),
        name="feed_step",
    )(*parts_of_sum, *parts_of_sum, *gate, *down, *earlier)


def on_device(
    tokens,
    cotangent,
    lengths,
    entry_weight,
    entry_first,
    entry_second,
    exit_weight,
    exit_first,
    exit_second,
    gate_weight,
    gate_first,
    gate_second,
    down_weight,
    down_first,
    down_second,
    bias_rows,
    bias_first,
    bias_second,
    norm_gains,
    gains_first,
    gains_second,
):
    parts = lax.axis_size("tensor")
    part_index = lax.axis_index("tensor")
    dp_index = lax.axis_index("dp")
    dp_count = lax.axis_size("dp")
    lines = dp_count // 2
    last = lines - 1
    place = dp_index // 2
    core = dp_index % 2
    local_rows = tokens.shape[0]
    group = local_rows * parts
    width = tokens.shape[1]
    size = width // dp_count
    head_cols = entry_weight.shape[2]
    hidden_cols = down_weight.shape[1]
    bf16 = jnp.bfloat16
    own_blocks = [((place - s + lines) % lines) * 2 + core for s in range(lines)]
    other_blocks = [((place - s + lines) % lines) * 2 + 1 - core for s in range(lines)]
    none = (None, None)

    def advance(streams):
        return [
            (blocks, scatter_step(blocks, *way, left, lines), left - 1) if left > 0 else stream
            for stream in streams
            for blocks, way, left in [stream]
        ]

    def begin(blocks):
        return advance([(blocks, none, last)])

    def finish(streams):
        while any(left > 0 for _, _, left in streams):
            streams = advance(streams)
        return streams

    def parts_of(stream):
        blocks, way, _ = stream
        return (blocks[0],) + tuple(way)

    def both_cores(array):
        both = turned_blocks(array, own_blocks + other_blocks, size)
        return both[: width // 2], other_core(both[width // 2 :])

    kinds_own = jnp.concatenate(
        [jnp.swapaxes(entry_weight, 0, 1).astype(bf16), exit_weight.astype(bf16)[None]], axis=0
    )
    kinds = lax.all_gather(kinds_own, "dp", axis=1, tiled=True)
    chunks = cuts(hidden_cols)

    def unit_of(a, b):
        gates = paired(gate_weight[:, :, a:b].astype(bf16)).reshape(size, -1)
        downs = jnp.pad(down_weight[:, a:b].astype(bf16), ((0, 0), (0, -(b - a) % 128)))
        return jnp.concatenate([gates, downs], axis=1)

    unit_a, unit_b = [unit_of(a, b) for a, b in chunks]
    full_a = lax.all_gather(after(unit_a, kinds_own), "dp", axis=0, tiled=True)

    segment, positions = segments(lengths[0], group)
    row_blocks = jnp.arange(parts, dtype=jnp.int32) ^ part_index
    row_index = (
        row_blocks[:, None] * local_rows + jnp.arange(local_rows, dtype=jnp.int32)[None, :]
    ).reshape(group)
    segment, positions = [
        jnp.concatenate(
            [
                lax.dynamic_slice_in_dim(array, (part_index ^ r) * local_rows, local_rows, 0)
                for r in range(parts)
            ]
        )
        for array in (segment, positions)
    ]
    cosine, sine = rotary_tables(positions.astype(jnp.float32))
    ones = jnp.ones((group, HD - ROT), jnp.float32)
    blank = jnp.zeros((group, ROT // 2), jnp.float32)
    empty = jnp.zeros((group, HD - ROT), jnp.float32)
    tables = [
        jnp.concatenate([a, b, c] * 2, axis=1)
        for a, b, c in ((cosine, cosine, ones), (-sine, blank, empty), (blank, sine, empty))
    ]
    marks = (jnp.stack([segment, row_index], axis=1), jnp.stack([segment, row_index], axis=0))
    column_start = part_index * head_cols
    rotmask = (jnp.arange(head_cols, dtype=jnp.int32) % HD < ROT).astype(jnp.float32)
    query_bias = lax.dynamic_slice_in_dim(bias_rows[0], column_start, head_cols, 0)
    key_bias = lax.dynamic_slice_in_dim(bias_rows[1], column_start, head_cols, 0) * rotmask
    value_bias = lax.dynamic_slice_in_dim(bias_rows[2], column_start, head_cols, 0)
    offsets = jnp.stack([query_bias, key_bias, value_bias])

    rows_in = tokens.astype(jnp.float32)
    normed, unit_one, factor_one = norm_forward(rows_in, norm_gains[0], bias_rows[3])
    normed_all = gather_rows(normed.astype(bf16), parts)
    cot_all = gather_rows(after(cotangent, normed_all), parts)
    normed_sides = both_cores(after(normed_all, cot_all))
    cot_sides = both_cores(after(cot_all, normed_sides[0]))
    kinds, normed_all, normed_sides, cot_all, cot_sides, tables, marks = together(
        kinds, normed_all, normed_sides, cot_all, cot_sides, tables, marks
    )

    mixed, context, log_totals = attend(normed_all, kinds, offsets, tables, marks)
    branch = dot(context, kinds[3], ((1,), (1,))).astype(bf16)
    branch = scatter_rows(branch, parts)
    middle = rows_in + branch
    second, unit_two, factor_two = norm_forward(middle, norm_gains[1], bias_rows[4])
    second_all = gather_rows(second.astype(bf16), parts)
    second_all, full_a, unit_b = together(second_all, full_a, unit_b)

    way_b = gather_from(([unit_b], [unit_b]), 1, 2, lines)
    natural = jnp.arange(dp_count, dtype=jnp.int32)
    acts, branch_a, second_a = feed(second_all, cot_all, [full_a], natural, size)
    acts, branch_a, second_a, way_b = together(acts, branch_a, second_a, way_b)

    way_b = gather_from(way_b, 2, 3, lines)
    acts_other = other_core(acts)
    second_sides = both_cores(after(second_all, acts))
    padded = acts.shape[1] // 3
    (terms,) = weight_terms(second_sides, cot_sides, (acts, acts_other), padded, 2, lines)
    terms, way_b = together(terms, way_b)

    way_b = gather_from(way_b, 3, lines, lines)
    streams = begin(terms)
    streams, way_b = together_streams(streams, way_b)

    streams = advance(streams)
    half = pack(*way_b, place, lines)
    order = jnp.stack(own_blocks + other_blocks).astype(jnp.int32)
    acts, branch_two, second_grad = feed(
        second_all, cot_all, [half, other_core(half)], order, size, (branch_a, second_a)
    )
    streams, (second_grad, branch_two, acts) = together_streams(
        streams, (second_grad, branch_two, acts)
    )

    streams = advance(streams)
    acts_other = other_core(acts)
    arrived = send_rows(second_grad, parts)
    padded = acts.shape[1] // 3
    (terms,) = weight_terms(second_sides, cot_sides, (acts, acts_other), padded, 2, lines)
    streams, (arrived, terms) = together_streams(streams, (arrived, terms))

    second_grad = add_up(arrived)
    middle_grad = cotangent.astype(jnp.float32) + norm_backward(
        second_grad, unit_two, factor_two, norm_gains[1]
    )
    middle_low = middle_grad.astype(bf16)
    streams, (middle_low, terms) = together_streams(streams, (middle_low, terms))
    middle_all = gather_rows(middle_low, parts)
    streams = advance(streams) + begin(terms)
    gate_params = (gate_weight, gate_first, gate_second)
    down_params = (down_weight, down_first, down_second)
    feed_news = feed_step(chunks[0], parts_of(finish(streams[:1])[0]), gate_params, down_params)
    streams, (middle_all, feed_news, branch_two) = together_streams(
        streams, (middle_all, feed_news, branch_two)
    )

    streams = advance(streams)
    leaving = send_rows(branch_two, parts)
    mixed_grad, normed_terms = attend_back(
        middle_all, kinds, mixed, context, log_totals, tables, marks
    )
    streams, (mixed_grad, normed_terms, middle_all, leaving) = together_streams(
        streams, (mixed_grad, normed_terms, middle_all, leaving)
    )

    arrived = send_rows(normed_terms, parts)
    streams = advance(streams)
    mixed_other = other_core(mixed_grad)
    middle_sides = both_cores(middle_all)
    entry_terms = weight_terms(
        normed_sides, middle_sides, (mixed_grad, mixed_other), head_cols, 3, lines, 2
    )

    early, late = begin(entry_terms[0]), begin(entry_terms[1])
    feed_news = feed_step(chunks[1], parts_of(streams[1]), gate_params, down_params, feed_news)
    early, (arrived, feed_news) = together_streams(early, (arrived, feed_news))
    (
        gate_gradient, gate_updated, gate_first_new, gate_second_new,
        down_gradient, down_updated, down_first_new, down_second_new,
    ) = feed_news

    early = advance(early)
    late, arrived = together_streams(late, arrived)
    late = advance(late)
    normed_grad = add_up(arrived)
    input_gradient = middle_grad + norm_backward(normed_grad, unit_one, factor_one, norm_gains[0])
    gain_two_grad = jnp.sum(second_grad * unit_two, axis=0)
    shift_two_grad = jnp.sum(second_grad, axis=0)
    gain_one_grad = jnp.sum(normed_grad * unit_one, axis=0)
    shift_one_grad = jnp.sum(normed_grad, axis=0)
    column_sums = jnp.sum(mixed_grad[:, : 3 * head_cols].astype(jnp.float32), axis=0).reshape(3, head_cols)
    column_sums = column_sums * jnp.stack([jnp.ones_like(rotmask), rotmask, jnp.ones_like(rotmask)])
    placed = lax.dynamic_update_slice_in_dim(
        jnp.zeros((3, width), jnp.float32), column_sums, column_start, 1
    )
    norms_local = jnp.stack([shift_one_grad, shift_two_grad, gain_one_grad, gain_two_grad])
    vectors = jnp.concatenate([placed, norms_local], axis=0)
    hops = [
        (axis, 1 << power)
        for axis, count in (("tensor", parts), ("dp", dp_count))
        for power in range(count.bit_length() - 1)
    ]
    vectors = hop(vectors, *hops[0])
    early, vectors = together_streams(early, vectors)

    early = advance(early)
    for which in hops[1:3]:
        vectors = hop(vectors, *which)
    late, vectors = together_streams(late, vectors)

    late = advance(late)
    vectors = hop(vectors, *hops[3])
    early = finish(early)
    early, (vectors, leaving) = together_streams(early, (vectors, leaving))
    output_rows = (middle + add_up(leaving)).astype(bf16)

    for which in hops[4:]:
        vectors = hop(vectors, *which)
    kind_first = lambda array: jnp.swapaxes(array, 0, 1)
    entry_params = [kind_first(array) for array in (entry_weight, entry_first, entry_second)]
    entry_news = plain_step(0, parts_of(early[0]), entry_params, (0, 1))
    late = finish(late)
    late, entry_news = together_streams(late, entry_news)
    bias_gradient = vectors[:5]
    gains_gradient = vectors[5:]
    entry_gradient, entry_updated, entry_first_new, entry_second_new = [
        kind_first(array) for array in plain_step(0, parts_of(late[0]), entry_params, (2,), entry_news)
    ]
    exit_gradient, exit_updated, exit_first_new, exit_second_new = [
        array[0]
        for array in plain_step(
            1, parts_of(late[0]), [array[None] for array in (exit_weight, exit_first, exit_second)], (0,)
        )
    ]
    bias_updated, bias_first_new, bias_second_new = adamw(
        bias_rows, bias_first, bias_second, bias_gradient, vector_rate, 0.0
    )
    gains_updated, gains_first_new, gains_second_new = adamw(
        norm_gains, gains_first, gains_second, gains_gradient, vector_rate, 0.0
    )
    return (
        output_rows,
        input_gradient,
        entry_gradient,
        entry_updated,
        entry_first_new,
        entry_second_new,
        exit_gradient,
        exit_updated,
        exit_first_new,
        exit_second_new,
        gate_gradient,
        gate_updated,
        gate_first_new,
        gate_second_new,
        down_gradient,
        down_updated,
        down_first_new,
        down_second_new,
        bias_gradient,
        bias_updated,
        bias_first_new,
        bias_second_new,
        gains_gradient,
        gains_updated,
        gains_first_new,
        gains_second_new,
    )


def solution(mesh):
    return jax.shard_map(
        on_device,
        mesh=mesh,
        in_specs=(
            P(("dp", "tensor"), None),
            P(("dp", "tensor"), None),
            P("dp", None),
            P("dp", None, "tensor"),
            P("dp", None, "tensor"),
            P("dp", None, "tensor"),
            P("dp", "tensor"),
            P("dp", "tensor"),
            P("dp", "tensor"),
            P("dp", None, "tensor"),
            P("dp", None, "tensor"),
            P("dp", None, "tensor"),
            P("dp", "tensor"),
            P("dp", "tensor"),
            P("dp", "tensor"),
            P(),
            P(),
            P(),
            P(),
            P(),
            P(),
        ),
        out_specs=(
            P(("dp", "tensor"), None),
            P(("dp", "tensor"), None),
            P("dp", None, "tensor"),
            P("dp", None, "tensor"),
            P("dp", None, "tensor"),
            P("dp", None, "tensor"),
            P("dp", "tensor"),
            P("dp", "tensor"),
            P("dp", "tensor"),
            P("dp", "tensor"),
            P("dp", None, "tensor"),
            P("dp", None, "tensor"),
            P("dp", None, "tensor"),
            P("dp", None, "tensor"),
            P("dp", "tensor"),
            P("dp", "tensor"),
            P("dp", "tensor"),
            P("dp", "tensor"),
            P(),
            P(),
            P(),
            P(),
            P(),
            P(),
            P(),
            P(),
        ),
        check_vma=False,
    )
```

```python
import jax
import jax.numpy as jnp
from jax import lax
from jax.experimental import pallas as pl
from jax.experimental.pallas import tpu as pltpu
from jax.sharding import PartitionSpec as P

HD = 64
ROT = 16
STEP = 3


norm_eps = 1e-05
rope_base = 10000.0
masked_score = -1e30
beta_one = 0.9
beta_two = 0.95
adam_eps = 1e-08
matrix_rate = 0.08
vector_rate = 0.4
weight_decay = 0.1


def norm_forward(rows, gain, shift):
    centre = jnp.mean(rows, axis=-1, keepdims=True)
    centred = rows - centre
    spread = jnp.mean(centred * centred, axis=-1, keepdims=True)
    factor = lax.rsqrt(spread + norm_eps)
    unit = centred * factor
    return (unit * gain + shift, unit, factor)


def norm_backward(incoming, unit, factor, gain):
    scaled = incoming * gain
    mean_plain = jnp.mean(scaled, axis=-1, keepdims=True)
    mean_along = jnp.mean(scaled * unit, axis=-1, keepdims=True)
    return factor * (scaled - mean_plain - unit * mean_along)


def segments(lengths_row, count):
    ends = jnp.cumsum(lengths_row)
    index = jnp.arange(count, dtype=jnp.int32)
    after = index[:, None] >= ends[None, :]
    segment = jnp.sum(after.astype(jnp.int32), axis=1)
    begin = jnp.max(jnp.where(after, ends[None, :], jnp.zeros_like(ends)[None, :]), axis=1)
    return (segment, index - begin)


def rotary_tables(positions):
    half = ROT // 2
    freqs = rope_base ** (-2.0 * jnp.arange(half, dtype=jnp.float32) / ROT)
    angles = positions[:, None] * freqs[None, :]
    return (jnp.cos(angles), jnp.sin(angles))


def adamw(weight, first, second, gradient, rate, decay):
    first_new = beta_one * first + (1.0 - beta_one) * gradient
    second_new = beta_two * second + (1.0 - beta_two) * gradient * gradient
    first_hat = first_new / (1.0 - beta_one**STEP)
    second_hat = second_new / (1.0 - beta_two**STEP)
    updated = weight - rate * (first_hat / (jnp.sqrt(second_hat) + adam_eps) + decay * weight)
    return (updated, first_new, second_new)


def together(*groups):
    flat, tree = jax.tree.flatten(groups)
    return jax.tree.unflatten(tree, lax.optimization_barrier(flat))


def after(value, *earlier):
    return lax.optimization_barrier((value,) + tuple(earlier))[0]


def pairs_up(lines, low, high, step):
    return [(z * 2 + c, (z + step) * 2 + c) for z in range(low, high) for c in range(2)]


def other_core(array):
    count = lax.axis_size("dp")
    return lax.ppermute(array, "dp", [(d, d ^ 1) for d in range(count)])


def gather_step(ups, downs, s, lines):
    up = lax.ppermute(ups[-1], "dp", pairs_up(lines, s - 1, lines - 1, 1))
    down = lax.ppermute(downs[-1], "dp", pairs_up(lines, 1, lines - s + 1, -1))
    return ups + [up], downs + [down]


def gather_from(way, low, high, lines):
    for s in range(low, high):
        way = gather_step(*way, s, lines)
    return way


def pack_kernel(lines, place_ref, *refs):
    pieces, out = refs[:-1], refs[-1]
    place = place_ref[0]
    s = pl.program_id(0)
    for at in range(lines):

        @pl.when((s == at) & (place >= at))
        def _():
            out[...] = pieces[at][...]

        if at > 0:

            @pl.when((s == at) & (place < at))
            def _():
                out[...] = pieces[2 * lines - 1 - at][...]


def pack(ups, downs, place, lines):
    rows, columns = ups[0].shape
    tile = min(128, rows)
    tiles = rows // tile

    def spec(at, is_up):
        def index(s, t, place_ref):
            wanted = (s == at) & ((place_ref[0] >= at) if is_up else (place_ref[0] < at))
            return (jnp.where(wanted, t, jnp.where(s > at, tiles - 1, 0)), 0)

        return pl.BlockSpec((tile, columns), index)

    return pl.pallas_call(
        lambda *refs: pack_kernel(lines, *refs),
        grid_spec=pltpu.PrefetchScalarGridSpec(
            num_scalar_prefetch=1,
            grid=(lines, tiles),
            in_specs=[spec(at, True) for at in range(lines)]
            + [spec(lines - at, False) for at in range(1, lines)],
            out_specs=pl.BlockSpec((tile, columns), lambda s, t, place_ref: (s * tiles + t, 0)),
        ),
        out_shape=jax.ShapeDtypeStruct((lines * rows, columns), ups[0].dtype),
        compiler_params=pltpu.CompilerParams(vmem_limit_bytes=40 * 1024 * 1024),
        cost_estimate=pl.CostEstimate(
            flops=0, bytes_accessed=4 * lines * rows * columns, transcendentals=0
        ),
        name="pack_blocks",
    )(place.reshape(1).astype(jnp.int32), *ups, *downs[1:])


def scatter_step(blocks, up, down, j, lines):
    up_send = blocks[lines - j] if up is None else blocks[lines - j] + up
    down_send = blocks[j] if down is None else blocks[j] + down
    up = lax.ppermute(up_send, "dp", pairs_up(lines, 0, lines - j, 1))
    down = lax.ppermute(down_send, "dp", pairs_up(lines, j, lines, -1))
    return up, down


def swap_rows(array, offset):
    count = lax.axis_size("tensor")
    return lax.ppermute(array, "tensor", [(t, t ^ offset) for t in range(count)])


def gather_rows(own, parts):
    return jnp.concatenate([own] + [swap_rows(own, r) for r in range(1, parts)], axis=0)


def send_rows(partial, parts):
    rows = partial.shape[0] // parts
    blocks = [partial[r * rows : (r + 1) * rows] for r in range(parts)]
    return [blocks[0]] + [swap_rows(blocks[r], r) for r in range(1, parts)]


def add_up(terms):
    total = terms[0].astype(jnp.float32)
    for term in terms[1:]:
        total = total + term.astype(jnp.float32)
    return total


def scatter_rows(partial, parts):
    return add_up(send_rows(partial, parts))


def together_streams(streams, others):
    ways, blocks, others = together(
        [way for _, way, _ in streams], [blocks for blocks, _, _ in streams], others
    )
    return [(b, w, left) for b, w, (_, _, left) in zip(blocks, ways, streams)], others


def hop(array, axis, bit):
    count = lax.axis_size(axis)
    return array + lax.ppermute(array, axis, [(i, i ^ bit) for i in range(count)])


def cuts(columns):
    first = min(columns, 128 * -(-(-(-columns // 128) * 5) // 11))
    return [(0, first), (first, columns)]


def paired(array):
    rows, kinds, columns = array.shape
    array = jnp.pad(array, ((0, 0), (0, 0), (0, -columns % 128)))
    return jnp.swapaxes(array.reshape(rows, kinds, -1, 128), 1, 2)


def dot(a, b, contract):
    return lax.dot_general(a, b, (contract, ((), ())), preferred_element_type=jnp.float32)


def whole(shape):
    return pl.BlockSpec(shape, lambda *_: (0,) * len(shape))


def kernel_call(kernel, grid, in_specs, out_specs, out_shape, scratch, name, flops=1, moved=1):
    return pl.pallas_call(
        kernel,
        grid=grid,
        in_specs=in_specs,
        out_specs=out_specs,
        out_shape=out_shape,
        scratch_shapes=scratch,
        compiler_params=pltpu.CompilerParams(vmem_limit_bytes=56 * 1024 * 1024),
        cost_estimate=pl.CostEstimate(flops=flops, bytes_accessed=moved, transcendentals=0),
        name=name,
    )


def turn(x, keep, low, high, direction):
    return (
        x * keep
        + pltpu.roll(x, 120, 1) * (low * direction)
        + pltpu.roll(x, 8, 1) * (high * direction)
    )


def row_steps(rows):
    return 128 if rows % 128 == 0 else rows


def fill_bias(bias_ref, column_ref, row_ref):
    rows = bias_ref.shape[0]
    step = row_steps(rows)

    def body(r, _):
        at = pl.ds(pl.multiple_of(r * step, step), step)
        marks = column_ref[at, :]
        visible = (marks[:, 0:1] == row_ref[0:1, :]) & (marks[:, 1:2] >= row_ref[1:2, :])
        bias_ref[at, :] = jnp.where(visible, 0.0, masked_score)
        return 0

    lax.fori_loop(0, rows // step, body, 0)


def matmul(a, b, contract=((1,), (0,))):
    return lax.dot_general(a, b, (contract, ((), ())), preferred_element_type=jnp.float32)


def attend_kernel(
    normed_ref, weight_ref, offset_ref, keep_ref, low_ref, high_ref, column_ref, row_ref,
    mixed_ref, context_ref, totals_ref, bias_ref, score_ref, prob_ref,
):
    kind = pl.program_id(0)
    rows, columns = context_ref.shape
    step = row_steps(rows)
    raw = matmul(normed_ref[...], weight_ref[0]) + offset_ref[0]
    here = pl.multiple_of(kind * columns, 128)

    @pl.when(kind < 2)
    def _():
        for b in range(columns // 128):
            block = turn(raw[:, b * 128 : (b + 1) * 128], keep_ref[...], low_ref[...], high_ref[...], 1.0)
            mixed_ref[:, pl.ds(pl.multiple_of(here + b * 128, 128), 128)] = block.astype(jnp.bfloat16)

    @pl.when(kind == 2)
    def _():
        mixed_ref[:, pl.ds(here, columns)] = raw.astype(jnp.bfloat16)
        fill_bias(bias_ref, column_ref, row_ref)
        lane = lax.broadcasted_iota(jnp.int32, (1, 128), 1)

        def pair_body(pair, _):
            first = pl.multiple_of(pair * 128, 128)
            queries = mixed_ref[:, pl.ds(first, 128)]
            keys = mixed_ref[:, pl.ds(pl.multiple_of(columns + first, 128), 128)]
            values = mixed_ref[:, pl.ds(pl.multiple_of(2 * columns + first, 128), 128)]
            parts = []
            for h in range(2):
                mine = (lane >= HD * h) & (lane < HD * (h + 1))
                score_ref[...] = matmul(
                    jnp.where(mine, queries, jnp.zeros_like(queries)), keys, ((1,), (1,))
                )

                def rows_body(r, _):
                    at = pl.ds(pl.multiple_of(r * step, step), step)
                    scores = score_ref[at, :] * (HD**-0.5) + bias_ref[at, :]
                    summit = jnp.max(scores, axis=1, keepdims=True)
                    weights = jnp.exp(scores - summit)
                    total = jnp.sum(weights, axis=1, keepdims=True)
                    prob_ref[at, :] = (weights * (1.0 / total)).astype(jnp.bfloat16)
                    spot = lane == pair * 2 + h
                    totals_ref[at, :] = jnp.where(
                        spot, summit + jnp.log(total), totals_ref[at, :]
                    )
                    return 0

                lax.fori_loop(0, rows // step, rows_body, 0, unroll=True)
                parts.append(matmul(prob_ref[...], values))
            both = jnp.where(lane < HD, parts[0], parts[1])
            context_ref[:, pl.ds(first, 128)] = both.astype(jnp.bfloat16)
            return 0

        totals_ref[...] = jnp.zeros_like(totals_ref)
        lax.fori_loop(0, columns // 128, pair_body, 0)


def attend(normed_all, entry_full, offsets, tables, marks):
    rows, width = normed_all.shape
    columns = entry_full.shape[2]
    bf16, f32 = jnp.bfloat16, jnp.float32
    return kernel_call(
        attend_kernel,
        (3,),
        [whole((rows, width)), pl.BlockSpec((1, width, columns), lambda k: (k, 0, 0)),
         pl.BlockSpec((1, 1, columns), lambda k: (k, 0, 0))]
        + [whole((rows, 128))] * 3 + [whole((rows, 2)), whole((2, rows))],
        [whole((rows, 3 * columns)), whole((rows, columns)), whole((rows, 128))],
        [jax.ShapeDtypeStruct((rows, 3 * columns), bf16), jax.ShapeDtypeStruct((rows, columns), bf16),
         jax.ShapeDtypeStruct((rows, 128), f32)],
        [pltpu.VMEM((rows, rows), f32), pltpu.VMEM((rows, rows), f32), pltpu.VMEM((rows, rows), bf16)],
        "attention",
        24 * rows * width * columns,
        8 * rows * width,
    )(normed_all, entry_full, offsets.reshape(3, 1, columns), *tables, *marks)


def attend_back_kernel(
    middle_ref, exit_ref, mixed_ref, context_ref, totals_ref, keep_ref, low_ref, high_ref, column_ref,
    row_ref, kinds_ref, grad_ref, normed_ref, bias_ref, score_ref, prob_grad_ref, prob_ref,
    score_grad_ref, context_grad_ref, weight_ref, sem,
):
    rows = middle_ref.shape[0]
    columns = exit_ref.shape[2]
    step = row_steps(rows)
    load = pltpu.make_async_copy(kinds_ref.at[pl.ds(0, 3)], weight_ref, sem)
    load.start()
    grad_ref[:, 3 * columns :] = context_ref[...]
    context_grad_ref[...] = matmul(middle_ref[...], exit_ref[0]).astype(jnp.bfloat16)
    fill_bias(bias_ref, column_ref, row_ref)
    lane = lax.broadcasted_iota(jnp.int32, (1, 128), 1)

    def pair_body(pair, _):
        first = pl.multiple_of(pair * 128, 128)
        second = pl.multiple_of(columns + first, 128)
        third = pl.multiple_of(2 * columns + first, 128)
        queries = mixed_ref[:, pl.ds(first, 128)]
        keys = mixed_ref[:, pl.ds(second, 128)]
        values = mixed_ref[:, pl.ds(third, 128)]
        incoming = context_grad_ref[:, pl.ds(first, 128)]
        query_parts, key_parts, value_parts = [], [], []
        for h in range(2):
            mine = (lane >= HD * h) & (lane < HD * (h + 1))
            score_ref[...] = matmul(
                jnp.where(mine, queries, jnp.zeros_like(queries)), keys, ((1,), (1,))
            )
            prob_grad_ref[...] = matmul(
                jnp.where(mine, incoming, jnp.zeros_like(incoming)), values, ((1,), (1,))
            )

            def rows_body(r, _):
                at = pl.ds(pl.multiple_of(r * step, step), step)
                spot = lane == pair * 2 + h
                total = jnp.sum(jnp.where(spot, totals_ref[at, :], 0.0), axis=1, keepdims=True)
                probs = jnp.exp(score_ref[at, :] * (HD**-0.5) + bias_ref[at, :] - total)
                prob_grad = prob_grad_ref[at, :]
                inner = jnp.sum(probs * prob_grad, axis=1, keepdims=True)
                score_grad_ref[at, :] = (probs * (prob_grad - inner)).astype(jnp.bfloat16)
                prob_ref[at, :] = probs.astype(jnp.bfloat16)
                return 0

            lax.fori_loop(0, rows // step, rows_body, 0, unroll=True)
            query_parts.append(matmul(score_grad_ref[...], keys))
            key_parts.append(matmul(score_grad_ref[...], queries, ((0,), (0,))))
            value_parts.append(matmul(prob_ref[...], incoming, ((0,), (0,))))
        keep, low, high = keep_ref[...], low_ref[...], high_ref[...]
        scale = HD**-0.5
        query_grad = jnp.where(lane < HD, query_parts[0], query_parts[1]) * scale
        key_grad = jnp.where(lane < HD, key_parts[0], key_parts[1]) * scale
        value_grad = jnp.where(lane < HD, value_parts[0], value_parts[1])
        grad_ref[:, pl.ds(first, 128)] = turn(query_grad, keep, low, high, -1.0).astype(jnp.bfloat16)
        grad_ref[:, pl.ds(second, 128)] = turn(key_grad, keep, low, high, -1.0).astype(jnp.bfloat16)
        grad_ref[:, pl.ds(third, 128)] = value_grad.astype(jnp.bfloat16)
        return 0

    lax.fori_loop(0, columns // 128, pair_body, 0)
    load.wait()
    width = normed_ref.shape[1]
    for low in range(0, width, 512):
        here = slice(low, min(low + 512, width))
        total = None
        for k in range(3):
            term = matmul(
                grad_ref[:, k * columns : (k + 1) * columns], weight_ref[k, here, :], ((1,), (1,))
            )
            total = term if total is None else total + term
        normed_ref[:, here] = total.astype(jnp.bfloat16)


def attend_back(middle_all, exit_full, mixed, context, totals, tables, marks):
    rows, width = middle_all.shape
    columns = exit_full.shape[2]
    bf16, f32 = jnp.bfloat16, jnp.float32
    square = (rows, rows)
    return kernel_call(
        attend_back_kernel,
        (1,),
        [whole((rows, width)), pl.BlockSpec((1, width, columns), lambda *_: (3, 0, 0)),
         whole((rows, 3 * columns)), whole((rows, columns)), whole((rows, 128))]
        + [whole((rows, 128))] * 3 + [whole((rows, 2)), whole((2, rows))]
        + [pl.BlockSpec(memory_space=pl.ANY)],
        [whole((rows, 4 * columns)), whole((rows, width))],
        [jax.ShapeDtypeStruct((rows, 4 * columns), bf16), jax.ShapeDtypeStruct((rows, width), bf16)],
        [pltpu.VMEM(square, f32), pltpu.VMEM(square, f32), pltpu.VMEM(square, f32),
         pltpu.VMEM(square, bf16), pltpu.VMEM(square, bf16), pltpu.VMEM((rows, columns), bf16),
         pltpu.VMEM((3, width, columns), bf16), pltpu.SemaphoreType.DMA],
        "attention_back",
        24 * rows * width * columns,
        8 * rows * width,
    )(middle_all, exit_full, mixed, context, totals, *tables, *marks, exit_full)


def feed_kernel(pieces, order_ref, second_in, cot_in, *refs):
    fulls, refs = refs[:pieces], refs[pieces:]
    earlier, refs = (refs[:2], refs[2:]) if pieces > 1 else ((), refs)
    acts_ref, branch_ref, second_grad_ref, weight_ref, hidden_grad_ref, sems = refs[:6]
    j = pl.program_id(0)
    rows, width = second_in.shape
    padded = acts_ref.shape[1] // 3
    pairs = padded // 128
    size = branch_ref.shape[1]
    height = width // pieces
    bf16 = jnp.bfloat16
    second_ref, cot_ref = (second_in, cot_in) if pieces == 1 else refs[6:]

    def loads(at, columns, which):
        here = pl.ds(at, columns)
        return [
            pltpu.make_async_copy(
                full.at[:, here], weight_ref.at[pl.ds(p * height, height), here], sems.at[p, which]
            )
            for p, full in enumerate(fulls)
        ]

    @pl.when(j == 0)
    def _():
        for load in loads(2 * padded, padded, 0):
            load.start()
        for p in range(min(2, pairs)):
            for load in loads(p * 256, 256, p + 1):
                load.start()
        if pieces > 1:
            for b in range(width // size):
                there = pl.ds(pl.multiple_of(order_ref[b] * size, size), size)
                second_ref[:, b * size : (b + 1) * size] = second_in[:, there]
                cot_ref[:, b * size : (b + 1) * size] = cot_in[:, there]
        for load in loads(2 * padded, padded, 0):
            load.wait()
        for p in range(2, pairs):
            for load in loads(p * 256, 256, p + 1):
                load.start()
        for low in range(0, padded, 256):
            high = min(low + 256, padded)
            hidden_grad_ref[:, low:high] = matmul(
                cot_ref[...], weight_ref[:, 2 * padded + low : 2 * padded + high]
            )
        for p in range(pairs):
            for load in loads(p * 256, 256, p + 1):
                load.wait()
            gate_up = matmul(second_ref[...], weight_ref[:, p * 256 : (p + 1) * 256])
            gate, upper = gate_up[:, :128], gate_up[:, 128:]
            grad = hidden_grad_ref[:, p * 128 : (p + 1) * 128]
            sigmoid = jax.nn.sigmoid(gate)
            activated = gate * sigmoid
            acts_ref[:, p * 256 : p * 256 + 128] = (
                grad * upper * sigmoid * (1.0 + gate * (1.0 - sigmoid))
            ).astype(bf16)
            acts_ref[:, p * 256 + 128 : (p + 1) * 256] = (grad * activated).astype(bf16)
            hidden = 2 * padded + p * 128
            acts_ref[:, hidden : hidden + 128] = (activated * upper).astype(bf16)

    @pl.when(j > 0)
    def _():
        here = pl.ds(pl.multiple_of((j - 1) * size, size), size)
        over = ((1,), (1,))
        branch = matmul(acts_ref[:, 2 * padded :], weight_ref[here, 2 * padded :], over)
        second_grad = matmul(acts_ref[:, : 2 * padded], weight_ref[here, : 2 * padded], over)
        if pieces > 1:
            branch = branch + earlier[0][...].astype(jnp.float32)
            second_grad = second_grad + earlier[1][...].astype(jnp.float32)
        branch_ref[...] = branch.astype(bf16)
        second_grad_ref[...] = second_grad.astype(bf16)


def feed(second_all, cot_all, fulls, order, size, earlier=()):
    rows, width = second_all.shape
    padded = fulls[0].shape[1] // 3
    pieces = len(fulls)
    bf16, f32 = jnp.bfloat16, jnp.float32
    full = pl.BlockSpec((rows, width), lambda j, order_ref: (0, 0))
    out = pl.BlockSpec((rows, size), lambda j, order_ref: (0, order_ref[jnp.maximum(j - 1, 0)]))
    scratch = [
        pltpu.VMEM((width, 3 * padded), bf16), pltpu.VMEM((rows, padded), f32),
        pltpu.SemaphoreType.DMA((pieces, 1 + padded // 128)),
    ]
    if pieces > 1:
        scratch += [pltpu.VMEM((rows, width), bf16)] * 2
    return pl.pallas_call(
        lambda *refs: feed_kernel(pieces, *refs),
        grid_spec=pltpu.PrefetchScalarGridSpec(
            num_scalar_prefetch=1,
            grid=(1 + width // size,),
            in_specs=[full] * 2 + [pl.BlockSpec(memory_space=pl.ANY)] * pieces + [out] * len(earlier),
            out_specs=[pl.BlockSpec((rows, 3 * padded), lambda j, order_ref: (0, 0)), out, out],
            scratch_shapes=scratch,
        ),
        out_shape=[jax.ShapeDtypeStruct((rows, 3 * padded), bf16)]
        + [jax.ShapeDtypeStruct((rows, width), bf16)] * 2,
        compiler_params=pltpu.CompilerParams(vmem_limit_bytes=56 * 1024 * 1024),
        cost_estimate=pl.CostEstimate(
            flops=24 * rows * width * padded,
            bytes_accessed=12 * width * padded + 16 * rows * width,
            transcendentals=0,
        ),
        name="feed_forward",
    )(order, second_all, cot_all, *fulls, *earlier)


def turned_kernel(blocks_ref, rows_ref, out_ref):
    out_ref[...] = rows_ref[...].T


def turned_blocks(array, blocks, size):
    rows = array.shape[0]
    return pl.pallas_call(
        turned_kernel,
        grid_spec=pltpu.PrefetchScalarGridSpec(
            num_scalar_prefetch=1,
            grid=(len(blocks),),
            in_specs=[pl.BlockSpec((rows, size), lambda b, blocks_ref: (0, blocks_ref[b]))],
            out_specs=pl.BlockSpec((size, rows), lambda b, blocks_ref: (b, 0)),
        ),
        out_shape=jax.ShapeDtypeStruct((len(blocks) * size, rows), array.dtype),
        compiler_params=pltpu.CompilerParams(vmem_limit_bytes=32 * 1024 * 1024),
        cost_estimate=pl.CostEstimate(flops=1, bytes_accessed=1, transcendentals=0),
        name="turned_blocks",
    )(jnp.stack(blocks).astype(jnp.int32), array)


def terms_kernel(split, groups, own_left, other_left, own_last, other_last, own_ref, other_ref, *outs):
    k = pl.program_id(0)
    lines = len(outs) // groups
    per_group = pl.num_programs(0) // groups

    def write(own, other):
        total = (matmul(own[...], own_ref[...]) + matmul(other[...], other_ref[...])).astype(jnp.bfloat16)
        size = outs[0].shape[0]
        for g in range(groups):

            @pl.when(k // per_group == g)
            def _():
                for s, out in enumerate(outs[g * lines : (g + 1) * lines]):
                    out[...] = total[s * size : (s + 1) * size]

    @pl.when(k < split)
    def _():
        write(own_left, other_left)

    @pl.when(k >= split)
    def _():
        write(own_last, other_last)


def weight_terms(left, left_last, right, tile, split, lines, groups=1):
    count, rows = left[0].shape
    columns = right[0].shape[1]
    size = count // lines
    per_group = columns // tile // groups
    left_spec = whole((count, rows))
    right_spec = pl.BlockSpec((rows, tile), lambda k: (0, k))

    def out_spec(g):
        return pl.BlockSpec((size, tile), lambda k: (0, jnp.clip(k - g * per_group, 0, per_group - 1)))

    outs = kernel_call(
        lambda *refs: terms_kernel(split, groups, *refs),
        (columns // tile,),
        [left_spec] * 4 + [right_spec] * 2,
        [out_spec(g) for g in range(groups) for _ in range(lines)],
        [jax.ShapeDtypeStruct((size, columns // groups), jnp.bfloat16)] * (lines * groups),
        [],
        "weight_terms",
        4 * count * rows * columns,
        2 * (4 * count * rows + 2 * rows * columns + count * columns),
    )(*left, *left_last, *right)
    return [list(outs[g * lines : (g + 1) * lines]) for g in range(groups)]


def summed(refs, rows, columns):
    own, up, down = [ref[rows, columns].astype(jnp.float32) for ref in refs]
    return own + up + down


def plain_step_kernel(own, up, down, weight, first, second, *outs):
    outs = outs[-4:]
    everything = slice(None)
    gradient = summed((own, up, down), everything, everything)
    news = adamw(weight[0], first[0], second[0], gradient, matrix_rate, weight_decay)
    for out, value in zip(outs, (gradient,) + tuple(news)):
        out[0] = value


def plain_step(start, parts_of_sum, params, kinds, earlier=()):
    count, rows, columns = params[0].shape
    tile = rows // 2
    part = pl.BlockSpec((tile, columns), lambda k, r: (r, start + k))
    block = pl.BlockSpec((1, tile, columns), lambda k, r: (kinds[0] + k, r, 0))
    return pl.pallas_call(
        plain_step_kernel,
        grid=(len(kinds), 2),
        in_specs=[part] * 3 + [block] * 3 + [pl.BlockSpec(memory_space=pl.ANY)] * len(earlier),
        out_specs=[block] * 4,
        out_shape=[jax.ShapeDtypeStruct((count, rows, columns), jnp.float32)] * 4,
        input_output_aliases={6 + i: i for i in range(len(earlier))},
        compiler_params=pltpu.CompilerParams(vmem_limit_bytes=56 * 1024 * 1024),
        cost_estimate=pl.CostEstimate(flops=1, bytes_accessed=1, transcendentals=0),
        name="plain_step",
    )(*parts_of_sum, *params, *earlier)


def feed_step_kernel(*refs):
    pairs, singles, gate, down = refs[:3], refs[3:6], refs[6:9], refs[9:12]
    gate_outs, down_outs = refs[-8:-4], refs[-4:]
    everything = slice(None)
    for k in range(2):
        gradient = summed(pairs, everything, slice(128 * k, 128 * k + 128))
        news = adamw(*[ref[:, k, :] for ref in gate], gradient, matrix_rate, weight_decay)
        for out, value in zip(gate_outs, (gradient,) + tuple(news)):
            out[:, k, :] = value
    gradient = summed(singles, everything, everything)
    news = adamw(*[ref[...] for ref in down], gradient, matrix_rate, weight_decay)
    for out, value in zip(down_outs, (gradient,) + tuple(news)):
        out[...] = value


def feed_step(run, parts_of_sum, gate, down, earlier=()):
    rows, columns = down[0].shape
    low, high = run
    blocks = -(-(high - low) // 128)
    gate_block = pl.BlockSpec((rows, 2, 128), lambda c: (0, 0, low // 128 + c))
    down_block = pl.BlockSpec((rows, 128), lambda c: (0, low // 128 + c))
    pair = pl.BlockSpec((rows, 256), lambda c: (0, c))
    single = pl.BlockSpec((rows, 128), lambda c: (0, 2 * blocks + c))
    return pl.pallas_call(
        feed_step_kernel,
        grid=(blocks,),
        in_specs=[pair] * 3 + [single] * 3 + [gate_block] * 3 + [down_block] * 3
        + [pl.BlockSpec(memory_space=pl.ANY)] * len(earlier),
        out_specs=[gate_block] * 4 + [down_block] * 4,
        out_shape=[jax.ShapeDtypeStruct((rows, 2, columns), jnp.float32)] * 4
        + [jax.ShapeDtypeStruct((rows, columns), jnp.float32)] * 4,
        input_output_aliases={12 + i: i for i in range(len(earlier))},
        compiler_params=pltpu.CompilerParams(vmem_limit_bytes=56 * 1024 * 1024),
        cost_estimate=pl.CostEstimate(
            flops=0, bytes_accessed=84 * rows * (high - low), transcendentals=0
        ),
        name="feed_step",
    )(*parts_of_sum, *parts_of_sum, *gate, *down, *earlier)


def on_device(
    tokens,
    cotangent,
    lengths,
    entry_weight,
    entry_first,
    entry_second,
    exit_weight,
    exit_first,
    exit_second,
    gate_weight,
    gate_first,
    gate_second,
    down_weight,
    down_first,
    down_second,
    bias_rows,
    bias_first,
    bias_second,
    norm_gains,
    gains_first,
    gains_second,
):
    parts = lax.axis_size("tensor")
    part_index = lax.axis_index("tensor")
    dp_index = lax.axis_index("dp")
    dp_count = lax.axis_size("dp")
    lines = dp_count // 2
    last = lines - 1
    place = dp_index // 2
    core = dp_index % 2
    local_rows = tokens.shape[0]
    group = local_rows * parts
    width = tokens.shape[1]
    size = width // dp_count
    head_cols = entry_weight.shape[2]
    hidden_cols = down_weight.shape[1]
    bf16 = jnp.bfloat16
    own_blocks = [((place - s + lines) % lines) * 2 + core for s in range(lines)]
    other_blocks = [((place - s + lines) % lines) * 2 + 1 - core for s in range(lines)]
    none = (None, None)

    def advance(streams):
        return [
            (blocks, scatter_step(blocks, *way, left, lines), left - 1) if left > 0 else stream
            for stream in streams
            for blocks, way, left in [stream]
        ]

    def begin(blocks):
        return advance([(blocks, none, last)])

    def finish(streams):
        while any(left > 0 for _, _, left in streams):
            streams = advance(streams)
        return streams

    def parts_of(stream):
        blocks, way, _ = stream
        return (blocks[0],) + tuple(way)

    def both_cores(array):
        both = turned_blocks(array, own_blocks + other_blocks, size)
        return both[: width // 2], other_core(both[width // 2 :])

    kinds_own = jnp.concatenate(
        [jnp.swapaxes(entry_weight, 0, 1).astype(bf16), exit_weight.astype(bf16)[None]], axis=0
    )
    kinds = lax.all_gather(kinds_own, "dp", axis=1, tiled=True)
    chunks = cuts(hidden_cols)

    def unit_of(a, b):
        gates = paired(gate_weight[:, :, a:b].astype(bf16)).reshape(size, -1)
        downs = jnp.pad(down_weight[:, a:b].astype(bf16), ((0, 0), (0, -(b - a) % 128)))
        return jnp.concatenate([gates, downs], axis=1)

    unit_a, unit_b = [unit_of(a, b) for a, b in chunks]
    full_a = lax.all_gather(after(unit_a, kinds_own), "dp", axis=0, tiled=True)

    segment, positions = segments(lengths[0], group)
    row_blocks = jnp.arange(parts, dtype=jnp.int32) ^ part_index
    row_index = (
        row_blocks[:, None] * local_rows + jnp.arange(local_rows, dtype=jnp.int32)[None, :]
    ).reshape(group)
    segment, positions = [
        jnp.concatenate(
            [
                lax.dynamic_slice_in_dim(array, (part_index ^ r) * local_rows, local_rows, 0)
                for r in range(parts)
            ]
        )
        for array in (segment, positions)
    ]
    cosine, sine = rotary_tables(positions.astype(jnp.float32))
    ones = jnp.ones((group, HD - ROT), jnp.float32)
    blank = jnp.zeros((group, ROT // 2), jnp.float32)
    empty = jnp.zeros((group, HD - ROT), jnp.float32)
    tables = [
        jnp.concatenate([a, b, c] * 2, axis=1)
        for a, b, c in ((cosine, cosine, ones), (-sine, blank, empty), (blank, sine, empty))
    ]
    marks = (jnp.stack([segment, row_index], axis=1), jnp.stack([segment, row_index], axis=0))
    column_start = part_index * head_cols
    rotmask = (jnp.arange(head_cols, dtype=jnp.int32) % HD < ROT).astype(jnp.float32)
    query_bias = lax.dynamic_slice_in_dim(bias_rows[0], column_start, head_cols, 0)
    key_bias = lax.dynamic_slice_in_dim(bias_rows[1], column_start, head_cols, 0) * rotmask
    value_bias = lax.dynamic_slice_in_dim(bias_rows[2], column_start, head_cols, 0)
    offsets = jnp.stack([query_bias, key_bias, value_bias])

    rows_in = tokens.astype(jnp.float32)
    normed, unit_one, factor_one = norm_forward(rows_in, norm_gains[0], bias_rows[3])
    normed_all = gather_rows(normed.astype(bf16), parts)
    cot_all = gather_rows(after(cotangent, normed_all), parts)
    normed_sides = both_cores(after(normed_all, cot_all))
    cot_sides = both_cores(after(cot_all, normed_sides[0]))
    kinds, normed_all, normed_sides, cot_all, cot_sides, tables, marks = together(
        kinds, normed_all, normed_sides, cot_all, cot_sides, tables, marks
    )

    mixed, context, log_totals = attend(normed_all, kinds, offsets, tables, marks)
    branch = dot(context, kinds[3], ((1,), (1,))).astype(bf16)
    branch = scatter_rows(branch, parts)
    middle = rows_in + branch
    second, unit_two, factor_two = norm_forward(middle, norm_gains[1], bias_rows[4])
    second_all = gather_rows(second.astype(bf16), parts)
    second_all, full_a, unit_b = together(second_all, full_a, unit_b)

    way_b = gather_from(([unit_b], [unit_b]), 1, 2, lines)
    natural = jnp.arange(dp_count, dtype=jnp.int32)
    acts, branch_a, second_a = feed(second_all, cot_all, [full_a], natural, size)
    acts, branch_a, second_a, way_b = together(acts, branch_a, second_a, way_b)

    way_b = gather_from(way_b, 2, 3, lines)
    acts_other = other_core(acts)
    second_sides = both_cores(after(second_all, acts))
    padded = acts.shape[1] // 3
    (terms,) = weight_terms(second_sides, cot_sides, (acts, acts_other), padded, 2, lines)
    terms, way_b = together(terms, way_b)

    way_b = gather_from(way_b, 3, lines, lines)
    streams = begin(terms)
    streams, way_b = together_streams(streams, way_b)

    streams = advance(streams)
    half = pack(*way_b, place, lines)
    order = jnp.stack(own_blocks + other_blocks).astype(jnp.int32)
    acts, branch_two, second_grad = feed(
        second_all, cot_all, [half, other_core(half)], order, size, (branch_a, second_a)
    )
    streams, (second_grad, branch_two, acts) = together_streams(
        streams, (second_grad, branch_two, acts)
    )

    streams = advance(streams)
    acts_other = other_core(acts)
    arrived = send_rows(second_grad, parts)
    padded = acts.shape[1] // 3
    (terms,) = weight_terms(second_sides, cot_sides, (acts, acts_other), padded, 2, lines)
    streams, (arrived, terms) = together_streams(streams, (arrived, terms))

    second_grad = add_up(arrived)
    middle_grad = cotangent.astype(jnp.float32) + norm_backward(
        second_grad, unit_two, factor_two, norm_gains[1]
    )
    middle_low = middle_grad.astype(bf16)
    streams, (middle_low, terms) = together_streams(streams, (middle_low, terms))
    middle_all = gather_rows(middle_low, parts)
    streams = advance(streams) + begin(terms)
    gate_params = (gate_weight, gate_first, gate_second)
    down_params = (down_weight, down_first, down_second)
    feed_news = feed_step(chunks[0], parts_of(finish(streams[:1])[0]), gate_params, down_params)
    streams, (middle_all, feed_news, branch_two) = together_streams(
        streams, (middle_all, feed_news, branch_two)
    )

    streams = advance(streams)
    leaving = send_rows(branch_two, parts)
    mixed_grad, normed_terms = attend_back(
        middle_all, kinds, mixed, context, log_totals, tables, marks
    )
    streams, (mixed_grad, normed_terms, middle_all, leaving) = together_streams(
        streams, (mixed_grad, normed_terms, middle_all, leaving)
    )

    arrived = send_rows(normed_terms, parts)
    streams = advance(streams)
    mixed_other = other_core(mixed_grad)
    middle_sides = both_cores(middle_all)
    entry_terms = weight_terms(
        normed_sides, middle_sides, (mixed_grad, mixed_other), head_cols, 3, lines, 2
    )

    early, late = begin(entry_terms[0]), begin(entry_terms[1])
    feed_news = feed_step(chunks[1], parts_of(streams[1]), gate_params, down_params, feed_news)
    early, (arrived, feed_news) = together_streams(early, (arrived, feed_news))
    (
        gate_gradient, gate_updated, gate_first_new, gate_second_new,
        down_gradient, down_updated, down_first_new, down_second_new,
    ) = feed_news

    early = advance(early)
    late, arrived = together_streams(late, arrived)
    late = advance(late)
    normed_grad = add_up(arrived)
    input_gradient = middle_grad + norm_backward(normed_grad, unit_one, factor_one, norm_gains[0])
    gain_two_grad = jnp.sum(second_grad * unit_two, axis=0)
    shift_two_grad = jnp.sum(second_grad, axis=0)
    gain_one_grad = jnp.sum(normed_grad * unit_one, axis=0)
    shift_one_grad = jnp.sum(normed_grad, axis=0)
    column_sums = jnp.sum(mixed_grad[:, : 3 * head_cols].astype(jnp.float32), axis=0).reshape(3, head_cols)
    column_sums = column_sums * jnp.stack([jnp.ones_like(rotmask), rotmask, jnp.ones_like(rotmask)])
    placed = lax.dynamic_update_slice_in_dim(
        jnp.zeros((3, width), jnp.float32), column_sums, column_start, 1
    )
    norms_local = jnp.stack([shift_one_grad, shift_two_grad, gain_one_grad, gain_two_grad])
    vectors = jnp.concatenate([placed, norms_local], axis=0)
    hops = [
        (axis, 1 << power)
        for axis, count in (("tensor", parts), ("dp", dp_count))
        for power in range(count.bit_length() - 1)
    ]
    vectors = hop(vectors, *hops[0])
    early, vectors = together_streams(early, vectors)

    early = advance(early)
    for which in hops[1:3]:
        vectors = hop(vectors, *which)
    late, vectors = together_streams(late, vectors)

    late = advance(late)
    vectors = hop(vectors, *hops[3])
    early = finish(early)
    early, (vectors, leaving) = together_streams(early, (vectors, leaving))
    output_rows = (middle + add_up(leaving)).astype(bf16)

    for which in hops[4:]:
        vectors = hop(vectors, *which)
    kind_first = lambda array: jnp.swapaxes(array, 0, 1)
    entry_params = [kind_first(array) for array in (entry_weight, entry_first, entry_second)]
    entry_news = plain_step(0, parts_of(early[0]), entry_params, (0, 1))
    late = finish(late)
    late, entry_news = together_streams(late, entry_news)
    bias_gradient = vectors[:5]
    gains_gradient = vectors[5:]
    entry_gradient, entry_updated, entry_first_new, entry_second_new = [
        kind_first(array) for array in plain_step(0, parts_of(late[0]), entry_params, (2,), entry_news)
    ]
    exit_gradient, exit_updated, exit_first_new, exit_second_new = [
        array[0]
        for array in plain_step(
            1, parts_of(late[0]), [array[None] for array in (exit_weight, exit_first, exit_second)], (0,)
        )
    ]
    bias_updated, bias_first_new, bias_second_new = adamw(
        bias_rows, bias_first, bias_second, bias_gradient, vector_rate, 0.0
    )
    gains_updated, gains_first_new, gains_second_new = adamw(
        norm_gains, gains_first, gains_second, gains_gradient, vector_rate, 0.0
    )
    return (
        output_rows,
        input_gradient,
        entry_gradient,
        entry_updated,
        entry_first_new,
        entry_second_new,
        exit_gradient,
        exit_updated,
        exit_first_new,
        exit_second_new,
        gate_gradient,
        gate_updated,
        gate_first_new,
        gate_second_new,
        down_gradient,
        down_updated,
        down_first_new,
        down_second_new,
        bias_gradient,
        bias_updated,
        bias_first_new,
        bias_second_new,
        gains_gradient,
        gains_updated,
        gains_first_new,
        gains_second_new,
    )


def solution(mesh):
    return jax.shard_map(
        on_device,
        mesh=mesh,
        in_specs=(
            P(("dp", "tensor"), None),
            P(("dp", "tensor"), None),
            P("dp", None),
            P("dp", None, "tensor"),
            P("dp", None, "tensor"),
            P("dp", None, "tensor"),
            P("dp", "tensor"),
            P("dp", "tensor"),
            P("dp", "tensor"),
            P("dp", None, "tensor"),
            P("dp", None, "tensor"),
            P("dp", None, "tensor"),
            P("dp", "tensor"),
            P("dp", "tensor"),
            P("dp", "tensor"),
            P(),
            P(),
            P(),
            P(),
            P(),
            P(),
        ),
        out_specs=(
            P(("dp", "tensor"), None),
            P(("dp", "tensor"), None),
            P("dp", None, "tensor"),
            P("dp", None, "tensor"),
            P("dp", None, "tensor"),
            P("dp", None, "tensor"),
            P("dp", "tensor"),
            P("dp", "tensor"),
            P("dp", "tensor"),
            P("dp", "tensor"),
            P("dp", None, "tensor"),
            P("dp", None, "tensor"),
            P("dp", None, "tensor"),
            P("dp", None, "tensor"),
            P("dp", "tensor"),
            P("dp", "tensor"),
            P("dp", "tensor"),
            P("dp", "tensor"),
            P(),
            P(),
            P(),
            P(),
            P(),
            P(),
            P(),
            P(),
        ),
        check_vma=False,
    )
```
